32 devices in a mesh: batch: 16 (over z, y, core), mem: 2 (over x).
Axes of the slice: x: 2, y: 2, z: 4, core: 2. Of those that a mesh axis runs over, the one named last changes fastest.
Arguments:
- hidden: bfloat16 [16, 1024, 768], P('batch', 'mem'), may hold values from -6 to 6
- memory: bfloat16 [16, 2048, 768], P('batch', 'mem'), may hold values from -6 to 6
- decoder_lengths: int32 [16, 4], P('batch'), may hold values from 1 to 768, as said below
- memory_lengths: int32 [16, 4], P('batch'), may hold values from 1 to 1536, as said below
- distance_buckets: int32 [1024], replicated, may hold values from 0 to 31, as said below
- norm_gains: float32 [3, 768], replicated, may hold values from 0.5 to 1.5
- position_bias: float32 [32, 12], replicated, may hold values from -4 to 4
- self_weights: bfloat16 [3, 768, 768], P(None, 'batch', 'mem'), may hold values from -0.078125 to 0.078125
- self_output: bfloat16 [768, 768], P('batch', 'mem'), may hold values from -12 to 12
- cross_weights: bfloat16 [3, 768, 768], P(None, 'batch', 'mem'), may hold values from -0.078125 to 0.078125
- cross_output: bfloat16 [768, 768], P('batch', 'mem'), may hold values from -16 to 16
- expand_weights: bfloat16 [2, 768, 2048], P(None, 'batch', 'mem'), may hold values from -0.21875 to 0.21875
- contract_weight: bfloat16 [2048, 768], P('batch', 'mem'), may hold values from -0.125 to 0.125
- cotangent: bfloat16 [16, 1024, 768], P('batch', 'mem'), may hold values from -6 to 6
Outputs:
- output: bfloat16 [16, 1024, 768], P('batch', 'mem')
- hidden_grad: float32 [16, 1024, 768], P('batch', 'mem')
- memory_grad: float32 [16, 2048, 768], P('batch', 'mem')
- gains_grad: float32 [3, 768], replicated
- bias_grad: float32 [32, 12], replicated
- self_weights_grad: float32 [3, 768, 768], P(None, 'batch', 'mem')
- self_output_grad: float32 [768, 768], P('batch', 'mem')
- cross_weights_grad: float32 [3, 768, 768], P(None, 'batch', 'mem')
- cross_output_grad: float32 [768, 768], P('batch', 'mem')
- expand_grad: float32 [2, 768, 2048], P(None, 'batch', 'mem')
- contract_grad: float32 [2048, 768], P('batch', 'mem')
The draws below stay inside these ranges and needn't reach their ends.
Inputs may be any that keep to these rules, and one draw needn't show every extreme that they name: `decoder_lengths`: in each group the 4 lengths sum to 1024; one of them, in a slot drawn from the seed, is 768. `memory_lengths`: in each group the 4 lengths sum to 2048; the slot of length 1536 is the slot of the group's longest decoder sequence. `distance_buckets`: Non-decreasing along the distance; 0 at distance 0, 31 from distance 768 - 1 on.
All inputs are finite; a program needn't handle non-finite values.
Results may differ from the reference program's by a relative error of at most 0.028.
Values may be sent and summed in bfloat16 or wider, within the bound.
No kernel may reach another device: no remote copies, remote signals or barrier semaphores. Data moves between devices by JAX's collectives and lax.ppermute only.
A program may use at most 128 MiB of HBM per device.

```python
import jax
import jax.numpy as jnp
from jax import lax

D = 768
H = 12
HD = 64
FF = 2048
BUCKETS = 32
DEC_GRP = 1024
SLOTS = 4
GROUPS = 16
MEM_GRP = 2048
DEC_LONG = 768
MEM_LONG = 1536


def long_place(key):
    return jax.random.randint(key, (GROUPS,), 0, SLOTS)


def short_lengths(key, remainder):
    group_keys = jax.random.split(key, GROUPS)

    def per_group(group_key):
        cut_points = jnp.sort(jax.random.permutation(group_key, remainder - 1)[:SLOTS - 2] + 1).astype(jnp.int32)
        edge_points = jnp.concatenate([jnp.zeros((1,), jnp.int32), cut_points, jnp.full((1,), remainder, jnp.int32)])
        return edge_points[1:] - edge_points[:-1]
    return jax.vmap(per_group)(group_keys)


def assemble(chosen, shorts, longest):
    slot_index = jnp.arange(SLOTS, dtype=jnp.int32)[None, :]
    source = jnp.clip(slot_index - (slot_index > chosen[:, None]).astype(jnp.int32), 0, SLOTS - 2)
    picked = jnp.take_along_axis(shorts, source, axis=1)
    return jnp.where(slot_index == chosen[:, None], longest, picked).astype(jnp.int32)


def draw_decoder_lengths(key, part):
    chosen = long_place(key)
    key = jax.random.fold_in(key, 5)
    return assemble(chosen, short_lengths(key, DEC_GRP - DEC_LONG), DEC_LONG)


def draw_memory_lengths(key, part):
    chosen = long_place(key)
    key = jax.random.fold_in(key, 7)
    return assemble(chosen, short_lengths(key, MEM_GRP - MEM_LONG), MEM_LONG)


def draw_distance_buckets(key, part):
    key = jax.random.fold_in(key, 3)
    values = jnp.sort(jax.random.randint(key, (DEC_LONG,), 0, BUCKETS))
    places = jnp.arange(DEC_LONG, dtype=jnp.int32)
    values = jnp.where(places == 0, 0, jnp.where(places == DEC_LONG - 1, BUCKETS - 1, values)).astype(jnp.int32)
    tail_part = jnp.full((DEC_GRP - DEC_LONG,), BUCKETS - 1, jnp.int32)
    return jnp.concatenate([values, tail_part]).astype(jnp.int32)


def steps_of(stream_key, shape, shards, low, largest):
    loudness, own = 1.0, jax.random.fold_in(stream_key, 6)
    for axis_at, blocks in shards:
        heights = jnp.exp(jax.random.uniform(jax.random.fold_in(own, axis_at), (blocks,), jnp.float32, low / len(shards), largest / len(shards)))
        loudness = loudness * jnp.repeat(heights, shape[axis_at] // blocks).reshape([-1 if axis == axis_at else 1 for axis in range(len(shape))])
    return loudness


def scatter_about(stream_key, dims, scale, bound, cuts=(), kind=jnp.bfloat16):
    drawn = jax.random.normal(stream_key, dims, jnp.float32) * scale
    if len(cuts) > 0:
        drawn = steps_of(stream_key, dims, cuts, -0.22, 0.18) * drawn
    return jnp.clip(drawn, min=-bound, max=bound).astype(kind)


def setup_inputs(seed: int = 0) -> dict:
    keys = jax.random.split(jax.random.key(seed), 15)
    return {
        "hidden": scatter_about(keys[0], (GROUPS, DEC_GRP, D), 1.0, 6.0, ((0, 16), (1, 2))),
        "memory": scatter_about(keys[1], (GROUPS, MEM_GRP, D), 1.0, 6.0, ((0, 16), (1, 2))),
        "decoder_lengths": draw_decoder_lengths(jax.random.fold_in(keys[14], 71), 0),
        "memory_lengths": draw_memory_lengths(jax.random.fold_in(keys[14], 71), 0),
        "distance_buckets": draw_distance_buckets(jax.random.fold_in(keys[14], 71), 0),
        "norm_gains": jnp.clip(1.0 + 0.1 * jax.random.normal(keys[5], (3, D), jnp.float32), 0.5, 1.5),
        "position_bias": scatter_about(keys[6], (BUCKETS, H), 1.0, 4.0, (), jnp.float32),
        "self_weights": scatter_about(keys[7], (3, D, D), (8 * D) ** -0.5, 0.078125, ((1, 16), (2, 2))),
        "self_output": scatter_about(keys[8], (D, D), 2.0, 12.0, ((0, 16), (1, 2))),
        "cross_weights": scatter_about(keys[9], (3, D, D), (8 * D) ** -0.5, 0.078125, ((1, 16), (2, 2))),
        "cross_output": scatter_about(keys[10], (D, D), 3.0, 16.0, ((0, 16), (1, 2))),
        "expand_weights": scatter_about(keys[11], (2, D, FF), D ** -0.5, 0.21875, ((1, 16), (2, 2))),
        "contract_weight": scatter_about(keys[12], (FF, D), FF ** -0.5, 0.125, ((0, 16), (1, 2))),
        "cotangent": scatter_about(keys[13], (GROUPS, DEC_GRP, D), 1.0, 6.0, ((0, 16), (1, 2))),
    }


EPSILON = 1e-06
NEGATIVE = -1e+30
HIGHEST_PRECISION = lax.Precision.HIGHEST

@jax.custom_vjp
def low(v):
    return lax.optimization_barrier(v.astype(jnp.bfloat16)).astype(jnp.float32)

@jax.custom_vjp
def low_back(v):
    return v

def low_keep(v):
    return (low(v), None)

def low_pass(kept, grad):
    return (grad,)

def back_keep(v):
    return (v, None)

def back_low(kept, grad):
    return (low(grad),)
low.defvjp(low_keep, low_pass)
low_back.defvjp(back_keep, back_low)

def product(left, right):
    return jnp.dot(left, right, precision=HIGHEST_PRECISION)

def rms_norm(values, gain_row):
    return values * lax.rsqrt(lax.optimization_barrier(jnp.mean(values * values, axis=-1, keepdims=True)) + EPSILON) * gain_row

def segment_ids(lengths, count):
    boundary = jnp.cumsum(lengths).astype(jnp.int32)
    places = jnp.arange(count, dtype=jnp.int32)
    return lax.optimization_barrier(jnp.sum((places[:, None] >= boundary[None, :]).astype(jnp.int32), axis=1))

def split_heads(matrix):
    return matrix.reshape(matrix.shape[0], H, HD).transpose(1, 0, 2)

def join_heads(stacked):
    return stacked.transpose(1, 0, 2).reshape(stacked.shape[1], H * HD)

def attend(queries, key_rows, value_rows, tables, buckets, allowed):

    def per_head(inputs):
        query_head, key_head, value_head, table_row = inputs
        scores = product(query_head, key_head.T) + table_row[buckets]
        scores = low_back(jnp.where(allowed, scores, NEGATIVE))
        attn_probs = jax.nn.softmax(scores, axis=-1)
        return product(low(attn_probs), value_head)
    return join_heads(lax.map(jax.checkpoint(per_head), (split_heads(queries), split_heads(key_rows), split_heads(value_rows), tables)))

def group_layer(tokens, memory_rows, decoder_sizes, memory_sizes, distance_buckets, norm_gains, position_bias, self_weights, self_output, cross_weights, cross_output, expand_weights, contract_weight):
    dec_seq = segment_ids(decoder_sizes, DEC_GRP)
    mem_seq = segment_ids(memory_sizes, MEM_GRP)
    places = jnp.arange(DEC_GRP, dtype=jnp.int32)
    distance = places[:, None] - places[None, :]
    self_allowed = (distance >= 0) & (dec_seq[:, None] == dec_seq[None, :])
    buckets = distance_buckets[jnp.clip(distance, 0, DEC_GRP - 1)]
    cross_allowed = dec_seq[:, None] == mem_seq[None, :]
    normed_self = low(rms_norm(tokens, norm_gains[0]))
    query_self = low_back(low(product(normed_self, self_weights[0])))
    key_self = low_back(low(product(normed_self, self_weights[1])))
    value_self = low_back(low(product(normed_self, self_weights[2])))
    attn_self = attend(query_self, key_self, value_self, position_bias.T, buckets, self_allowed)
    attn_self = low_back(low(attn_self))
    middle_one = tokens + low_back(product(attn_self, self_output))
    normed_cross = low(rms_norm(middle_one, norm_gains[1]))
    query_cross = low_back(low(product(normed_cross, cross_weights[0])))
    key_memory = low_back(low(product(memory_rows, cross_weights[1])))
    value_memory = low_back(low(product(memory_rows, cross_weights[2])))
    no_tables = jnp.zeros((H, 1), jnp.float32)
    no_buckets = jnp.zeros((1, 1), jnp.int32)
    attn_cross = attend(query_cross, key_memory, value_memory, no_tables, no_buckets, cross_allowed)
    attn_cross = low_back(low(attn_cross))
    middle_two = middle_one + low_back(product(attn_cross, cross_output))
    normed_feed = low(rms_norm(middle_two, norm_gains[2]))
    gate = low_back(product(normed_feed, expand_weights[0]))
    up_part = low_back(product(normed_feed, expand_weights[1]))
    activated = low(jax.nn.gelu(gate, approximate=True) * up_part)
    return middle_two + low_back(product(activated, contract_weight))

def reference(hidden, memory, decoder_lengths, memory_lengths, distance_buckets, norm_gains, position_bias, self_weights, self_output, cross_weights, cross_output, expand_weights, contract_weight, cotangent):
    floats = (hidden.astype(jnp.float32), memory.astype(jnp.float32), norm_gains.astype(jnp.float32), position_bias.astype(jnp.float32), self_weights.astype(jnp.float32), self_output.astype(jnp.float32), cross_weights.astype(jnp.float32), cross_output.astype(jnp.float32), expand_weights.astype(jnp.float32), contract_weight.astype(jnp.float32))

    def forward(all_tokens, all_memory, *parameters):

        def per_group(inputs):
            tokens, memory_rows, decoder_sizes, memory_sizes = inputs
            return group_layer(tokens, memory_rows, decoder_sizes, memory_sizes, distance_buckets, *parameters)
        return lax.map(jax.checkpoint(per_group), (all_tokens, all_memory, decoder_lengths, memory_lengths))
    result, pull_back = jax.vjp(forward, *floats)
    gradients = pull_back(cotangent.astype(jnp.float32))
    return (result.astype(jnp.bfloat16), gradients[0], gradients[1], gradients[2], gradients[3], gradients[4], gradients[5], gradients[6], gradients[7], gradients[8], gradients[9])
```

```python
import functools

import jax
import jax.numpy as jnp
from jax import lax
from jax.experimental import pallas as pl
from jax.experimental.pallas import tpu as pltpu
from jax.sharding import PartitionSpec as P

EPSILON = 1e-06
NEGATIVE = -1e30
F32 = jnp.float32
BF16 = jnp.bfloat16
EXACT = lax.Precision.HIGHEST
NT = (((1,), (1,)), ((), ()))
NN = (((1,), (0,)), ((), ()))


def rms_norm(values, gain_row):
    return (
        values * lax.rsqrt(jnp.mean(values * values, axis=-1, keepdims=True) + EPSILON) * gain_row
    )


def activate(gate_part, up_part):
    return jax.nn.gelu(gate_part, approximate=True) * up_part


def dot(left, right, dims):
    return lax.dot_general(left, right, dims, preferred_element_type=F32)


def bounds_of(sizes_ref):
    edges = [jnp.int32(0)]
    for slot in range(sizes_ref.shape[1]):
        edges.append(edges[-1] + sizes_ref[0, slot])
    return edges


def pick(place, edges, values):
    chosen = jnp.zeros_like(place) + values[0]
    for slot in range(1, len(edges) - 1):
        chosen = jnp.where(place >= edges[slot], values[slot], chosen)
    return chosen


def stack_heads(block, width):
    lane = lax.broadcasted_iota(jnp.int32, block.shape, 1)
    zero = jnp.zeros_like(block)
    return jnp.concatenate(
        [jnp.where(lane < width, block, zero), jnp.where(lane < width, zero, block)], axis=0
    )


def transposed_blocks(source_ref, scratch, step):
    for index in range(scratch.shape[0]):
        scratch[index] = source_ref[index * step : (index + 1) * step, :].T


def ranges(first, rows, q_edges, k_edges, causal, step):
    last = first + rows - 1
    starts, ends = k_edges[:-1], k_edges[1:]
    low_start = pick(first, q_edges, starts)
    high_start = pick(last, q_edges, starts)
    low_end = pick(first, q_edges, ends)
    high_end = pick(last, q_edges, ends)
    if causal:
        low_end = jnp.minimum(low_end, first + 1)
        high_end = jnp.minimum(high_end, last + 1)
    low = low_start // step
    high = (high_end + step - 1) // step
    clear_low = (high_start + step - 1) // step
    clear_high = low_end // step
    return low, high, clear_low, clear_high


def limits(first, rows, q_edges, k_edges, causal):
    place = lax.rem(lax.broadcasted_iota(jnp.int32, (1, 2 * rows), 1), rows) + first
    begin = pick(place, q_edges, k_edges[:-1])
    end = pick(place, q_edges, k_edges[1:])
    if causal:
        end = jnp.minimum(end, place + 1)
    return begin, end


def toeplitz(table_ref, tiles, rows):
    for delta in range(tiles.shape[0]):
        for head in range(2):
            base = table_ref[0, head : head + 1, delta * rows : (delta + 2) * rows]
            wide = jnp.broadcast_to(base, (rows, 2 * rows))
            wide = pltpu.roll(wide, 0, 1, stride=1, stride_axis=0)
            tiles[delta, :, head * rows : (head + 1) * rows] = wide[:, rows:]


def masked(scores, index, step, begin, end):
    place = lax.broadcasted_iota(jnp.int32, scores.shape, 0) + index * step
    return jnp.where((place >= begin) & (place < end), scores, NEGATIVE)


def forward_kernel(
    causal, step, width, first_ref, q_sizes, k_sizes, q_ref, k_ref, v_ref, *rest
):
    if causal:
        table_ref, out_ref, total_ref, value_t, scores, tiles = rest
    else:
        out_ref, total_ref, value_t, scores = rest
    blocks, rows = total_ref.shape[1], total_ref.shape[3] // 2
    q_edges = bounds_of(q_sizes)
    k_edges = bounds_of(k_sizes)
    transposed_blocks(v_ref, value_t, step)
    if causal:
        toeplitz(table_ref, tiles, rows)
    for block in range(blocks):
        first = first_ref[0] + block * rows
        low, high, clear_low, clear_high = ranges(first, rows, q_edges, k_edges, causal, step)
        begin, end = limits(first, rows, q_edges, k_edges, causal)
        queries = stack_heads(q_ref[block * rows : (block + 1) * rows, :], width)

        def measure(index, top):
            keys = k_ref[pl.ds(pl.multiple_of(index * step, step), step), :]
            block_scores = dot(keys, queries, NT)
            if causal:
                block_scores = block_scores + tiles[first // rows - index]
            clear = (index >= clear_low) & (index < clear_high)

            def plain():
                scores[index] = block_scores
                return jnp.max(block_scores, axis=0, keepdims=True)

            def cut():
                kept = masked(block_scores, index, step, begin, end)
                scores[index] = kept
                return jnp.max(kept, axis=0, keepdims=True)

            return jnp.maximum(top, lax.cond(clear, plain, cut))

        top = lax.fori_loop(low, high, measure, jnp.full((1, 2 * rows), NEGATIVE, F32))

        def gather(index, carry):
            total, out_a, out_b = carry
            weights = jnp.exp(scores[index] - top)
            total = total + jnp.sum(weights, axis=0, keepdims=True)
            rounded = weights.astype(BF16)
            out_a = out_a + dot(value_t[index, :width, :], rounded[:, :rows], NN)
            out_b = out_b + dot(value_t[index, width:, :], rounded[:, rows:], NN)
            return total, out_a, out_b

        zero = jnp.zeros((width, rows), F32)
        total, out_a, out_b = lax.fori_loop(
            low, high, gather, (jnp.zeros((1, 2 * rows), F32), zero, zero)
        )
        joined = jnp.concatenate([out_a / total[:, :rows], out_b / total[:, rows:]], axis=0)
        out_ref[block * rows : (block + 1) * rows, :] = joined.T.astype(BF16)
        total_ref[0, block] = top + jnp.log(total)


def backward_kernel(
    causal, step, width, first_ref, q_sizes, k_sizes, q_ref, k_ref, v_ref, g_ref, total_ref, *rest
):
    if causal:
        table_ref, dq_ref, dk_ref, dv_ref, diag_ref, key_t, probs, grads, dk, dv, tiles, sums = rest
    else:
        dq_ref, dk_ref, dv_ref, key_t, probs, grads, dk, dv = rest
    blocks, rows = total_ref.shape[1], total_ref.shape[3] // 2
    q_edges = bounds_of(q_sizes)
    k_edges = bounds_of(k_sizes)
    transposed_blocks(k_ref, key_t, step)
    dk[...] = jnp.zeros_like(dk)
    dv[...] = jnp.zeros_like(dv)
    if causal:
        toeplitz(table_ref, tiles, rows)
        sums[...] = jnp.zeros_like(sums)
    for block in range(blocks):
        first = first_ref[0] + block * rows
        low, high, clear_low, clear_high = ranges(first, rows, q_edges, k_edges, causal, step)
        begin, end = limits(first, rows, q_edges, k_edges, causal)
        queries = stack_heads(q_ref[block * rows : (block + 1) * rows, :], width)
        targets = stack_heads(g_ref[block * rows : (block + 1) * rows, :], width)
        total = total_ref[0, block]

        def measure(index, inner):
            here = pl.ds(pl.multiple_of(index * step, step), step)
            block_scores = dot(k_ref[here, :], queries, NT)
            if causal:
                block_scores = block_scores + tiles[first // rows - index]
            weights = jnp.exp(block_scores - total)
            clear = (index >= clear_low) & (index < clear_high)
            place = lax.broadcasted_iota(jnp.int32, weights.shape, 0) + index * step
            weights = jnp.where((place >= begin) & (place < end), weights, 0.0)
            pulled = dot(v_ref[here, :], targets, NT)
            probs[index] = weights
            grads[index] = pulled
            dv[here, :] += dot(weights.astype(BF16), targets, NN)
            return inner + jnp.sum(weights * pulled, axis=0, keepdims=True)

        inner = lax.fori_loop(low, high, measure, jnp.zeros((1, 2 * rows), F32))

        def gather(index, carry):
            out_a, out_b = carry
            here = pl.ds(pl.multiple_of(index * step, step), step)
            rounded = (probs[index] * (grads[index] - inner)).astype(BF16)
            dk[here, :] += dot(rounded, queries, NN)
            if causal:
                sums[first // rows - index] += rounded.astype(F32)
            out_a = out_a + dot(key_t[index, :width, :], rounded[:, :rows], NN)
            out_b = out_b + dot(key_t[index, width:, :], rounded[:, rows:], NN)
            return out_a, out_b

        zero = jnp.zeros((width, rows), F32)
        out_a, out_b = lax.fori_loop(low, high, gather, (zero, zero))
        joined = jnp.concatenate([out_a, out_b], axis=0)
        dq_ref[block * rows : (block + 1) * rows, :] = joined.T.astype(BF16)
    dk_ref[...] = dk[...].astype(BF16)
    dv_ref[...] = dv[...].astype(BF16)
    if causal:
        for delta in range(sums.shape[0]):
            for head in range(2):
                parts = jnp.zeros((8, 2 * rows), F32)
                for chunk in range(rows // 8):
                    piece = sums[delta, chunk * 8 : chunk * 8 + 8, head * rows : (head + 1) * rows]
                    piece = jnp.concatenate([jnp.zeros_like(piece), piece], axis=1)
                    parts = parts + (pltpu.roll(piece, 2 * rows - 8 * chunk, 1) if chunk else piece)
                line = parts[0:1]
                for row in range(1, 8):
                    line = line + pltpu.roll(parts[row : row + 1], 2 * rows - row, 1)
                diag_ref[0, head, delta : delta + 1, :] = line


def smem():
    return pl.BlockSpec(memory_space=pltpu.SMEM)


def attention_forward(first, q_sizes, k_sizes, queries, keys, values, table, width, step):
    causal = table is not None
    count, model = queries.shape
    key_count = keys.shape[0]
    rows = min(256, count)
    step = rows if causal else step
    pairs, blocks = model // (2 * width), count // rows
    column = lambda size: pl.BlockSpec((size, 2 * width), lambda pair: (0, pair))
    scratch = [
        pltpu.VMEM((key_count // step, 2 * width, step), BF16),
        pltpu.VMEM((key_count // step, step, 2 * rows), F32),
    ]
    in_specs = [smem(), smem(), smem(), column(count), column(key_count), column(key_count)]
    args = [first, q_sizes, k_sizes, queries, keys, values]
    if causal:
        in_specs.append(pl.BlockSpec((1, 2, table.shape[2]), lambda pair: (pair, 0, 0)))
        args.append(table)
        scratch.append(pltpu.VMEM((key_count // rows, rows, 2 * rows), F32))
    return pl.pallas_call(
        functools.partial(forward_kernel, causal, step, width),
        grid=(pairs,),
        in_specs=in_specs,
        out_specs=[
            column(count),
            pl.BlockSpec((1, blocks, 1, 2 * rows), lambda pair: (pair, 0, 0, 0)),
        ],
        out_shape=[
            jax.ShapeDtypeStruct((count, model), BF16),
            jax.ShapeDtypeStruct((pairs, blocks, 1, 2 * rows), F32),
        ],
        scratch_shapes=scratch,
        compiler_params=pltpu.CompilerParams(vmem_limit_bytes=56 << 20),
        name="self_forward" if causal else "cross_forward",
    )(*args)


def attention_backward(
    first, q_sizes, k_sizes, queries, keys, values, grads, totals, table, width, step
):
    causal = table is not None
    count, model = queries.shape
    key_count = keys.shape[0]
    rows = min(256, count)
    step = rows if causal else step
    pairs, blocks = model // (2 * width), count // rows
    column = lambda size: pl.BlockSpec((size, 2 * width), lambda pair: (0, pair))
    n_step = key_count // step
    scratch = [
        pltpu.VMEM((n_step, 2 * width, step), BF16),
        pltpu.VMEM((n_step, step, 2 * rows), F32),
        pltpu.VMEM((n_step, step, 2 * rows), F32),
        pltpu.VMEM((key_count, 2 * width), F32),
        pltpu.VMEM((key_count, 2 * width), F32),
    ]
    in_specs = [
        smem(), smem(), smem(), column(count), column(key_count), column(key_count), column(count),
        pl.BlockSpec((1, blocks, 1, 2 * rows), lambda pair: (pair, 0, 0, 0)),
    ]
    args = [first, q_sizes, k_sizes, queries, keys, values, grads, totals]
    out_specs = [column(count), column(key_count), column(key_count)]
    out_shape = [
        jax.ShapeDtypeStruct((count, model), BF16),
        jax.ShapeDtypeStruct((key_count, model), BF16),
        jax.ShapeDtypeStruct((key_count, model), BF16),
    ]
    if causal:
        in_specs.append(pl.BlockSpec((1, 2, table.shape[2]), lambda pair: (pair, 0, 0)))
        args.append(table)
        deltas = key_count // rows
        scratch += [pltpu.VMEM((deltas, rows, 2 * rows), F32), pltpu.VMEM((deltas, rows, 2 * rows), F32)]
        out_specs.append(pl.BlockSpec((1, 2, deltas, 2 * rows), lambda pair: (pair, 0, 0, 0)))
        out_shape.append(jax.ShapeDtypeStruct((pairs, 2, deltas, 2 * rows), F32))
    return pl.pallas_call(
        functools.partial(backward_kernel, causal, step, width),
        grid=(pairs,),
        in_specs=in_specs,
        out_specs=out_specs,
        out_shape=out_shape,
        scratch_shapes=scratch,
        compiler_params=pltpu.CompilerParams(vmem_limit_bytes=60 << 20),
        name="self_backward" if causal else "cross_backward",
    )(*args)


def shards(
    hidden,
    memory,
    decoder_lengths,
    memory_lengths,
    distance_buckets,
    norm_gains,
    position_bias,
    self_weights,
    self_output,
    cross_weights,
    cross_output,
    expand_weights,
    contract_weight,
    cotangent,
):
    mem_count = lax.axis_size("mem")
    mem_index = lax.axis_index("mem")
    row_count = hidden.shape[1]
    memory_count = memory.shape[1]
    model_width = hidden.shape[2]
    head_count = position_bias.shape[1]
    head_width = model_width // head_count
    bucket_count = position_bias.shape[0]
    key_count = row_count * mem_count
    first_row = mem_index * row_count
    within = (
        lax.all_gather(self_weights, "mem", axis=2, tiled=True),
        lax.all_gather(self_output, "mem", axis=1, tiled=True),
        lax.all_gather(cross_weights, "mem", axis=2, tiled=True),
        lax.all_gather(cross_output, "mem", axis=1, tiled=True),
        lax.all_gather(expand_weights, "mem", axis=2, tiled=True),
        lax.all_gather(contract_weight, "mem", axis=1, tiled=True),
    )
    full_weights = (
        lax.all_gather(within[0], "batch", axis=1, tiled=True),
        lax.all_gather(within[1], "batch", axis=0, tiled=True),
        lax.all_gather(within[2], "batch", axis=1, tiled=True),
        lax.all_gather(within[3], "batch", axis=0, tiled=True),
        lax.all_gather(within[4], "batch", axis=1, tiled=True),
        lax.all_gather(within[5], "batch", axis=0, tiled=True),
    )
    self_full, self_out_full, cross_full, cross_out_full, expand_full, contract_full = full_weights
    first = jnp.reshape(first_row, (1,)).astype(jnp.int32)
    rows = min(256, row_count)
    buckets = jnp.arange(bucket_count, dtype=jnp.int32)
    one_hot = (distance_buckets[:, None] == buckets[None, :]).astype(F32)
    distance_table = jnp.einsum("db,bh->hd", one_hot, position_bias, precision=EXACT)
    distance_table = jnp.pad(distance_table, ((0, 0), (rows, 0)))
    distance_table = distance_table.reshape(head_count // 2, 2, key_count + rows)
    tokens = hidden[0].astype(jnp.float32)
    normed_self, pull_self = jax.vjp(rms_norm, tokens, norm_gains[0])
    input_self = normed_self.astype(jnp.bfloat16)
    query_self = jnp.dot(input_self, self_full[0], preferred_element_type=jnp.float32).astype(
        jnp.bfloat16
    )
    key_self = jnp.dot(input_self, self_full[1], preferred_element_type=jnp.float32).astype(
        jnp.bfloat16
    )
    value_self = jnp.dot(input_self, self_full[2], preferred_element_type=jnp.float32).astype(
        jnp.bfloat16
    )
    self_pairs = lax.all_gather(jnp.stack([key_self, value_self]), "mem", axis=1, tiled=True)

    attn_self, self_totals = attention_forward(
        first, decoder_lengths, decoder_lengths, query_self, self_pairs[0], self_pairs[1],
        distance_table, head_width, rows,
    )
    middle_one = tokens + jnp.dot(attn_self, self_out_full, preferred_element_type=jnp.float32)
    normed_cross, pull_cross = jax.vjp(rms_norm, middle_one, norm_gains[1])
    input_cross = normed_cross.astype(jnp.bfloat16)
    query_cross = jnp.dot(input_cross, cross_full[0], preferred_element_type=jnp.float32).astype(
        jnp.bfloat16
    )
    memory_local = memory[0]
    key_memory = jnp.dot(memory_local, cross_full[1], preferred_element_type=jnp.float32).astype(
        jnp.bfloat16
    )
    value_memory = jnp.dot(memory_local, cross_full[2], preferred_element_type=jnp.float32).astype(
        jnp.bfloat16
    )
    memory_pairs = lax.all_gather(jnp.stack([key_memory, value_memory]), "mem", axis=1, tiled=True)

    attn_cross, cross_totals = attention_forward(
        first, decoder_lengths, memory_lengths, query_cross, memory_pairs[0], memory_pairs[1],
        None, head_width, 512,
    )
    middle_two = middle_one + jnp.dot(
        attn_cross, cross_out_full, preferred_element_type=jnp.float32
    )
    normed_feed, pull_feed = jax.vjp(rms_norm, middle_two, norm_gains[2])
    input_feed = normed_feed.astype(jnp.bfloat16)
    gate_part = jnp.dot(input_feed, expand_full[0], preferred_element_type=jnp.float32)
    up_part = jnp.dot(input_feed, expand_full[1], preferred_element_type=jnp.float32)
    activated, pull_activate = jax.vjp(activate, gate_part, up_part)
    hidden_act = activated.astype(jnp.bfloat16)
    result_rows = middle_two + jnp.dot(
        hidden_act, contract_full, preferred_element_type=jnp.float32
    )
    grad_branch_three = cotangent[0]
    grad_out = grad_branch_three.astype(jnp.float32)
    grad_contract = jnp.einsum(
        "rf,rd->fd", hidden_act, grad_branch_three, preferred_element_type=jnp.float32
    )
    grad_activated = jnp.einsum(
        "rd,fd->rf", grad_branch_three, contract_full, preferred_element_type=jnp.float32
    )
    grad_gate, grad_up = pull_activate(grad_activated)
    gate_rounded = grad_gate.astype(jnp.bfloat16)
    up_rounded = grad_up.astype(jnp.bfloat16)
    grad_expand = jnp.stack(
        [
            jnp.einsum("rd,rf->df", input_feed, gate_rounded, preferred_element_type=jnp.float32),
            jnp.einsum("rd,rf->df", input_feed, up_rounded, preferred_element_type=jnp.float32),
        ]
    )
    grad_input_feed = jnp.einsum(
        "rf,df->rd", gate_rounded, expand_full[0], preferred_element_type=jnp.float32
    ) + jnp.einsum("rf,df->rd", up_rounded, expand_full[1], preferred_element_type=jnp.float32)
    grad_norm_two, gain_grad_three = pull_feed(grad_input_feed)
    grad_middle_two = grad_out + grad_norm_two
    grad_branch_two = grad_middle_two.astype(jnp.bfloat16)
    grad_cross_out = jnp.einsum(
        "rd,re->de", attn_cross, grad_branch_two, preferred_element_type=jnp.float32
    )
    grad_attn_cross = jnp.einsum(
        "re,de->rd", grad_branch_two, cross_out_full, preferred_element_type=jnp.float32
    ).astype(jnp.bfloat16)

    grad_query_cross, cross_key_grads, cross_value_grads = attention_backward(
        first, decoder_lengths, memory_lengths, query_cross, memory_pairs[0], memory_pairs[1],
        grad_attn_cross, cross_totals, None, head_width, 512,
    )
    own_memory = lax.psum_scatter(
        jnp.stack([cross_key_grads, cross_value_grads]),
        "mem",
        scatter_dimension=1,
        tiled=True,
    )
    grad_cross = jnp.stack(
        [
            jnp.einsum(
                "rd,re->de", input_cross, grad_query_cross, preferred_element_type=jnp.float32
            ),
            jnp.einsum(
                "md,me->de", memory_local, own_memory[0], preferred_element_type=jnp.float32
            ),
            jnp.einsum(
                "md,me->de", memory_local, own_memory[1], preferred_element_type=jnp.float32
            ),
        ]
    )
    memory_gradient = jnp.einsum(
        "me,de->md", own_memory[0], cross_full[1], preferred_element_type=jnp.float32
    ) + jnp.einsum("me,de->md", own_memory[1], cross_full[2], preferred_element_type=jnp.float32)
    grad_input_cross = jnp.einsum(
        "re,de->rd", grad_query_cross, cross_full[0], preferred_element_type=jnp.float32
    )
    grad_norm_one, gain_grad_two = pull_cross(grad_input_cross)
    grad_middle_one = grad_middle_two + grad_norm_one
    grad_branch_one = grad_middle_one.astype(jnp.bfloat16)
    grad_self_out = jnp.einsum(
        "rd,re->de", attn_self, grad_branch_one, preferred_element_type=jnp.float32
    )
    grad_attn_self = jnp.einsum(
        "re,de->rd", grad_branch_one, self_out_full, preferred_element_type=jnp.float32
    ).astype(jnp.bfloat16)

    grad_query_self, self_key_grads, self_value_grads, diagonals = attention_backward(
        first, decoder_lengths, decoder_lengths, query_self, self_pairs[0], self_pairs[1],
        grad_attn_self, self_totals, distance_table, head_width, rows,
    )
    diagonals = diagonals.reshape(head_count, key_count // rows, 2 * rows)
    by_distance = jnp.zeros((head_count, key_count + rows), F32)
    for delta in range(key_count // rows):
        here = slice(delta * rows, delta * rows + 2 * rows)
        by_distance = by_distance.at[:, here].add(diagonals[:, delta])
    bias_partial = jnp.einsum("db,hd->bh", one_hot, by_distance[:, rows:], precision=EXACT)
    own_self = lax.psum_scatter(
        jnp.stack([self_key_grads, self_value_grads]),
        "mem",
        scatter_dimension=1,
        tiled=True,
    )
    grad_self = jnp.stack(
        [
            jnp.einsum(
                "rd,re->de", input_self, grad_query_self, preferred_element_type=jnp.float32
            ),
            jnp.einsum("rd,re->de", input_self, own_self[0], preferred_element_type=jnp.float32),
            jnp.einsum("rd,re->de", input_self, own_self[1], preferred_element_type=jnp.float32),
        ]
    )
    grad_input_self = (
        jnp.einsum("re,de->rd", grad_query_self, self_full[0], preferred_element_type=jnp.float32)
        + jnp.einsum("re,de->rd", own_self[0], self_full[1], preferred_element_type=jnp.float32)
        + jnp.einsum("re,de->rd", own_self[1], self_full[2], preferred_element_type=jnp.float32)
    )
    grad_norm_zero, gain_grad_one = pull_self(grad_input_self)
    grad_tokens = grad_middle_one + grad_norm_zero
    gain_sums, bias_sums = lax.psum(
        (jnp.stack([gain_grad_one, gain_grad_two, gain_grad_three]), bias_partial), ("batch", "mem")
    )
    summed_groups = (
        lax.psum_scatter(
            grad_self.astype(jnp.bfloat16), "batch", scatter_dimension=1, tiled=True
        ).astype(jnp.float32),
        lax.psum_scatter(
            grad_self_out.astype(jnp.bfloat16), "batch", scatter_dimension=0, tiled=True
        ).astype(jnp.float32),
        lax.psum_scatter(
            grad_cross.astype(jnp.bfloat16), "batch", scatter_dimension=1, tiled=True
        ).astype(jnp.float32),
        lax.psum_scatter(
            grad_cross_out.astype(jnp.bfloat16), "batch", scatter_dimension=0, tiled=True
        ).astype(jnp.float32),
        lax.psum_scatter(
            grad_expand.astype(jnp.bfloat16), "batch", scatter_dimension=1, tiled=True
        ).astype(jnp.float32),
        lax.psum_scatter(
            grad_contract.astype(jnp.bfloat16), "batch", scatter_dimension=0, tiled=True
        ).astype(jnp.float32),
    )
    final_grads = (
        lax.psum_scatter(
            summed_groups[0].astype(jnp.bfloat16), "mem", scatter_dimension=2, tiled=True
        ).astype(jnp.float32),
        lax.psum_scatter(
            summed_groups[1].astype(jnp.bfloat16), "mem", scatter_dimension=1, tiled=True
        ).astype(jnp.float32),
        lax.psum_scatter(
            summed_groups[2].astype(jnp.bfloat16), "mem", scatter_dimension=2, tiled=True
        ).astype(jnp.float32),
        lax.psum_scatter(
            summed_groups[3].astype(jnp.bfloat16), "mem", scatter_dimension=1, tiled=True
        ).astype(jnp.float32),
        lax.psum_scatter(
            summed_groups[4].astype(jnp.bfloat16), "mem", scatter_dimension=2, tiled=True
        ).astype(jnp.float32),
        lax.psum_scatter(
            summed_groups[5].astype(jnp.bfloat16), "mem", scatter_dimension=1, tiled=True
        ).astype(jnp.float32),
    )
    return (
        result_rows.astype(jnp.bfloat16)[None],
        grad_tokens[None],
        memory_gradient[None],
        gain_sums,
        bias_sums,
        final_grads[0],
        final_grads[1],
        final_grads[2],
        final_grads[3],
        final_grads[4],
        final_grads[5],
    )


def solution(mesh):
    placed = (
        P("batch", "mem", None),
        P("batch", "mem", None),
        P("batch", None),
        P("batch", None),
        P(),
        P(),
        P(),
        P(None, "batch", "mem"),
        P("batch", "mem"),
        P(None, "batch", "mem"),
        P("batch", "mem"),
        P(None, "batch", "mem"),
        P("batch", "mem"),
        P("batch", "mem", None),
    )
    return jax.shard_map(
        shards,
        mesh=mesh,
        in_specs=placed,
        out_specs=(
            P("batch", "mem", None),
            P("batch", "mem", None),
            P("batch", "mem", None),
            P(),
            P(),
            P(None, "batch", "mem"),
            P("batch", "mem"),
            P(None, "batch", "mem"),
            P("batch", "mem"),
            P(None, "batch", "mem"),
            P("batch", "mem"),
        ),
        check_vma=False,
    )
```

```python
import functools
import math

import jax
import jax.numpy as jnp
from jax import lax
from jax.experimental import pallas as pl
from jax.experimental.pallas import tpu as pltpu
from jax.sharding import PartitionSpec as P

EPSILON = 1e-06
NEGATIVE = -1e30
F32 = jnp.float32
BF16 = jnp.bfloat16
EXACT = lax.Precision.HIGHEST
GELU_SCALE = (2 / math.pi) ** 0.5
GELU_CUBE = 0.044715
LONG = pl.CostEstimate(flops=20_000_000_000, bytes_accessed=1_000, transcendentals=0)
MEDIUM = pl.CostEstimate(flops=6_000_000_000, bytes_accessed=1_000, transcendentals=0)
BRIEF = pl.CostEstimate(flops=2_000_000_000, bytes_accessed=1_000, transcendentals=0)
SHORT = pl.CostEstimate(flops=100_000, bytes_accessed=1_000, transcendentals=0)
NT = (((1,), (1,)), ((), ()))
NN = (((1,), (0,)), ((), ()))


def rms_norm(values, gain_row):
    return (
        values * lax.rsqrt(jnp.mean(values * values, axis=-1, keepdims=True) + EPSILON) * gain_row
    )


def activate(gate_part, up_part):
    return jax.nn.gelu(gate_part, approximate=True) * up_part


def dot(left, right, dims):
    return lax.dot_general(left, right, dims, preferred_element_type=F32)


def bounds_of(sizes_ref):
    edges = [jnp.int32(0)]
    for slot in range(sizes_ref.shape[1]):
        edges.append(edges[-1] + sizes_ref[0, slot])
    return edges


def pick(place, edges, values):
    chosen = jnp.zeros_like(place) + values[0]
    for slot in range(1, len(edges) - 1):
        chosen = jnp.where(place >= edges[slot], values[slot], chosen)
    return chosen


def stack_heads(block, width):
    lane = lax.broadcasted_iota(jnp.int32, block.shape, 1)
    zero = jnp.zeros_like(block)
    return jnp.concatenate(
        [jnp.where(lane < width, block, zero), jnp.where(lane < width, zero, block)], axis=0
    )


def transposed_blocks(source_ref, scratch, step):
    for index in range(scratch.shape[0]):
        scratch[index] = source_ref[index * step : (index + 1) * step, :].T


def ranges(first, rows, q_edges, k_edges, causal, step):
    last = first + rows - 1
    starts, ends = k_edges[:-1], k_edges[1:]
    low_start = pick(first, q_edges, starts)
    high_start = pick(last, q_edges, starts)
    low_end = pick(first, q_edges, ends)
    high_end = pick(last, q_edges, ends)
    if causal:
        low_end = jnp.minimum(low_end, first + 1)
        high_end = jnp.minimum(high_end, last + 1)
    low = low_start // step
    high = (high_end + step - 1) // step
    clear_low = (high_start + step - 1) // step
    clear_high = low_end // step
    return low, high, clear_low, clear_high


def limits(first, rows, q_edges, k_edges, causal):
    place = lax.rem(lax.broadcasted_iota(jnp.int32, (1, 2 * rows), 1), rows) + first
    begin = pick(place, q_edges, k_edges[:-1])
    end = pick(place, q_edges, k_edges[1:])
    if causal:
        end = jnp.minimum(end, place + 1)
    return begin, end


def toeplitz(table_ref, tiles, rows):
    for delta in range(tiles.shape[0]):
        for head in range(2):
            base = table_ref[0, head : head + 1, delta * rows : (delta + 2) * rows]
            wide = jnp.broadcast_to(base, (rows, 2 * rows))
            wide = pltpu.roll(wide, 0, 1, stride=1, stride_axis=0)
            tiles[delta, :, head * rows : (head + 1) * rows] = wide[:, rows:]


def masked(scores, index, step, begin, end):
    place = lax.broadcasted_iota(jnp.int32, scores.shape, 0) + index * step
    return jnp.where((place >= begin) & (place < end), scores, NEGATIVE)


def forward_kernel(
    causal, step, width, first_ref, q_sizes, k_sizes, q_ref, k_ref, v_ref, *rest
):
    if causal:
        table_ref, out_ref, total_ref, value_t, scores, tiles = rest
    else:
        out_ref, total_ref, value_t, scores = rest
    blocks, rows = total_ref.shape[1], total_ref.shape[3] // 2
    q_edges = bounds_of(q_sizes)
    k_edges = bounds_of(k_sizes)
    transposed_blocks(v_ref, value_t, step)
    if causal:
        toeplitz(table_ref, tiles, rows)
    for block in range(blocks):
        first = first_ref[0] + block * rows
        low, high, clear_low, clear_high = ranges(first, rows, q_edges, k_edges, causal, step)
        begin, end = limits(first, rows, q_edges, k_edges, causal)
        queries = stack_heads(q_ref[block * rows : (block + 1) * rows, :], width)

        def measure(index, top):
            keys = k_ref[pl.ds(pl.multiple_of(index * step, step), step), :]
            block_scores = dot(keys, queries, NT)
            if causal:
                block_scores = block_scores + tiles[first // rows - index]
            clear = (index >= clear_low) & (index < clear_high)

            def plain():
                scores[index] = block_scores
                return jnp.max(block_scores, axis=0, keepdims=True)

            def cut():
                kept = masked(block_scores, index, step, begin, end)
                scores[index] = kept
                return jnp.max(kept, axis=0, keepdims=True)

            return jnp.maximum(top, lax.cond(clear, plain, cut))

        top = lax.fori_loop(low, high, measure, jnp.full((1, 2 * rows), NEGATIVE, F32))

        def gather(index, carry):
            total, out_a, out_b = carry
            weights = jnp.exp(scores[index] - top)
            total = total + jnp.sum(weights, axis=0, keepdims=True)
            rounded = weights.astype(BF16)
            out_a = out_a + dot(value_t[index, :width, :], rounded[:, :rows], NN)
            out_b = out_b + dot(value_t[index, width:, :], rounded[:, rows:], NN)
            return total, out_a, out_b

        zero = jnp.zeros((width, rows), F32)
        total, out_a, out_b = lax.fori_loop(
            low, high, gather, (jnp.zeros((1, 2 * rows), F32), zero, zero)
        )
        joined = jnp.concatenate([out_a / total[:, :rows], out_b / total[:, rows:]], axis=0)
        out_ref[block * rows : (block + 1) * rows, :] = joined.T.astype(BF16)
        total_ref[0, block] = top + jnp.log(total)


def backward_kernel(
    causal, step, width, first_ref, q_sizes, k_sizes, q_ref, k_ref, v_ref, g_ref, total_ref, *rest
):
    if causal:
        table_ref, dq_ref, dk_ref, dv_ref, diag_ref, key_t, probs, grads, dk, dv, tiles, sums = rest
    else:
        dq_ref, dk_ref, dv_ref, key_t, probs, grads, dk, dv = rest
    blocks, rows = total_ref.shape[1], total_ref.shape[3] // 2
    q_edges = bounds_of(q_sizes)
    k_edges = bounds_of(k_sizes)
    transposed_blocks(k_ref, key_t, step)
    dk[...] = jnp.zeros_like(dk)
    dv[...] = jnp.zeros_like(dv)
    if causal:
        toeplitz(table_ref, tiles, rows)
        sums[...] = jnp.zeros_like(sums)
    for block in range(blocks):
        first = first_ref[0] + block * rows
        low, high, clear_low, clear_high = ranges(first, rows, q_edges, k_edges, causal, step)
        begin, end = limits(first, rows, q_edges, k_edges, causal)
        queries = stack_heads(q_ref[block * rows : (block + 1) * rows, :], width)
        targets = stack_heads(g_ref[block * rows : (block + 1) * rows, :], width)
        total = total_ref[0, block]

        def measure(index, inner):
            here = pl.ds(pl.multiple_of(index * step, step), step)
            block_scores = dot(k_ref[here, :], queries, NT)
            if causal:
                block_scores = block_scores + tiles[first // rows - index]
            weights = jnp.exp(block_scores - total)
            clear = (index >= clear_low) & (index < clear_high)
            place = lax.broadcasted_iota(jnp.int32, weights.shape, 0) + index * step
            weights = jnp.where((place >= begin) & (place < end), weights, 0.0)
            pulled = dot(v_ref[here, :], targets, NT)
            probs[index] = weights
            grads[index] = pulled
            dv[here, :] += dot(weights.astype(BF16), targets, NN)
            return inner + jnp.sum(weights * pulled, axis=0, keepdims=True)

        inner = lax.fori_loop(low, high, measure, jnp.zeros((1, 2 * rows), F32))

        def gather(index, carry):
            out_a, out_b = carry
            here = pl.ds(pl.multiple_of(index * step, step), step)
            rounded = (probs[index] * (grads[index] - inner)).astype(BF16)
            dk[here, :] += dot(rounded, queries, NN)
            if causal:
                sums[first // rows - index] += rounded.astype(F32)
            out_a = out_a + dot(key_t[index, :width, :], rounded[:, :rows], NN)
            out_b = out_b + dot(key_t[index, width:, :], rounded[:, rows:], NN)
            return out_a, out_b

        zero = jnp.zeros((width, rows), F32)
        out_a, out_b = lax.fori_loop(low, high, gather, (zero, zero))
        joined = jnp.concatenate([out_a, out_b], axis=0)
        dq_ref[block * rows : (block + 1) * rows, :] = joined.T.astype(BF16)
    dk_ref[...] = dk[...].astype(BF16)
    dv_ref[...] = dv[...].astype(BF16)
    if causal:
        for delta in range(sums.shape[0]):
            for head in range(2):
                parts = jnp.zeros((8, 2 * rows), F32)
                for chunk in range(rows // 8):
                    piece = sums[delta, chunk * 8 : chunk * 8 + 8, head * rows : (head + 1) * rows]
                    piece = jnp.concatenate([jnp.zeros_like(piece), piece], axis=1)
                    parts = parts + (pltpu.roll(piece, 2 * rows - 8 * chunk, 1) if chunk else piece)
                line = parts[0:1]
                for row in range(1, 8):
                    line = line + pltpu.roll(parts[row : row + 1], 2 * rows - row, 1)
                diag_ref[0, head, delta : delta + 1, :] = line


def unread():
    return pl.BlockSpec(memory_space=pl.ANY)


def ignoring(body, first, count):
    return lambda *refs: body(*refs[:first], *refs[first + count :])


def hold(values, after):
    count = len(values)
    return pl.pallas_call(
        lambda *refs: None,
        in_specs=[unread()] * (count + len(after)),
        out_specs=[unread()] * count,
        out_shape=[jax.ShapeDtypeStruct(value.shape, value.dtype) for value in values],
        input_output_aliases={index: index for index in range(count)},
        cost_estimate=SHORT,
        name="hold",
    )(*values, *after)


def smem():
    return pl.BlockSpec(memory_space=pltpu.SMEM)


def attention_forward(
    first, q_sizes, k_sizes, queries, keys, values, table, width, step, span, after=(), cost=LONG
):
    causal = table is not None
    count, model = queries.shape
    key_count = keys.shape[0]
    rows = min(256, count)
    step = rows if causal else step
    pair_first, pairs = span
    blocks = count // rows
    column = lambda size: pl.BlockSpec((size, 2 * width), lambda pair: (0, pair + pair_first))
    result = lambda size: pl.BlockSpec((size, 2 * width), lambda pair: (0, pair))
    scratch = [
        pltpu.VMEM((key_count // step, 2 * width, step), BF16),
        pltpu.VMEM((key_count // step, step, 2 * rows), F32),
    ]
    in_specs = [smem(), smem(), smem(), column(count), column(key_count), column(key_count)]
    args = [first, q_sizes, k_sizes, queries, keys, values]
    if causal:
        in_specs.append(
            pl.BlockSpec((1, 2, table.shape[2]), lambda pair: (pair + pair_first, 0, 0))
        )
        args.append(table)
        scratch.append(pltpu.VMEM((key_count // rows, rows, 2 * rows), F32))
    return pl.pallas_call(
        ignoring(functools.partial(forward_kernel, causal, step, width), len(args), len(after)),
        grid=(pairs,),
        in_specs=in_specs + [unread()] * len(after),
        out_specs=[
            result(count),
            pl.BlockSpec((1, blocks, 1, 2 * rows), lambda pair: (pair, 0, 0, 0)),
        ],
        out_shape=[
            jax.ShapeDtypeStruct((count, pairs * 2 * width), BF16),
            jax.ShapeDtypeStruct((pairs, blocks, 1, 2 * rows), F32),
        ],
        scratch_shapes=scratch,
        compiler_params=pltpu.CompilerParams(vmem_limit_bytes=56 << 20),
        cost_estimate=cost,
        name="self_forward" if causal else "cross_forward",
    )(*args, *after)


def attention_backward(
    first, q_sizes, k_sizes, queries, keys, values, grads, totals, table, width, step, span, after=()
):
    causal = table is not None
    count, model = queries.shape
    key_count = keys.shape[0]
    rows = min(256, count)
    step = rows if causal else step
    pair_first, pairs = span
    blocks = count // rows
    column = lambda size: pl.BlockSpec((size, 2 * width), lambda pair: (0, pair + pair_first))
    result = lambda size: pl.BlockSpec((size, 2 * width), lambda pair: (0, pair))
    n_step = key_count // step
    scratch = [
        pltpu.VMEM((n_step, 2 * width, step), BF16),
        pltpu.VMEM((n_step, step, 2 * rows), F32),
        pltpu.VMEM((n_step, step, 2 * rows), F32),
        pltpu.VMEM((key_count, 2 * width), F32),
        pltpu.VMEM((key_count, 2 * width), F32),
    ]
    in_specs = [
        smem(), smem(), smem(), column(count), column(key_count), column(key_count), column(count),
        pl.BlockSpec((1, blocks, 1, 2 * rows), lambda pair: (pair + pair_first, 0, 0, 0)),
    ]
    args = [first, q_sizes, k_sizes, queries, keys, values, grads, totals]
    out_specs = [result(count), result(key_count), result(key_count)]
    out_shape = [
        jax.ShapeDtypeStruct((count, pairs * 2 * width), BF16),
        jax.ShapeDtypeStruct((key_count, pairs * 2 * width), BF16),
        jax.ShapeDtypeStruct((key_count, pairs * 2 * width), BF16),
    ]
    if causal:
        in_specs.append(
            pl.BlockSpec((1, 2, table.shape[2]), lambda pair: (pair + pair_first, 0, 0))
        )
        args.append(table)
        deltas = key_count // rows
        scratch += [pltpu.VMEM((deltas, rows, 2 * rows), F32), pltpu.VMEM((deltas, rows, 2 * rows), F32)]
        out_specs.append(pl.BlockSpec((1, 2, deltas, 2 * rows), lambda pair: (pair, 0, 0, 0)))
        out_shape.append(jax.ShapeDtypeStruct((pairs, 2, deltas, 2 * rows), F32))
    return pl.pallas_call(
        ignoring(functools.partial(backward_kernel, causal, step, width), len(args), len(after)),
        grid=(pairs,),
        in_specs=in_specs + [unread()] * len(after),
        out_specs=out_specs,
        out_shape=out_shape,
        scratch_shapes=scratch,
        compiler_params=pltpu.CompilerParams(vmem_limit_bytes=60 << 20),
        cost_estimate=LONG,
        name="self_backward" if causal else "cross_backward",
    )(*args, *after)


def send_batch(block, distance):
    count = lax.axis_size("batch")
    return lax.ppermute(block, "batch", [(i, i ^ distance) for i in range(count)])


def send_mem(block):
    return lax.ppermute(block, "mem", [(0, 1), (1, 0)])


def place(pieces, mine):
    ordered = []
    for index in range(len(pieces)):
        chosen = pieces[0]
        for distance in range(1, len(pieces)):
            chosen = jnp.where(mine == (index ^ distance), pieces[distance], chosen)
        ordered.append(chosen)
    return jnp.stack(ordered)


def grid_place():
    batch_index = lax.axis_index("batch")
    return batch_index >> 2, (batch_index >> 1) & 1, batch_index & 1, lax.axis_index("mem")


def gather_plain(shard):
    within = lax.all_gather(shard, "mem", axis=2, tiled=True)
    return lax.all_gather(within, "batch", axis=1, tiled=True)


def scatter_plain(whole):
    part = lax.psum_scatter(whole, "batch", scatter_dimension=1, tiled=True)
    return lax.psum_scatter(part, "mem", scatter_dimension=2, tiled=True).astype(F32)


def whole_spec(shape):
    return pl.BlockSpec(tuple(shape), lambda *_: (0,) * len(shape))


def kernel_call(
    body, name, grid, in_specs, out_specs, out_shape, args, scratch=(), after=()
):
    return pl.pallas_call(
        ignoring(body, len(args), len(after)),
        grid=grid,
        in_specs=in_specs + [unread()] * len(after),
        out_specs=out_specs,
        out_shape=out_shape,
        scratch_shapes=list(scratch),
        compiler_params=pltpu.CompilerParams(vmem_limit_bytes=60 << 20),
        cost_estimate=MEDIUM if name.endswith("kernel") else SHORT,
        name=name,
    )(*args, *after)


def simple_call(body, name, out_shape, args, after=(), spot=None):
    lead = [] if spot is None else [spot]
    return kernel_call(
        body, name, (1,), [smem()] * len(lead) + [whole_spec(arg.shape) for arg in args],
        [whole_spec(shape.shape) for shape in out_shape], out_shape, (*lead, *args), after=after,
    )


def place_line(spot, pieces, after=()):
    count = len(pieces)
    half = count // 2
    shape = jax.ShapeDtypeStruct((half, *pieces[0].shape), BF16)

    def body(spot_ref, *refs):
        low_ref, high_ref = refs[count:]
        for distance in range(count):
            z = spot_ref[0] ^ distance

            @pl.when(z < half)
            def lower():
                low_ref[z] = refs[distance][...]

            @pl.when(z >= half)
            def upper():
                high_ref[z - half] = refs[distance][...]

    return simple_call(body, "place_line", [shape, shape], pieces, after, spot)


def place_pairs(spot, axes, pairs, after=()):
    shapes = [jax.ShapeDtypeStruct((2, *own.shape), BF16) for own, _ in pairs]

    def body(spot_ref, *refs):
        for index, axis in enumerate(axes):
            own_ref, far_ref, out_ref = refs[2 * index], refs[2 * index + 1], refs[2 * len(axes) + index]
            mine = spot_ref[axis]
            out_ref[mine] = own_ref[...]
            out_ref[1 - mine] = far_ref[...]

    return simple_call(body, "place_pairs", shapes, [part for pair in pairs for part in pair], after, spot)


def line_of(shard):
    return [shard] + [send_batch(shard, 4 * d) for d in range(1, lax.axis_size("batch") // 4)]


def gather_first(spot, low, high, after=()):
    return place_pairs(spot, (3, 1), ((low, send_mem(low)), (high, send_batch(high, 2))), after)


def gather_second(spot, low, high, after=()):
    return place_pairs(spot, (1, 3), ((low, send_batch(low, 2)), (high, send_mem(high))), after)


def gather_cores(low, high):
    return low, send_batch(low, 1), high, send_batch(high, 1)


def add_refs(refs):
    total = refs[0][...].astype(F32)
    for ref in refs[1:]:
        total = total + ref[...].astype(F32)
    return total


def scatter_step(groups, after, axes):
    def body(*refs):
        outs = refs[2 * len(groups) :]
        for index, axis in enumerate(axes):
            total = add_refs(refs[2 * index : 2 * index + 2]).astype(BF16)
            cut = (slice(None),) * axis
            outs[2 * index][...] = total[(*cut, 0)]
            outs[2 * index + 1][...] = total[(*cut, 1)]

    in_specs, out_specs, shapes, args = [], [], [], []
    for (kept, received), axis in zip(groups, axes):
        args += [kept, received]
        block = (1, *kept.shape[1:])
        zeros = (0,) * (len(block) - 1)
        in_specs += [pl.BlockSpec(block, lambda z, zeros=zeros: (z, *zeros))] * 2
        rest = kept.shape[:axis] + kept.shape[axis + 1 :]
        out_specs += [pl.BlockSpec((1, *rest[1:]), lambda z, zeros=zeros: (z, *zeros[1:]))] * 2
        shapes += [jax.ShapeDtypeStruct(rest, BF16)] * 2
    outs = kernel_call(
        body, "scatter_step", (args[0].shape[0],), in_specs, out_specs, shapes, args, after=after
    )
    return [tuple(outs[2 * index : 2 * index + 2]) for index in range(len(groups))]


def scatter_to_line(groups, after):
    count = groups[0][0].shape[0]

    def body(*refs):
        outs = refs[2 * len(groups) :]
        for index in range(len(groups)):
            total = add_refs(refs[2 * index : 2 * index + 2]).astype(BF16)
            for distance in range(count):
                outs[count * index + distance][...] = total[distance]

    shapes = [jax.ShapeDtypeStruct(kept.shape[1:], BF16) for kept, _ in groups for _ in range(count)]
    outs = simple_call(body, "scatter_to_line", shapes, [part for group in groups for part in group], after)
    return [outs[count * index : count * (index + 1)] for index in range(len(groups))]


def send_line(pieces):
    return [pieces[0]] + [send_batch(pieces[d], 4 * d) for d in range(1, len(pieces))]


def scatter_end(groups, out_shapes, moves, after):
    def body(*refs):
        outs = refs[sum(len(group) for group in groups) :]
        totals, start = [], 0
        for group in groups:
            totals.append(add_refs(refs[start : start + len(group)]))
            start += len(group)
        for group, first, rows, out, index in moves:
            outs[out][index] = totals[group][first : first + rows]

    shapes = [jax.ShapeDtypeStruct(shape, F32) for shape in out_shapes]
    return simple_call(body, "scatter_end", shapes, [part for group in groups for part in group], after)


def square_moves(units, slab, columns, outputs):
    moves, used = [], {}
    for group, matrix, block in units:
        first = used.get(group, 0)
        used[group] = first + slab
        out, index = outputs[matrix]
        span = slice(block * 128, (block + 1) * 128)
        moves.append((group, first, slab, out, (slice(None), span) if index is None else (index, slice(None), span)))
    return moves


def sum_small(block, distances, after):
    count = lax.axis_size("batch") * 2
    parts = [block]
    for distance in distances:
        pairs = [(i, i ^ distance) for i in range(count)]
        parts.append(lax.ppermute(block, ("batch", "mem"), pairs))

    def body(*refs):
        values = [ref[...] for ref in refs[:-1]]
        while len(values) > 1:
            values = [values[i] + values[i + 1] for i in range(0, len(values), 2)]
        refs[-1][...] = values[0]

    return simple_call(body, "sum_small", [jax.ShapeDtypeStruct(block.shape, F32)], parts, after)[0]


def add_rows(block, far, after):
    rows, width = block.shape

    def body(one_ref, two_ref, out_ref):
        out_ref[...] = one_ref[...] + two_ref[...].astype(F32)

    spec = pl.BlockSpec((rows // 4, width), lambda i: (i, 0))
    shape = jax.ShapeDtypeStruct(block.shape, F32)
    return kernel_call(body, "add_rows", (4,), [spec, spec], spec, shape, (block, far), after=after)


def chosen(block, axis, index):
    return lax.dynamic_index_in_dim(block, index, axis, keepdims=False)


def all_rows(block):
    if lax.axis_size("mem") == 2:
        return place([block, send_mem(block)], lax.axis_index("mem")).reshape(-1, block.shape[1])
    return lax.all_gather(block, "mem", axis=0, tiled=True)


def own_rows(partial_rows):
    mem_count = lax.axis_size("mem")
    if mem_count == 2:
        halves = partial_rows.reshape(2, -1, partial_rows.shape[1])
        index = lax.axis_index("mem")
        far = send_mem(chosen(halves, 0, 1 - index).astype(BF16))
        return chosen(halves, 0, index) + far.astype(F32)
    return lax.psum_scatter(
        partial_rows.astype(BF16), "mem", scatter_dimension=0, tiled=True
    ).astype(F32)


def mm(left, right):
    return dot(left, right, NN)


def mm_t(left, right):
    return dot(left, right, NT)


def t_mm(left, right):
    return dot(left, right, (((0,), (0,)), ((), ())))


def weight_specs(pack, index):
    return [
        pl.BlockSpec(
            part.shape[:3] + (1,) + part.shape[4:], lambda *_: (0, 0, 0, index, 0, 0)
        )
        for part in pack
    ]


def columns_of(spot_ref, refs, index, column):
    low_own, low_far, high_own, high_far = refs
    half = low_own.shape[2]
    pieces = []
    for z in range(2 * half):
        for y in range(2):
            for core in range(2):
                if z < half:
                    spot = (y, column, z, index)
                    own, far = low_own[spot], low_far[spot]
                else:
                    spot = (column, y, z - half, index)
                    own, far = high_own[spot], high_far[spot]
                pieces.append(jnp.where(spot_ref[2] == core, own, far))
    return jnp.concatenate(pieces, axis=0)


def matrix_of(spot_ref, refs, index=0):
    return jnp.concatenate(
        [columns_of(spot_ref, refs, index, 0), columns_of(spot_ref, refs, index, 1)], axis=1
    )


def join(parts):
    return jnp.concatenate([part[...] for part in parts], axis=1)


def store_shard(place_ref, keep_ref, send_ref, z, y, x, unit, even, odd):
    at_z, at_y, at_core, at_x = (place_ref[axis] for axis in range(4))
    rows = even.shape[0]
    span = slice(unit, unit + rows)
    keep_ref[z ^ at_z, y ^ at_y, x ^ at_x, span, :] = jnp.where(at_core == 0, even, odd)
    send_ref[z ^ at_z, y ^ at_y, x ^ at_x, span, :] = jnp.where(at_core == 0, odd, even)


def store_square(place_ref, targets, matrix, z_count):
    rounded = matrix.astype(BF16)
    rows, columns = rounded.shape[0] // (4 * z_count), rounded.shape[1] // 2
    for z in range(z_count):
        for y in range(2):
            start = (z * 2 + y) * 2 * rows
            for x in range(2):
                for index, (keep_ref, send_ref, unit) in enumerate(targets):
                    span = slice(x * columns + index * 128, x * columns + (index + 1) * 128)
                    store_shard(
                        place_ref, keep_ref, send_ref, z, y, x, unit,
                        rounded[start : start + rows, span],
                        rounded[start + rows : start + 2 * rows, span],
                    )


def piece_shape(z_count, rows):
    return jax.ShapeDtypeStruct((z_count, 2, 2, rows, 128), BF16)


def inverse_rms(values):
    return lax.rsqrt(jnp.mean(values * values, axis=1, keepdims=True) + EPSILON)


def norm_backward(values, gain_row, grads):
    scale = inverse_rms(values)
    normed = values * scale
    gain_grad = jnp.sum(grads * normed, axis=0, keepdims=True)
    pulled = grads * gain_row
    inner = jnp.mean(pulled * normed, axis=1, keepdims=True)
    return scale * (pulled - normed * inner), gain_grad


def project_self(place, own, far, gains, pack, after):
    rows, width = own.shape
    columns = width // 2

    def body(place_ref, own_ref, far_ref, gains_ref, *refs):
        weights, (q_ref, k_ref, v_ref, normed_ref) = refs[:4], refs[4:]
        at_x = place_ref[3]
        here = pl.ds(pl.multiple_of(at_x * rows, rows), rows)
        there = pl.ds(pl.multiple_of((1 - at_x) * rows, rows), rows)

        @pl.when(pl.program_id(0) == 0)
        def normalise():
            for source, span in ((own_ref, here), (far_ref, there)):
                values = source[...].astype(F32)
                normed_ref[span, :] = (values * inverse_rms(values) * gains_ref[0:1, :]).astype(BF16)

        q_ref[...] = mm(normed_ref[here, :], columns_of(place_ref, weights, 0, 0)).astype(BF16)
        normed = normed_ref[...]
        k_ref[...] = mm(normed, columns_of(place_ref, weights, 1, 0)).astype(BF16)
        v_ref[...] = mm(normed, columns_of(place_ref, weights, 2, 0)).astype(BF16)

    low, high = pack[0], pack[2]
    low_spec = pl.BlockSpec(low.shape[:1] + (1,) + low.shape[2:], lambda m: (0, m, 0, 0, 0, 0))
    high_spec = pl.BlockSpec((1,) + high.shape[1:], lambda m: (m, 0, 0, 0, 0, 0))
    return kernel_call(
        body, "project_self_kernel", (2,),
        [
            smem(), whole_spec(own.shape), whole_spec(far.shape), whole_spec(gains.shape),
            low_spec, low_spec, high_spec, high_spec,
        ],
        [
            pl.BlockSpec((rows, columns), lambda m: (0, m)),
            pl.BlockSpec((2 * rows, columns), lambda m: (0, m)),
            pl.BlockSpec((2 * rows, columns), lambda m: (0, m)),
            whole_spec((2 * rows, width)),
        ],
        [
            jax.ShapeDtypeStruct((rows, width), BF16),
            jax.ShapeDtypeStruct((2 * rows, width), BF16),
            jax.ShapeDtypeStruct((2 * rows, width), BF16),
            jax.ShapeDtypeStruct((2 * rows, width), BF16),
        ],
        (place, own, far, gains, *pack),
        after=after,
    )


def specs_of(arrays):
    return [whole_spec(array.shape) for array in arrays]


def after_self(place, own, attn, gains, pack):
    rows, width = own.shape
    count = len(attn)

    def body(place_ref, own_ref, gains_ref, *refs):
        attended = join(refs[:count])
        out_weight, q_weight = refs[count : count + 4], refs[count + 4 : count + 8]
        middle_ref, normed_ref, q_ref = refs[count + 8 :]
        middle = own_ref[...].astype(F32) + mm(attended, matrix_of(place_ref, out_weight))
        middle_ref[...] = middle
        normed = (middle * inverse_rms(middle) * gains_ref[1:2, :]).astype(BF16)
        normed_ref[...] = normed
        q_ref[...] = mm(normed, matrix_of(place_ref, q_weight)).astype(BF16)

    return kernel_call(
        body, "after_self_kernel", (1,),
        [smem(), whole_spec(own.shape), whole_spec(gains.shape), *specs_of(attn)]
        + weight_specs(pack, 3) + weight_specs(pack, 0),
        [whole_spec(own.shape)] * 3,
        [
            jax.ShapeDtypeStruct((rows, width), F32),
            jax.ShapeDtypeStruct((rows, width), BF16),
            jax.ShapeDtypeStruct((rows, width), BF16),
        ],
        (place, own, gains, *attn, *pack, *pack),
    )


def three_way(step, own_ref, far_a, far_b):
    return jnp.where(step < 2, own_ref[...], jnp.where(step == 2, far_a[...], far_b[...]))


def project_memory(place, own, far, pack):
    rows, width = own.shape
    step = rows // 2

    def body(place_ref, own_ref, far_a, far_b, *refs):
        k_ref, v_ref = refs[8:]
        source = three_way(pl.program_id(0), own_ref, far_a, far_b)
        k_ref[...] = mm(source, matrix_of(place_ref, refs[:4])).astype(BF16)
        v_ref[...] = mm(source, matrix_of(place_ref, refs[4:8])).astype(BF16)

    def result(i, place_ref):
        return ((place_ref[3] ^ (i // 2)) * 2 + i % 2, 0)

    shape = jax.ShapeDtypeStruct((2 * rows, width), BF16)
    return pl.pallas_call(
        body,
        grid_spec=pltpu.PrefetchScalarGridSpec(
            num_scalar_prefetch=1,
            grid=(4,),
            in_specs=[
                pl.BlockSpec((step, width), lambda i, _: (jnp.minimum(i, 1), 0)),
                whole_spec((step, width)),
                whole_spec((step, width)),
            ]
            + weight_specs(pack, 1) + weight_specs(pack, 2),
            out_specs=[pl.BlockSpec((step, width), result)] * 2,
        ),
        out_shape=[shape, shape],
        compiler_params=pltpu.CompilerParams(vmem_limit_bytes=60 << 20),
        cost_estimate=MEDIUM,
        name="project_memory_kernel",
    )(place, own, *far, *pack, *pack)


def feed_forward(place, middle_one, attn, cotangent, gains, pack, wide, half):
    rows, width = cotangent.shape
    batch_count = wide.shape[0]
    slab = width // batch_count
    chunk = half // 2
    across = chunk // 128
    down_rows = half * 2 // batch_count
    down_across = width // 256
    down_units = down_across * down_rows

    def body(
        place_ref, middle_ref, attn_ref, cot_ref, gains_ref, co_one, co_two, co_three, co_four,
        gate_ref, up_ref, down_ref, out_ref, grad_middle_ref, grad_attn_ref, gain_ref, wide_grad,
        middle_two, normed, normed_t, grad_normed, result,
    ):
        step = pl.program_id(0)
        co_refs = (co_one, co_two, co_three, co_four)

        @pl.when(step == 0)
        def start():
            middle = middle_ref[...] + mm(attn_ref[...], matrix_of(place_ref, co_refs))
            middle_two[...] = middle
            rounded = (middle * inverse_rms(middle) * gains_ref[2:3, :]).astype(BF16)
            normed[...] = rounded
            normed_t[...] = rounded.T
            grad_normed[...] = jnp.zeros_like(grad_normed)
            result[...] = middle

        def wide_weight(ref):
            blocks = [
                ref[:, 0, index * slab : (index + 1) * slab, :].reshape(width, 128)
                for index in range(across)
            ]
            return jnp.concatenate(blocks, axis=1)

        cot = cot_ref[...]
        gate_weight, up_weight = wide_weight(gate_ref), wide_weight(up_ref)
        down_weight = jnp.concatenate(
            [
                down_ref[:, x, index * down_rows : (index + 1) * down_rows, :].reshape(chunk, 128)
                for x in range(2)
                for index in range(down_across)
            ],
            axis=1,
        )
        gate = mm(normed[...], gate_weight)
        up = mm(normed[...], up_weight)
        square = gate * gate
        bend = jnp.tanh(GELU_SCALE * (gate + GELU_CUBE * (gate * square)))
        half_one = 0.5 * (1.0 + bend)
        gelu = gate * half_one
        slope = half_one + 0.5 * gate * (1.0 - bend * bend) * (
            GELU_SCALE * (1.0 + 3.0 * GELU_CUBE * square)
        )
        act = (gelu * up).astype(BF16)
        result[...] += mm(act, down_weight)
        grad_act = mm_t(cot, down_weight)
        grad_gate = (grad_act * up * slope).astype(BF16)
        grad_up = (grad_act * gelu).astype(BF16)
        grad_normed[...] += mm_t(grad_gate, gate_weight) + mm_t(grad_up, up_weight)
        down_grad = t_mm(act, cot).astype(BF16)
        gate_rows = 2 * across * slab
        for block in range(chunk // down_rows):
            for x in range(2):
                for index in range(down_across):
                    span = slice((x * down_across + index) * 128, (x * down_across + index + 1) * 128)
                    start_row = 2 * gate_rows + index * down_rows
                    wide_grad[step * (chunk // down_rows) + block, x, start_row : start_row + down_rows, :] = (
                        down_grad[block * down_rows : (block + 1) * down_rows, span]
                    )
        for which, grad in enumerate((grad_gate, grad_up)):
            whole = mm(normed_t[...], grad).astype(BF16).reshape(batch_count, slab, chunk)
            for index in range(across):
                start_row = pl.multiple_of(
                    which * gate_rows + (step % 2) * across * slab + index * slab, slab
                )
                wide_grad[:, step // 2, pl.ds(start_row, slab), :] = whole[
                    :, :, index * 128 : (index + 1) * 128
                ]

        @pl.when(step == pl.num_programs(0) - 1)
        def finish():
            out_ref[...] = result[...].astype(BF16)
            pulled, gain_grad = norm_backward(middle_two[...], gains_ref[2:3, :], grad_normed[...])
            gain_ref[...] = gain_grad
            grad_middle = cot_ref[...].astype(F32) + pulled
            grad_middle_ref[...] = grad_middle
            branch = grad_middle.astype(BF16)
            grad_attn_ref[...] = mm_t(branch, matrix_of(place_ref, co_refs)).astype(BF16)

    row_shape = (rows, width)
    wide_spec = lambda which: pl.BlockSpec(
        (batch_count, 1, across * slab, 128), lambda i: (0, i // 2, 2 * which + i % 2, 0)
    )
    down_spec = pl.BlockSpec(
        (chunk // down_rows, 2, down_units, 128), lambda i: (i, 0, 4 * across * slab // down_units, 0)
    )
    return kernel_call(
        body, "feed_forward_kernel", (4,),
        [smem(), *[whole_spec(row_shape)] * 3, whole_spec(gains.shape)] + weight_specs(pack, 4) + [wide_spec(0), wide_spec(1), down_spec],
        [whole_spec(row_shape)] * 3 + [whole_spec((1, width)), whole_spec(wide.shape)],
        [
            jax.ShapeDtypeStruct(row_shape, BF16),
            jax.ShapeDtypeStruct(row_shape, F32),
            jax.ShapeDtypeStruct(row_shape, BF16),
            jax.ShapeDtypeStruct((1, width), F32),
            jax.ShapeDtypeStruct(wide.shape, BF16),
        ],
        (place, middle_one, attn, cotangent, gains, *pack, wide, wide, wide),
        scratch=[
            pltpu.VMEM(row_shape, F32), pltpu.VMEM(row_shape, BF16), pltpu.VMEM((width, rows), BF16),
            pltpu.VMEM(row_shape, F32), pltpu.VMEM(row_shape, F32),
        ],
    )


def after_cross(
    place, grad_query, middle_one, grad_middle_two, normed_cross, attn_self, attn_cross, gains, pack, after
):
    rows, width = middle_one.shape
    z_count = pack[0].shape[2] * 2
    slab = pack[0].shape[4]
    one, two = len(grad_query), len(attn_self)

    def body(place_ref, middle_ref, grad_ref, normed_ref, cross_ref, gains_ref, *refs):
        grad_query = join(refs[:one])
        attended = join(refs[one : one + two])
        so_refs, q_refs = refs[one + two : one + two + 4], refs[one + two + 4 : one + two + 8]
        grad_middle_ref, grad_attn_ref, gain_ref, keep_ref, send_ref = refs[one + two + 8 :]
        grads = mm_t(grad_query, matrix_of(place_ref, q_refs))
        pulled, gain_grad = norm_backward(middle_ref[...], gains_ref[1:2, :], grads)
        gain_ref[...] = gain_grad
        grad_middle = grad_ref[...] + pulled
        grad_middle_ref[...] = grad_middle
        branch = grad_middle.astype(BF16)
        grad_attn_ref[...] = mm_t(branch, matrix_of(place_ref, so_refs)).astype(BF16)
        branch_two = grad_ref[...].astype(BF16)
        for index, (left, right) in enumerate(
            ((normed_ref[...], grad_query), (attended, branch), (cross_ref[...], branch_two))
        ):
            targets = [(keep_ref, send_ref, (3 * index + part) * slab) for part in range(3)]
            store_square(place_ref, targets, t_mm(left, right), z_count)

    pieces = piece_shape(z_count, 9 * slab)
    row_shape = (rows, width)
    return kernel_call(
        body, "after_cross_kernel", (1,),
        [smem()] + [whole_spec(row_shape)] * 4 + [whole_spec(gains.shape)]
        + specs_of(grad_query) + specs_of(attn_self)
        + weight_specs(pack, 3) + weight_specs(pack, 0),
        [whole_spec(row_shape), whole_spec(row_shape), whole_spec((1, width))]
        + [whole_spec(pieces.shape)] * 2,
        [
            jax.ShapeDtypeStruct(row_shape, F32),
            jax.ShapeDtypeStruct(row_shape, BF16),
            jax.ShapeDtypeStruct((1, width), F32),
            pieces,
            pieces,
        ],
        (
            place, middle_one, grad_middle_two, normed_cross, attn_cross, gains,
            *grad_query, *attn_self, *pack, *pack,
        ),
        after=after,
    )


def memory_backward(place, grad_key, grad_value, own, far, pack):
    rows, width = own.shape
    step = rows // 2
    z_count = pack[0].shape[2] * 2
    slab = pack[0].shape[4]

    def body(
        place_ref, dk_ref, dv_ref, own_ref, far_a, far_b, *refs,
    ):
        k_refs, v_refs = refs[:4], refs[4:8]
        grad_own_ref, grad_far_ref, keep_ref, send_ref, key_total, value_total = refs[8:]
        i = pl.program_id(0)
        source = three_way(i ^ 2, own_ref, far_a, far_b)
        source_t = source.T

        @pl.when(i == 0)
        def clear():
            key_total[...] = jnp.zeros_like(key_total)
            value_total[...] = jnp.zeros_like(value_total)

        grad_key, grad_value = dk_ref[...], dv_ref[...]
        key_total[...] += mm(source_t, grad_key)
        value_total[...] += mm(source_t, grad_value)
        grads = mm_t(grad_key, matrix_of(place_ref, k_refs)) + mm_t(
            grad_value, matrix_of(place_ref, v_refs)
        )

        @pl.when(i < 2)
        def here():
            grad_far_ref[...] = grads.astype(BF16)

        @pl.when(i >= 2)
        def there():
            grad_own_ref[...] = grads

        @pl.when(i == 3)
        def finish():
            for index, total in enumerate((key_total, value_total)):
                targets = [(keep_ref, send_ref, (3 * index + part) * slab) for part in range(3)]
                store_square(place_ref, targets, total[...], z_count)

    def block(i, place_ref):
        return ((place_ref[3] ^ (1 - i // 2)) * 2 + i % 2, 0)

    pieces = piece_shape(z_count, 6 * slab)
    return pl.pallas_call(
        body,
        grid_spec=pltpu.PrefetchScalarGridSpec(
            num_scalar_prefetch=1,
            grid=(4,),
            in_specs=[
                *[pl.BlockSpec((step, width), block)] * 2,
                pl.BlockSpec((step, width), lambda i, _: (jnp.maximum(i - 2, 0), 0)),
                whole_spec((step, width)),
                whole_spec((step, width)),
            ]
            + weight_specs(pack, 1) + weight_specs(pack, 2),
            out_specs=[
                pl.BlockSpec((step, width), lambda i, _: (jnp.maximum(i - 2, 0), 0)),
                pl.BlockSpec((step, width), lambda i, _: (jnp.minimum(i, 1), 0)),
                whole_spec(pieces.shape),
                whole_spec(pieces.shape),
            ],
            scratch_shapes=[pltpu.VMEM((width, width), F32), pltpu.VMEM((width, width), F32)],
        ),
        out_shape=[
            jax.ShapeDtypeStruct((rows, width), F32),
            jax.ShapeDtypeStruct((rows, width), BF16),
            pieces,
            pieces,
        ],
        compiler_params=pltpu.CompilerParams(vmem_limit_bytes=60 << 20),
        cost_estimate=MEDIUM,
        name="memory_backward_kernel",
    )(place, grad_key, grad_value, own, *far, *pack, *pack)


def self_weight_grads(place, grad_query, grad_key, grad_value, normed, z_count, after):
    rows, half = grad_query[0].shape
    width = 2 * half
    slab = width // (4 * z_count)

    def body(place_ref, dq_a, dq_b, dk_a, dk_b, dv_a, dv_b, normed_ref, keep_a, send_a, keep_b, send_b):
        here = pl.ds(pl.multiple_of(place_ref[3] * rows, rows), rows)
        normed_t = normed_ref[...].T
        grads = (
            t_mm(normed_ref[here, :], join((dq_a, dq_b))),
            mm(normed_t, join((dk_a, dk_b))),
            mm(normed_t, join((dv_a, dv_b))),
        )
        for index, grad in enumerate(grads):
            targets = []
            for unit in range(3 * index, 3 * index + 3):
                first = unit < 5
                targets.append(
                    (keep_a if first else keep_b, send_a if first else send_b, (unit if first else unit - 5) * slab)
                )
            store_square(place_ref, targets, grad, z_count)

    shapes = [piece_shape(z_count, count * slab) for count in (5, 5, 4, 4)]
    return kernel_call(
        body, "self_weight_grads_kernel", (1,),
        [smem()] + [whole_spec((rows, half))] * 2 + [whole_spec((2 * rows, half))] * 4
        + [whole_spec((2 * rows, width))],
        [whole_spec(shape.shape) for shape in shapes],
        shapes,
        (place, *grad_query, *grad_key, *grad_value, normed),
        after=after,
    )


def self_row_grads(place, own, far, gains, grad_query, grad_key, grad_value, pack, after):
    rows, half = grad_query[0].shape
    width = 2 * half

    def body(place_ref, own_rows, far_rows, dq_a, dq_b, dk_a, dk_b, dv_a, dv_b, *refs):
        weights, (own_ref, far_ref, gain_ref) = refs[:4], refs[4:]
        key_weight = matrix_of(place_ref, weights, 1)
        value_weight = matrix_of(place_ref, weights, 2)
        here = pl.ds(pl.multiple_of(place_ref[3] * rows, rows), rows)
        there = pl.ds(pl.multiple_of((1 - place_ref[3]) * rows, rows), rows)
        split = lambda pair, span: jnp.concatenate([pair[0][span, :], pair[1][span, :]], axis=1)
        keys, values = (dk_a, dk_b), (dv_a, dv_b)

        def gain_of(rows_ref, grads):
            values = rows_ref[...].astype(F32)
            return jnp.sum(grads * (values * inverse_rms(values)), axis=0, keepdims=True)

        far_grads = mm_t(split(keys, there), key_weight) + mm_t(split(values, there), value_weight)
        far_ref[...] = far_grads.astype(BF16)
        own_grads = (
            mm_t(split(keys, here), key_weight)
            + mm_t(split(values, here), value_weight)
            + mm_t(join((dq_a, dq_b)), matrix_of(place_ref, weights, 0))
        )
        own_ref[...] = own_grads
        gain_ref[...] = gain_of(own_rows, own_grads) + gain_of(far_rows, far_grads)

    row_shape = (rows, width)
    return kernel_call(
        body, "self_row_grads_kernel", (1,),
        [smem()] + [whole_spec(row_shape)] * 2
        + specs_of(grad_query) + specs_of(grad_key) + specs_of(grad_value) + specs_of(pack),
        [whole_spec(row_shape)] * 2 + [whole_spec((1, width))],
        [
            jax.ShapeDtypeStruct(row_shape, F32),
            jax.ShapeDtypeStruct(row_shape, BF16),
            jax.ShapeDtypeStruct((1, width), F32),
        ],
        (place, own, far, *grad_query, *grad_key, *grad_value, *pack),
        after=after,
    )


def finish_rows(own, grads, far_grads, grad_middle, gains, after):
    def body(own_ref, grads_ref, far_ref, middle_ref, gains_ref, out_ref):
        total = grads_ref[...] + far_ref[...].astype(F32)
        pulled, _ = norm_backward(own_ref[...].astype(F32), gains_ref[0:1, :], total)
        out_ref[...] = middle_ref[...] + pulled

    shape = jax.ShapeDtypeStruct(own.shape, F32)
    return simple_call(body, "finish_rows_kernel", [shape], [own, grads, far_grads, grad_middle, gains], after)[0]


def shards_plain(
    hidden,
    memory,
    decoder_lengths,
    memory_lengths,
    distance_buckets,
    norm_gains,
    position_bias,
    self_weights,
    self_output,
    cross_weights,
    cross_output,
    expand_weights,
    contract_weight,
    cotangent,
):
    mem_count = lax.axis_size("mem")
    mem_index = lax.axis_index("mem")
    row_count, model_width = hidden.shape[1:]
    head_count = position_bias.shape[1]
    head_width = model_width // head_count
    bucket_count = position_bias.shape[0]
    key_count = row_count * mem_count
    first_row = mem_index * row_count
    first = jnp.reshape(first_row, (1,)).astype(jnp.int32)
    rows = min(256, row_count)

    self_full = gather_plain(self_weights)
    tokens_all = all_rows(hidden[0])
    memory_all = all_rows(memory[0])
    square_full = gather_plain(
        jnp.concatenate([cross_weights, self_output[None], cross_output[None]])
    )
    cross_full, self_out_full, cross_out_full = square_full[:3], square_full[3], square_full[4]
    expand_full = gather_plain(expand_weights)
    contract_full = gather_plain(contract_weight[None])[0]

    buckets = jnp.arange(bucket_count, dtype=jnp.int32)
    one_hot = (distance_buckets[:, None] == buckets[None, :]).astype(F32)
    distance_table = jnp.einsum("db,bh->hd", one_hot, position_bias, precision=EXACT)
    distance_table = jnp.pad(distance_table, ((0, 0), (rows, 0)))
    distance_table = distance_table.reshape(head_count // 2, 2, key_count + rows)

    tokens = hidden[0].astype(F32)
    normed_self, pull_self = jax.vjp(rms_norm, tokens, norm_gains[0])
    input_self = normed_self.astype(BF16)
    input_all = rms_norm(tokens_all.astype(F32), norm_gains[0]).astype(BF16)
    query_self = mm(input_self, self_full[0]).astype(BF16)
    key_self = mm(input_all, self_full[1]).astype(BF16)
    value_self = mm(input_all, self_full[2]).astype(BF16)
    attn_self, self_totals = attention_forward(
        first, decoder_lengths, decoder_lengths, query_self, key_self, value_self,
        distance_table, head_width, rows, (0, head_count // 2),
    )
    middle_one = tokens + mm(attn_self, self_out_full)
    normed_cross, pull_cross = jax.vjp(rms_norm, middle_one, norm_gains[1])
    input_cross = normed_cross.astype(BF16)
    query_cross = mm(input_cross, cross_full[0]).astype(BF16)
    key_memory = mm(memory_all, cross_full[1]).astype(BF16)
    value_memory = mm(memory_all, cross_full[2]).astype(BF16)
    attn_cross, cross_totals = attention_forward(
        first, decoder_lengths, memory_lengths, query_cross, key_memory, value_memory,
        None, head_width, 512, (0, head_count // 2),
    )
    middle_two = middle_one + mm(attn_cross, cross_out_full)
    normed_feed, pull_feed = jax.vjp(rms_norm, middle_two, norm_gains[2])
    input_feed = normed_feed.astype(BF16)
    gate_part = mm(input_feed, expand_full[0])
    up_part = mm(input_feed, expand_full[1])
    activated, pull_activate = jax.vjp(activate, gate_part, up_part)
    hidden_act = activated.astype(BF16)
    result_rows = middle_two + mm(hidden_act, contract_full)
    grad_branch_three = cotangent[0]
    grad_out = grad_branch_three.astype(F32)
    grad_gate, grad_up = pull_activate(mm_t(grad_branch_three, contract_full))
    grad_gate, grad_up = grad_gate.astype(BF16), grad_up.astype(BF16)
    contract_grad = scatter_plain(t_mm(hidden_act, grad_branch_three).astype(BF16)[None])[0]
    expand_grad = scatter_plain(
        jnp.stack([t_mm(input_feed, grad_gate), t_mm(input_feed, grad_up)]).astype(BF16)
    )
    grad_norm_two, gain_grad_three = pull_feed(
        mm_t(grad_gate, expand_full[0]) + mm_t(grad_up, expand_full[1])
    )
    grad_middle_two = grad_out + grad_norm_two
    grad_branch_two = grad_middle_two.astype(BF16)
    grad_cross_out = t_mm(attn_cross, grad_branch_two)
    grad_attn_cross = mm_t(grad_branch_two, cross_out_full).astype(BF16)
    grad_query_cross, grad_key_memory, grad_value_memory = attention_backward(
        first, decoder_lengths, memory_lengths, query_cross, key_memory, value_memory,
        grad_attn_cross, cross_totals, None, head_width, 512, (0, head_count // 2),
    )
    cross_grads = scatter_plain(
        jnp.stack(
            [
                t_mm(input_cross, grad_query_cross),
                t_mm(memory_all, grad_key_memory),
                t_mm(memory_all, grad_value_memory),
                grad_cross_out,
            ]
        ).astype(BF16)
    )
    memory_gradient = own_rows(
        mm_t(grad_key_memory, cross_full[1]) + mm_t(grad_value_memory, cross_full[2])
    )
    grad_norm_one, gain_grad_two = pull_cross(mm_t(grad_query_cross, cross_full[0]))
    grad_middle_one = grad_middle_two + grad_norm_one
    grad_branch_one = grad_middle_one.astype(BF16)
    grad_self_out = t_mm(attn_self, grad_branch_one)
    grad_attn_self = mm_t(grad_branch_one, self_out_full).astype(BF16)
    grad_query_self, grad_key_self, grad_value_self, diagonals = attention_backward(
        first, decoder_lengths, decoder_lengths, query_self, key_self, value_self,
        grad_attn_self, self_totals, distance_table, head_width, rows, (0, head_count // 2),
    )
    diagonals = diagonals.reshape(head_count, key_count // rows, 2 * rows)
    by_distance = jnp.zeros((head_count, key_count + rows), F32)
    for delta in range(key_count // rows):
        here = slice(delta * rows, delta * rows + 2 * rows)
        by_distance = by_distance.at[:, here].add(diagonals[:, delta])
    bias_partial = jnp.einsum("db,hd->bh", one_hot, by_distance[:, rows:], precision=EXACT)
    self_grads = scatter_plain(
        jnp.stack(
            [
                t_mm(input_self, grad_query_self),
                t_mm(input_all, grad_key_self),
                t_mm(input_all, grad_value_self),
                grad_self_out,
            ]
        ).astype(BF16)
    )
    grad_input_self = own_rows(
        mm_t(grad_key_self, self_full[1]) + mm_t(grad_value_self, self_full[2])
    ) + mm_t(grad_query_self, self_full[0])
    grad_norm_zero, gain_grad_one = pull_self(grad_input_self)
    grad_tokens = grad_middle_one + grad_norm_zero
    gain_sums, bias_sums = lax.psum(
        (jnp.stack([gain_grad_one, gain_grad_two, gain_grad_three]), bias_partial), ("batch", "mem")
    )
    return (
        result_rows.astype(BF16)[None],
        grad_tokens[None],
        memory_gradient[None],
        gain_sums,
        bias_sums,
        self_grads[:3],
        self_grads[3],
        cross_grads[:3],
        cross_grads[3],
        expand_grad,
        contract_grad,
    )


def shards_hops(
    hidden,
    memory,
    decoder_lengths,
    memory_lengths,
    distance_buckets,
    norm_gains,
    position_bias,
    self_weights,
    self_output,
    cross_weights,
    cross_output,
    expand_weights,
    contract_weight,
    cotangent,
):
    batch_count, mem_count = lax.axis_size("batch"), lax.axis_size("mem")
    row_count, model_width = hidden.shape[1:]
    bucket_count, head_count = position_bias.shape
    head_width = model_width // head_count
    key_count = row_count * mem_count
    rows = min(256, row_count)
    spot = jnp.stack(grid_place()).astype(jnp.int32)
    first = jnp.reshape(lax.axis_index("mem") * row_count, (1,)).astype(jnp.int32)
    own, own_memory = hidden[0], memory[0]

    slab, columns = self_weights.shape[1:]
    z_count = batch_count // 4

    pairs = head_count // 2
    pairs = head_count // 2
    far = send_mem(own)
    low, high = place_line(spot, line_of(self_weights))
    across = expand_weights.shape[2] // 128
    wide = jnp.concatenate(
        [
            expand_weights.reshape(2, slab, across, 128).transpose(0, 2, 1, 3).reshape(-1, 128),
            contract_weight.reshape(-1, columns // 128, 128).transpose(1, 0, 2).reshape(-1, 128),
        ]
    )
    second = jnp.concatenate([cross_weights, self_output[None], cross_output[None]])
    (second,) = hold((second,), (low, high))
    line = line_of(second)
    low, high = gather_first(spot, low, high, (far,))
    next_low, next_high = place_line(spot, line, (low, high))
    low, high = gather_second(spot, low, high, (next_low, next_high))
    (memory_start,) = hold((own_memory[: own_memory.shape[0] // 2],), (low, high))
    far_memory_a = send_mem(memory_start)
    self_pack = gather_cores(low, high)
    low, high = next_low, next_high

    buckets = jnp.arange(bucket_count, dtype=jnp.int32)
    one_hot = (distance_buckets[:, None] == buckets[None, :]).astype(F32)
    distance_table = jnp.einsum("db,bh->hd", one_hot, position_bias, precision=EXACT)
    distance_table = jnp.pad(distance_table, ((0, 0), (rows, 0)))
    distance_table = distance_table.reshape(pairs, 2, key_count + rows)
    padded = jnp.pad(one_hot, ((rows, 0), (0, 0)))
    bucket_windows = jnp.concatenate(
        [padded[delta * rows : (delta + 2) * rows] for delta in range(key_count // rows)]
    )

    query_self, key_self, value_self, normed_self = project_self(
        spot, own, far, norm_gains, self_pack, (low, high)
    )

    def self_forward(span, after, cost):
        return attention_forward(
            first, decoder_lengths, decoder_lengths, query_self, key_self, value_self,
            distance_table, head_width, rows, span, after, cost,
        )

    low, high = gather_first(spot, low, high, (query_self, far_memory_a))
    (memory_start,) = hold((own_memory[own_memory.shape[0] // 2 :],), (low, high))
    far_memory = (far_memory_a, send_mem(memory_start))
    one = self_forward((0, 2 * pairs // 3), (low, high), LONG)
    low, high = gather_second(spot, low, high, (one[0],))
    (wide,) = hold((wide,), (low, high))
    square_pack = gather_cores(low, high)
    wide = lax.all_gather(wide, ("batch", "mem"), axis=0, tiled=False)
    wide = wide.reshape(batch_count, mem_count, *wide.shape[1:])
    two = self_forward((2 * pairs // 3, pairs // 3), (low, high), BRIEF)
    attn_self, self_totals = zip(one, two)
    self_totals = jnp.concatenate(self_totals, axis=0)
    middle_one, normed_cross, query_cross = after_self(spot, own, attn_self, norm_gains, square_pack)
    key_memory, value_memory = project_memory(spot, own_memory, far_memory, square_pack)
    attn_cross, cross_totals = attention_forward(
        first, decoder_lengths, memory_lengths, query_cross, key_memory, value_memory,
        None, head_width, 512, (0, pairs),
    )
    (
        result, grad_middle_two, grad_attn_cross, gain_three, wide_grad,
    ) = feed_forward(
        spot, middle_one, attn_cross, cotangent[0], norm_gains, square_pack, wide, expand_weights.shape[2]
    )
    halves = ((0, pairs // 2), (pairs // 2, pairs // 2))
    wide_grad = lax.psum_scatter(
        wide_grad.reshape(batch_count * mem_count, *wide_grad.shape[2:]),
        ("batch", "mem"), scatter_dimension=0, tiled=True,
    )[0]
    grad_query_cross, grad_key_memory, grad_value_memory = attention_backward(
        first, decoder_lengths, memory_lengths, query_cross, key_memory, value_memory,
        grad_attn_cross, cross_totals, None, head_width, 512, (0, pairs),
    )
    memory_own, memory_far, kv_keep, kv_send = memory_backward(
        spot, grad_key_memory, grad_value_memory, own_memory, far_memory, square_pack
    )
    grad_middle_one, grad_attn_self, gain_two, qo_keep, qo_send = after_cross(
        spot, (grad_query_cross,), middle_one, grad_middle_two, normed_cross, attn_self, attn_cross,
        norm_gains, square_pack, (memory_far,),
    )

    def self_backward(half, after):
        return attention_backward(
            first, decoder_lengths, decoder_lengths, query_self, key_self, value_self,
            grad_attn_self, self_totals, distance_table, head_width, rows, halves[half], after,
        )

    one = self_backward(0, (qo_keep,))
    (kv_keep, kv_send), (qo_keep, qo_send) = scatter_step(
        ((kv_keep, send_batch(kv_send, 1)), (qo_keep, send_batch(qo_send, 1))), (one[0],), (2, 1)
    )
    memory_far = send_mem(memory_far)
    two = self_backward(1, (kv_keep, one[0]))
    (kv_keep, kv_send), (qo_keep, qo_send) = scatter_step(
        ((kv_keep, send_mem(kv_send)), (qo_keep, send_batch(qo_send, 2))), (two[0],), (1, 1)
    )
    grad_query_self, grad_key_self, grad_value_self, diagonals = zip(one, two)
    rows_own, rows_far, gain_one = self_row_grads(
        spot, own, far, norm_gains, grad_query_self, grad_key_self, grad_value_self, self_pack,
        (kv_keep,),
    )
    line_kv, line_qo = scatter_to_line(
        ((kv_keep, send_batch(kv_send, 2)), (qo_keep, send_mem(qo_send))), (rows_far,)
    )
    diagonals = jnp.concatenate(diagonals, axis=0).reshape(head_count, -1)
    bias_partial = jnp.einsum("db,hd->bh", bucket_windows, diagonals, precision=EXACT)
    gains = jnp.concatenate([gain_one, gain_two, gain_three], axis=0)
    sums = jnp.concatenate([gains.reshape(-1), bias_partial.reshape(-1)]).reshape(-1, 128)
    keep_a, send_a, keep_b, send_b = self_weight_grads(
        spot, grad_query_self, grad_key_self, grad_value_self, normed_self, z_count, (line_kv[0],)
    )
    sums = sum_small(sums, (1, 2, 3), (keep_a,))
    memory_gradient = add_rows(memory_own, memory_far, (keep_a, sums))
    (keep_a, send_a), (keep_b, send_b) = scatter_step(
        ((keep_a, send_batch(send_a, 1)), (keep_b, send_batch(send_b, 1))), (memory_gradient,), (2, 1)
    )
    hidden_gradient = finish_rows(
        own, rows_own, send_mem(rows_far), grad_middle_one, norm_gains, (keep_a,)
    )
    sums = sum_small(sums, (4, 8, 12), (keep_a,))
    units = [(0, 0, block) for block in range(3)] + [(0, 1, block) for block in range(3)]
    units += [(1, matrix, block) for matrix in (2, 3, 4) for block in range(3)]
    cross_grad, self_out_grad, cross_out_grad = scatter_end(
        (send_line(line_kv), send_line(line_qo)),
        (cross_weights.shape, self_output.shape, cross_output.shape),
        square_moves(units, slab, columns, ((0, 1), (0, 2), (0, 0), (1, None), (2, None))),
        (hidden_gradient,),
    )
    (keep_a, send_a), (keep_b, send_b) = scatter_step(
        ((keep_a, send_mem(send_a)), (keep_b, send_batch(send_b, 2))), (cross_grad,), (1, 1)
    )
    sums = sum_small(sums, (16,), (keep_a,)).reshape(-1)
    line_a, line_b = scatter_to_line(
        ((keep_a, send_batch(send_a, 2)), (keep_b, send_mem(send_b))), ()
    )
    units = [(0 if unit < 5 else 1, unit // 3, unit % 3) for unit in range(9)]
    (self_grad,) = scatter_end(
        (send_line(line_a), send_line(line_b)), (self_weights.shape,),
        square_moves(units, slab, columns, ((0, 0), (0, 1), (0, 2))), (),
    )
    gate_rows, down_rows = across * slab, contract_weight.shape[0]
    moves = []
    for which in range(2):
        for block in range(across):
            span = (which, slice(None), slice(block * 128, block * 128 + 128))
            moves.append((0, which * gate_rows + block * slab, slab, 0, span))
    for block in range(columns // 128):
        span = (slice(None), slice(block * 128, block * 128 + 128))
        moves.append((0, 2 * gate_rows + block * down_rows, down_rows, 1, span))
    expand_grad, contract_grad = scatter_end(
        ((wide_grad,),), (expand_weights.shape, contract_weight.shape), moves, (line_a[0],)
    )
    return (
        result[None],
        hidden_gradient[None],
        memory_gradient[None],
        sums[: gains.size].reshape(gains.shape),
        sums[gains.size :].reshape(bucket_count, head_count),
        self_grad,
        self_out_grad,
        cross_grad,
        cross_out_grad,
        expand_grad,
        contract_grad,
    )


def shards(*arrays):
    row_count, slab, columns = arrays[0].shape[1], arrays[7].shape[1], arrays[7].shape[2]
    allowed = row_count % 256 == 0 and slab % 16 == 0 and columns % 128 == 0
    if lax.axis_size("mem") == 2 and lax.axis_size("batch") == 16 and allowed:
        return shards_hops(*arrays)
    return shards_plain(*arrays)


def solution(mesh):
    placed = (
        P("batch", "mem", None),
        P("batch", "mem", None),
        P("batch", None),
        P("batch", None),
        P(),
        P(),
        P(),
        P(None, "batch", "mem"),
        P("batch", "mem"),
        P(None, "batch", "mem"),
        P("batch", "mem"),
        P(None, "batch", "mem"),
        P("batch", "mem"),
        P("batch", "mem", None),
    )
    return jax.shard_map(
        shards,
        mesh=mesh,
        in_specs=placed,
        out_specs=(
            P("batch", "mem", None),
            P("batch", "mem", None),
            P("batch", "mem", None),
            P(),
            P(),
            P(None, "batch", "mem"),
            P("batch", "mem"),
            P(None, "batch", "mem"),
            P("batch", "mem"),
            P(None, "batch", "mem"),
            P("batch", "mem"),
        ),
        check_vma=False,
    )
```

```python
import functools
import math

import jax
import jax.numpy as jnp
from jax import lax
from jax.experimental import pallas as pl
from jax.experimental.pallas import tpu as pltpu
from jax.sharding import PartitionSpec as P

EPSILON = 1e-06
NEGATIVE = -1e30
F32 = jnp.float32
BF16 = jnp.bfloat16
EXACT = lax.Precision.HIGHEST
GELU_SCALE = (2 / math.pi) ** 0.5
GELU_CUBE = 0.044715
LONG = pl.CostEstimate(flops=20_000_000_000, bytes_accessed=1_000, transcendentals=0)
MEDIUM = pl.CostEstimate(flops=6_000_000_000, bytes_accessed=1_000, transcendentals=0)
BRIEF = pl.CostEstimate(flops=2_000_000_000, bytes_accessed=1_000, transcendentals=0)
SHORT = pl.CostEstimate(flops=100_000, bytes_accessed=1_000, transcendentals=0)
NT = (((1,), (1,)), ((), ()))
NN = (((1,), (0,)), ((), ()))


def rms_norm(values, gain_row):
    return (
        values * lax.rsqrt(jnp.mean(values * values, axis=-1, keepdims=True) + EPSILON) * gain_row
    )


def activate(gate_part, up_part):
    return jax.nn.gelu(gate_part, approximate=True) * up_part


def dot(left, right, dims):
    return lax.dot_general(left, right, dims, preferred_element_type=F32)


def bounds_of(sizes_ref):
    edges = [jnp.int32(0)]
    for slot in range(sizes_ref.shape[1]):
        edges.append(edges[-1] + sizes_ref[0, slot])
    return edges


def pick(place, edges, values):
    chosen = jnp.zeros_like(place) + values[0]
    for slot in range(1, len(edges) - 1):
        chosen = jnp.where(place >= edges[slot], values[slot], chosen)
    return chosen


def stack_heads(block, width):
    lane = lax.broadcasted_iota(jnp.int32, block.shape, 1)
    zero = jnp.zeros_like(block)
    return jnp.concatenate(
        [jnp.where(lane < width, block, zero), jnp.where(lane < width, zero, block)], axis=0
    )


def transposed_blocks(source_ref, scratch, step):
    for index in range(scratch.shape[0]):
        scratch[index] = source_ref[index * step : (index + 1) * step, :].T


def limits(first, rows, q_edges, k_edges, causal):
    place = lax.broadcasted_iota(jnp.int32, (1, rows), 1) + first
    begin = pick(place, q_edges, k_edges[:-1])
    end = pick(place, q_edges, k_edges[1:])
    if causal:
        end = jnp.minimum(end, place + 1)
    return begin, end


def fold(block, combine):
    parts = [block[start : start + 8] for start in range(0, block.shape[0], 8)]
    while len(parts) > 1:
        joined = [combine(parts[i], parts[i + 1]) for i in range(0, len(parts) - 1, 2)]
        parts = joined + parts[2 * len(joined) :]
    return parts[0]


def fill_mask(mask, first, q_edges, k_edges, causal):
    blocks, key_count, rows = mask.shape
    for block in range(blocks):
        begin, end = limits(first + block * rows, rows, q_edges, k_edges, causal)
        place = lax.broadcasted_iota(jnp.int32, (key_count, rows), 0)
        mask[block] = jnp.where((place >= begin) & (place < end), 0.0, NEGATIVE)


def fill_tiles(table_ref, tiles):
    count, tile = tiles.shape[:2]
    for head in range(2):
        wide = jnp.broadcast_to(table_ref[0, head : head + 1, :], (8, (count + 1) * tile))
        wide = pltpu.roll(wide, 0, 1, stride=1, stride_axis=0)
        for start in range(0, tile, 8):
            moved = pltpu.roll(wide, start, 1) if start else wide
            for index in range(count):
                tiles[index, start : start + 8, head * tile : (head + 1) * tile] = moved[
                    :, (index + 1) * tile : (index + 2) * tile
                ]


def sum_diagonals(tiles, out_ref):
    count, tile = tiles.shape[:2]
    for head in range(2):
        parts = jnp.zeros((8, (count + 1) * tile), F32)
        for start in range(0, tile, 8):
            line = [jnp.zeros((8, tile), F32)]
            for index in range(count):
                line.append(tiles[index, start : start + 8, head * tile : (head + 1) * tile])
            line = jnp.concatenate(line, axis=1)
            parts = parts + (pltpu.roll(line, line.shape[1] - start, 1) if start else line)
        line = parts[0:1]
        for row in range(1, 8):
            line = line + pltpu.roll(parts[row : row + 1], parts.shape[1] - row, 1)
        out_ref[0, head : head + 1, :] = line


def tile_of(u, t, key_tiles, row_tiles):
    return key_tiles - row_tiles + t - u


def bias_of(tiles, key_tiles, row_tiles):
    tile = tiles.shape[1]
    lines = []
    for u in range(key_tiles):
        line = [
            tiles[max(tile_of(u, t, key_tiles, row_tiles), 0), :, head * tile : (head + 1) * tile]
            for head in range(2)
            for t in range(row_tiles)
        ]
        lines.append(jnp.concatenate(line, axis=1))
    return jnp.concatenate(lines, axis=0)


def score_block(k_ref, queries, mask, tiles, block, index, step):
    here = pl.ds(pl.multiple_of(index * step, step), step)
    scores = dot(k_ref[here, :], queries, NT)
    if tiles is not None:
        tile = tiles.shape[1]
        scores = scores + bias_of(tiles, step // tile, queries.shape[0] // 2 // tile)
    hidden = mask[block, here, :]
    return scores + jnp.concatenate([hidden, hidden], axis=1)


def key_range(first, rows, q_edges, k_edges, step):
    high = pick(first + rows - 1, q_edges, k_edges[1:])
    return pick(first, q_edges, k_edges[:-1]) // step, (high + step - 1) // step


def forward_kernel(causal, step, width, first_ref, q_sizes, k_sizes, q_ref, k_ref, v_ref, *rest):
    if causal:
        table_ref, out_ref, total_ref, tiles_ref, value_t, scores, mask = rest
        tiles = tiles_ref.at[0]
    else:
        out_ref, total_ref, value_t, scores, mask = rest
        tiles = None
    blocks, rows = total_ref.shape[1], total_ref.shape[3] // 2
    q_edges = bounds_of(q_sizes)
    k_edges = bounds_of(k_sizes)

    @pl.when(pl.program_id(0) == 0)
    def once():
        fill_mask(mask, first_ref[0], q_edges, k_edges, causal)

    transposed_blocks(v_ref, value_t, step)
    if causal:
        fill_tiles(table_ref, tiles)
    for block in range(blocks):
        first = first_ref[0] + block * rows
        low, high = (0, 1) if causal else key_range(first, rows, q_edges, k_edges, step)
        queries = stack_heads(q_ref[block * rows : (block + 1) * rows, :], width)

        def measure(index, top):
            block_scores = score_block(k_ref, queries, mask, tiles, block, index, step)
            scores[index] = block_scores
            return jnp.maximum(top, fold(block_scores, jnp.maximum))

        top = lax.fori_loop(low, high, measure, jnp.full((8, 2 * rows), NEGATIVE, F32))
        top = jnp.max(top, axis=0, keepdims=True)

        def gather(index, carry):
            total, out_a, out_b = carry
            weights = jnp.exp(scores[index] - top)
            total = total + fold(weights, jnp.add)
            rounded = weights.astype(BF16)
            out_a = out_a + dot(value_t[index], rounded[:, :rows], NN)
            out_b = out_b + dot(value_t[index], rounded[:, rows:], NN)
            return total, out_a, out_b

        zero = jnp.zeros((2 * width, rows), F32)
        total, out_a, out_b = lax.fori_loop(
            low, high, gather, (jnp.zeros((8, 2 * rows), F32), zero, zero)
        )
        total = jnp.sum(total, axis=0, keepdims=True)
        joined = jnp.concatenate(
            [out_a[:width] / total[:, :rows], out_b[width:] / total[:, rows:]], axis=0
        )
        out_ref[block * rows : (block + 1) * rows, :] = joined.T.astype(BF16)
        total_ref[0, block] = top + jnp.log(total)


def backward_kernel(
    causal, step, width, first_ref, q_sizes, k_sizes, q_ref, k_ref, v_ref, g_ref, total_ref, *rest
):
    if causal:
        tiles_ref, dq_ref, dk_ref, dv_ref, diag_ref, key_t, probs, grads, dk, dv, mask, sums = rest
        tiles = tiles_ref.at[0]
    else:
        dq_ref, dk_ref, dv_ref, key_t, probs, grads, dk, dv, mask = rest
        tiles = None
    blocks, rows = total_ref.shape[1], total_ref.shape[3] // 2
    q_edges = bounds_of(q_sizes)
    k_edges = bounds_of(k_sizes)

    @pl.when(pl.program_id(0) == 0)
    def once():
        fill_mask(mask, first_ref[0], q_edges, k_edges, causal)

    transposed_blocks(k_ref, key_t, step)
    dk[...] = jnp.zeros_like(dk)
    dv[...] = jnp.zeros_like(dv)
    for block in range(blocks):
        first = first_ref[0] + block * rows
        low, high = (0, 1) if causal else key_range(first, rows, q_edges, k_edges, step)
        queries = stack_heads(q_ref[block * rows : (block + 1) * rows, :], width)
        targets = stack_heads(g_ref[block * rows : (block + 1) * rows, :], width)
        total = total_ref[0, block]

        def measure(index, inner):
            here = pl.ds(pl.multiple_of(index * step, step), step)
            block_scores = score_block(k_ref, queries, mask, tiles, block, index, step)
            weights = jnp.exp(block_scores - total)
            pulled = dot(v_ref[here, :], targets, NT)
            probs[index] = weights
            grads[index] = pulled
            dv[here, :] += dot(weights.astype(BF16), targets, NN)
            return inner + fold(weights * pulled, jnp.add)

        inner = lax.fori_loop(low, high, measure, jnp.zeros((8, 2 * rows), F32))
        inner = jnp.sum(inner, axis=0, keepdims=True)

        def gather(index, carry):
            out_a, out_b = carry
            here = pl.ds(pl.multiple_of(index * step, step), step)
            rounded = (probs[index] * (grads[index] - inner)).astype(BF16)
            dk[here, :] += dot(rounded, queries, NN)
            if causal:
                tile = tiles.shape[1]
                spots = [(u, t) for u in range(step // tile) for t in range(rows // tile)]
                for which in range(sums.shape[0]):
                    parts = [
                        jnp.concatenate(
                            [
                                rounded[u * tile : (u + 1) * tile, start + t * tile : start + (t + 1) * tile]
                                for start in (0, rows)
                            ],
                            axis=1,
                        ).astype(F32)
                        for u, t in spots
                        if tile_of(u, t, step // tile, rows // tile) == which
                    ]
                    sums[which] = functools.reduce(jnp.add, parts)
            out_a = out_a + dot(key_t[index], rounded[:, :rows], NN)
            out_b = out_b + dot(key_t[index], rounded[:, rows:], NN)
            return out_a, out_b

        zero = jnp.zeros((2 * width, rows), F32)
        out_a, out_b = lax.fori_loop(low, high, gather, (zero, zero))
        joined = jnp.concatenate([out_a[:width], out_b[width:]], axis=0)
        dq_ref[block * rows : (block + 1) * rows, :] = joined.T.astype(BF16)
    dk_ref[...] = dk[...].astype(BF16)
    dv_ref[...] = dv[...].astype(BF16)
    if causal:
        sum_diagonals(sums, diag_ref)


def unread():
    return pl.BlockSpec(memory_space=pl.ANY)


def ignoring(body, first, count):
    return lambda *refs: body(*refs[:first], *refs[first + count :])


def hold(values, after):
    count = len(values)
    return pl.pallas_call(
        lambda *refs: None,
        in_specs=[unread()] * (count + len(after)),
        out_specs=[unread()] * count,
        out_shape=[jax.ShapeDtypeStruct(value.shape, value.dtype) for value in values],
        input_output_aliases={index: index for index in range(count)},
        cost_estimate=SHORT,
        name="hold",
    )(*values, *after)


def smem():
    return pl.BlockSpec(memory_space=pltpu.SMEM)


def attention_forward(
    first, q_sizes, k_sizes, queries, keys, values, table, width, step, span, after=(), cost=LONG
):
    causal = table is not None
    count, model = queries.shape
    key_count = keys.shape[0]
    rows, tile = min(512, count), min(256, count)
    step = key_count if causal else min(step, key_count)
    pair_first, pairs = span
    blocks = count // rows
    column = lambda size: pl.BlockSpec((size, 2 * width), lambda pair: (0, pair + pair_first))
    result = lambda size: pl.BlockSpec((size, 2 * width), lambda pair: (0, pair))
    scratch = [
        pltpu.VMEM((key_count // step, 2 * width, step), BF16),
        pltpu.VMEM((key_count // step, step, 2 * rows), F32),
        pltpu.VMEM((count // rows, key_count, rows), F32),
    ]
    in_specs = [smem(), smem(), smem(), column(count), column(key_count), column(key_count)]
    args = [first, q_sizes, k_sizes, queries, keys, values]
    out_specs = [
        result(count),
        pl.BlockSpec((1, blocks, 1, 2 * rows), lambda pair: (pair, 0, 0, 0)),
    ]
    out_shape = [
        jax.ShapeDtypeStruct((count, pairs * 2 * width), BF16),
        jax.ShapeDtypeStruct((pairs, blocks, 1, 2 * rows), F32),
    ]
    if causal:
        in_specs.append(pl.BlockSpec((1, 2, table.shape[2]), lambda pair: (pair + pair_first, 0, 0)))
        args.append(table)
        tiles = (1, key_count // tile, tile, 2 * tile)
        out_specs.append(pl.BlockSpec(tiles, lambda pair: (pair, 0, 0, 0)))
        out_shape.append(jax.ShapeDtypeStruct((pairs, *tiles[1:]), F32))
    return pl.pallas_call(
        ignoring(functools.partial(forward_kernel, causal, step, width), len(args), len(after)),
        grid=(pairs,),
        in_specs=in_specs + [unread()] * len(after),
        out_specs=out_specs,
        out_shape=out_shape,
        scratch_shapes=scratch,
        compiler_params=pltpu.CompilerParams(vmem_limit_bytes=60 << 20),
        cost_estimate=cost,
        name="self_forward" if causal else "cross_forward",
    )(*args, *after)


def attention_backward(
    first, q_sizes, k_sizes, queries, keys, values, grads, totals, table, width, step, span, after=()
):
    causal = table is not None
    count, model = queries.shape
    key_count = keys.shape[0]
    rows, tile = min(512, count), min(256, count)
    step = key_count if causal else min(step, key_count)
    pair_first, pairs = span
    blocks = count // rows
    column = lambda size: pl.BlockSpec((size, 2 * width), lambda pair: (0, pair + pair_first))
    result = lambda size: pl.BlockSpec((size, 2 * width), lambda pair: (0, pair))
    n_step = key_count // step
    scratch = [
        pltpu.VMEM((n_step, 2 * width, step), BF16),
        pltpu.VMEM((n_step, step, 2 * rows), F32),
        pltpu.VMEM((n_step, step, 2 * rows), F32),
        pltpu.VMEM((key_count, 2 * width), F32),
        pltpu.VMEM((key_count, 2 * width), F32),
        pltpu.VMEM((count // rows, key_count, rows), F32),
    ]
    in_specs = [
        smem(), smem(), smem(), column(count), column(key_count), column(key_count), column(count),
        pl.BlockSpec((1, blocks, 1, 2 * rows), lambda pair: (pair, 0, 0, 0)),
    ]
    args = [first, q_sizes, k_sizes, queries, keys, values, grads, totals]
    out_specs = [result(count), result(key_count), result(key_count)]
    out_shape = [
        jax.ShapeDtypeStruct((count, pairs * 2 * width), BF16),
        jax.ShapeDtypeStruct((key_count, pairs * 2 * width), BF16),
        jax.ShapeDtypeStruct((key_count, pairs * 2 * width), BF16),
    ]
    if causal:
        in_specs.append(pl.BlockSpec((1, *table.shape[1:]), lambda pair: (pair, 0, 0, 0)))
        args.append(table)
        deltas = key_count // tile
        scratch.append(pltpu.VMEM((deltas, tile, 2 * tile), F32))
        out_specs.append(pl.BlockSpec((1, 2, (deltas + 1) * tile), lambda pair: (pair, 0, 0)))
        out_shape.append(jax.ShapeDtypeStruct((pairs, 2, (deltas + 1) * tile), F32))
    return pl.pallas_call(
        ignoring(functools.partial(backward_kernel, causal, step, width), len(args), len(after)),
        grid=(pairs,),
        in_specs=in_specs + [unread()] * len(after),
        out_specs=out_specs,
        out_shape=out_shape,
        scratch_shapes=scratch,
        compiler_params=pltpu.CompilerParams(vmem_limit_bytes=60 << 20),
        cost_estimate=LONG,
        name="self_backward" if causal else "cross_backward",
    )(*args, *after)


def bias_window(distance_buckets, position_bias, first, rows):
    key_count = distance_buckets.shape[0]
    tile = min(256, rows)
    margin = key_count - rows + tile
    buckets = jnp.arange(position_bias.shape[0], dtype=jnp.int32)
    one_hot = (distance_buckets[:, None] == buckets[None, :]).astype(F32)
    one_hot = jnp.pad(one_hot, ((margin, 0), (0, 0)))
    one_hot = lax.dynamic_slice_in_dim(one_hot, first, key_count + tile, 0)
    table = jnp.einsum("db,bh->hd", one_hot, position_bias, precision=EXACT)
    return table.reshape(position_bias.shape[1] // 2, 2, key_count + tile), one_hot


def bias_gradient(diagonals, one_hot):
    diagonals = diagonals.reshape(-1, one_hot.shape[0])
    return jnp.einsum("db,hd->bh", one_hot, diagonals, precision=EXACT)


def send_batch(block, distance):
    count = lax.axis_size("batch")
    return lax.ppermute(block, "batch", [(i, i ^ distance) for i in range(count)])


def send_mem(block):
    return lax.ppermute(block, "mem", [(0, 1), (1, 0)])


def place(pieces, mine):
    ordered = []
    for index in range(len(pieces)):
        chosen = pieces[0]
        for distance in range(1, len(pieces)):
            chosen = jnp.where(mine == (index ^ distance), pieces[distance], chosen)
        ordered.append(chosen)
    return jnp.stack(ordered)


def grid_place():
    batch_index = lax.axis_index("batch")
    return batch_index >> 2, (batch_index >> 1) & 1, batch_index & 1, lax.axis_index("mem")


def gather_plain(shard):
    within = lax.all_gather(shard, "mem", axis=2, tiled=True)
    return lax.all_gather(within, "batch", axis=1, tiled=True)


def scatter_plain(whole):
    part = lax.psum_scatter(whole, "batch", scatter_dimension=1, tiled=True)
    return lax.psum_scatter(part, "mem", scatter_dimension=2, tiled=True).astype(F32)


def whole_spec(shape):
    return pl.BlockSpec(tuple(shape), lambda *_: (0,) * len(shape))


def kernel_call(
    body, name, grid, in_specs, out_specs, out_shape, args, scratch=(), after=()
):
    return pl.pallas_call(
        ignoring(body, len(args), len(after)),
        grid=grid,
        in_specs=in_specs + [unread()] * len(after),
        out_specs=out_specs,
        out_shape=out_shape,
        scratch_shapes=list(scratch),
        compiler_params=pltpu.CompilerParams(vmem_limit_bytes=60 << 20),
        cost_estimate=MEDIUM if name.endswith("kernel") else SHORT,
        name=name,
    )(*args, *after)


def simple_call(body, name, out_shape, args, after=(), spot=None):
    lead = [] if spot is None else [spot]
    return kernel_call(
        body, name, (1,), [smem()] * len(lead) + [whole_spec(arg.shape) for arg in args],
        [whole_spec(shape.shape) for shape in out_shape], out_shape, (*lead, *args), after=after,
    )


def place_line(spot, pieces, after=()):
    count = len(pieces)
    half = count // 2
    shape = jax.ShapeDtypeStruct((half, *pieces[0].shape), BF16)

    def body(spot_ref, *refs):
        low_ref, high_ref = refs[count:]
        for distance in range(count):
            z = spot_ref[0] ^ distance

            @pl.when(z < half)
            def lower():
                low_ref[z] = refs[distance][...]

            @pl.when(z >= half)
            def upper():
                high_ref[z - half] = refs[distance][...]

    return simple_call(body, "place_line", [shape, shape], pieces, after, spot)


def place_pairs(spot, axes, pairs, after=()):
    shapes = [jax.ShapeDtypeStruct((2, *own.shape), BF16) for own, _ in pairs]

    def body(spot_ref, *refs):
        for index, axis in enumerate(axes):
            own_ref, far_ref, out_ref = refs[2 * index], refs[2 * index + 1], refs[2 * len(axes) + index]
            mine = spot_ref[axis]
            out_ref[mine] = own_ref[...]
            out_ref[1 - mine] = far_ref[...]

    return simple_call(body, "place_pairs", shapes, [part for pair in pairs for part in pair], after, spot)


def line_of(shard):
    return [shard] + [send_batch(shard, 4 * d) for d in range(1, lax.axis_size("batch") // 4)]


def gather_first(spot, low, high, after=()):
    return place_pairs(spot, (3, 1), ((low, send_mem(low)), (high, send_batch(high, 2))), after)


def gather_second(spot, low, high, after=()):
    return place_pairs(spot, (1, 3), ((low, send_batch(low, 2)), (high, send_mem(high))), after)


def gather_cores(low, high):
    return low, send_batch(low, 1), high, send_batch(high, 1)


def add_refs(refs):
    total = refs[0][...].astype(F32)
    for ref in refs[1:]:
        total = total + ref[...].astype(F32)
    return total


def scatter_step(groups, after, axes):
    def body(*refs):
        outs = refs[2 * len(groups) :]
        for index, axis in enumerate(axes):
            total = add_refs(refs[2 * index : 2 * index + 2]).astype(BF16)
            cut = (slice(None),) * axis
            outs[2 * index][...] = total[(*cut, 0)]
            outs[2 * index + 1][...] = total[(*cut, 1)]

    in_specs, out_specs, shapes, args = [], [], [], []
    for (kept, received), axis in zip(groups, axes):
        args += [kept, received]
        block = (1, *kept.shape[1:])
        zeros = (0,) * (len(block) - 1)
        in_specs += [pl.BlockSpec(block, lambda z, zeros=zeros: (z, *zeros))] * 2
        rest = kept.shape[:axis] + kept.shape[axis + 1 :]
        out_specs += [pl.BlockSpec((1, *rest[1:]), lambda z, zeros=zeros: (z, *zeros[1:]))] * 2
        shapes += [jax.ShapeDtypeStruct(rest, BF16)] * 2
    outs = kernel_call(
        body, "scatter_step", (args[0].shape[0],), in_specs, out_specs, shapes, args, after=after
    )
    return [tuple(outs[2 * index : 2 * index + 2]) for index in range(len(groups))]


def scatter_to_line(groups, after):
    count = groups[0][0].shape[0]
    ends = [0]
    for kept, _ in groups:
        ends.append(ends[-1] + kept.shape[1])

    def body(*refs):
        outs = refs[2 * len(groups) :]
        for index in range(len(groups)):
            total = add_refs(refs[2 * index : 2 * index + 2]).astype(BF16)
            for distance in range(count):
                outs[distance][ends[index] : ends[index + 1], :] = total[distance]

    shapes = [jax.ShapeDtypeStruct((ends[-1], 128), BF16)] * count
    return simple_call(body, "scatter_to_line", shapes, [part for group in groups for part in group], after)


def send_line(pieces):
    return [pieces[0]] + [send_batch(pieces[d], 4 * d) for d in range(1, len(pieces))]


def scatter_end(groups, out_shapes, moves, after):
    def body(*refs):
        outs = refs[sum(len(group) for group in groups) :]
        totals, start = [], 0
        for group in groups:
            totals.append(add_refs(refs[start : start + len(group)]))
            start += len(group)
        for group, first, rows, out, index in moves:
            outs[out][index] = totals[group][first : first + rows]

    shapes = [jax.ShapeDtypeStruct(shape, F32) for shape in out_shapes]
    return simple_call(body, "scatter_end", shapes, [part for group in groups for part in group], after)


def square_moves(units, slab, columns, outputs):
    moves, used = [], {}
    for group, matrix, block in units:
        first = used.get(group, 0)
        used[group] = first + slab
        out, index = outputs[matrix]
        span = slice(block * 128, (block + 1) * 128)
        moves.append((group, first, slab, out, (slice(None), span) if index is None else (index, slice(None), span)))
    return moves


def sum_small(block, distances, after):
    count = lax.axis_size("batch") * 2
    parts = [block]
    for distance in distances:
        pairs = [(i, i ^ distance) for i in range(count)]
        parts.append(lax.ppermute(block, ("batch", "mem"), pairs))

    def body(*refs):
        values = [ref[...] for ref in refs[:-1]]
        while len(values) > 1:
            values = [values[i] + values[i + 1] for i in range(0, len(values), 2)]
        refs[-1][...] = values[0]

    return simple_call(body, "sum_small", [jax.ShapeDtypeStruct(block.shape, F32)], parts, after)[0]


def add_rows(block, far, after):
    rows, width = block.shape

    def body(one_ref, far_a, far_b, out_ref):
        other = jnp.where(pl.program_id(0) < 2, far_a[...], far_b[...])
        out_ref[...] = one_ref[...] + other.astype(F32)

    part = (rows // 4, width)
    spec = pl.BlockSpec(part, lambda i: (i, 0))
    halves = [
        pl.BlockSpec(part, lambda i: (jnp.minimum(i, 1), 0)),
        pl.BlockSpec(part, lambda i: (jnp.maximum(i - 2, 0), 0)),
    ]
    shape = jax.ShapeDtypeStruct(block.shape, F32)
    return kernel_call(body, "add_rows", (4,), [spec, *halves], spec, shape, (block, *far), after=after)


def chosen(block, axis, index):
    return lax.dynamic_index_in_dim(block, index, axis, keepdims=False)


def all_rows(block):
    if lax.axis_size("mem") == 2:
        return place([block, send_mem(block)], lax.axis_index("mem")).reshape(-1, block.shape[1])
    return lax.all_gather(block, "mem", axis=0, tiled=True)


def own_rows(partial_rows):
    mem_count = lax.axis_size("mem")
    if mem_count == 2:
        halves = partial_rows.reshape(2, -1, partial_rows.shape[1])
        index = lax.axis_index("mem")
        far = send_mem(chosen(halves, 0, 1 - index).astype(BF16))
        return chosen(halves, 0, index) + far.astype(F32)
    return lax.psum_scatter(
        partial_rows.astype(BF16), "mem", scatter_dimension=0, tiled=True
    ).astype(F32)


def mm(left, right):
    return dot(left, right, NN)


def mm_t(left, right):
    return dot(left, right, NT)


def t_mm(left, right):
    return dot(left, right, (((0,), (0,)), ((), ())))


def weight_specs(pack, index):
    return [
        pl.BlockSpec(
            part.shape[:3] + (1,) + part.shape[4:], lambda *_: (0, 0, 0, index, 0, 0)
        )
        for part in pack
    ]


def columns_of(spot_ref, refs, index, column):
    low_own, low_far, high_own, high_far = refs
    half = low_own.shape[2]
    pieces = []
    for z in range(2 * half):
        for y in range(2):
            for core in range(2):
                if z < half:
                    spot = (y, column, z, index)
                    own, far = low_own[spot], low_far[spot]
                else:
                    spot = (column, y, z - half, index)
                    own, far = high_own[spot], high_far[spot]
                pieces.append(jnp.where(spot_ref[2] == core, own, far))
    return jnp.concatenate(pieces, axis=0)


def matrix_of(spot_ref, refs, index=0):
    return jnp.concatenate(
        [columns_of(spot_ref, refs, index, 0), columns_of(spot_ref, refs, index, 1)], axis=1
    )


def join(parts):
    return jnp.concatenate([part[...] for part in parts], axis=1)


def store_shard(place_ref, keep_ref, send_ref, z, y, x, unit, even, odd):
    at_z, at_y, at_core, at_x = (place_ref[axis] for axis in range(4))
    rows = even.shape[0]
    span = slice(unit, unit + rows)
    keep_ref[z ^ at_z, y ^ at_y, x ^ at_x, span, :] = jnp.where(at_core == 0, even, odd)
    send_ref[z ^ at_z, y ^ at_y, x ^ at_x, span, :] = jnp.where(at_core == 0, odd, even)


def store_square(place_ref, targets, matrix, z_count):
    rounded = matrix.astype(BF16)
    rows, columns = rounded.shape[0] // (4 * z_count), rounded.shape[1] // 2
    for z in range(z_count):
        for y in range(2):
            start = (z * 2 + y) * 2 * rows
            for x in range(2):
                for index, (keep_ref, send_ref, unit) in enumerate(targets):
                    span = slice(x * columns + index * 128, x * columns + (index + 1) * 128)
                    store_shard(
                        place_ref, keep_ref, send_ref, z, y, x, unit,
                        rounded[start : start + rows, span],
                        rounded[start + rows : start + 2 * rows, span],
                    )


def piece_shape(z_count, rows):
    return jax.ShapeDtypeStruct((z_count, 2, 2, rows, 128), BF16)


def inverse_rms(values):
    return lax.rsqrt(jnp.mean(values * values, axis=1, keepdims=True) + EPSILON)


def norm_backward(values, gain_row, grads):
    scale = inverse_rms(values)
    normed = values * scale
    gain_grad = jnp.sum(grads * normed, axis=0, keepdims=True)
    pulled = grads * gain_row
    inner = jnp.mean(pulled * normed, axis=1, keepdims=True)
    return scale * (pulled - normed * inner), gain_grad


def project_self(place, own, far, gains, pack, after):
    rows, width = own.shape
    columns = width // 2

    def body(place_ref, own_ref, far_ref, gains_ref, *refs):
        weights, (q_ref, k_ref, v_ref, normed_ref) = refs[:4], refs[4:]
        at_x = place_ref[3]
        here = pl.ds(pl.multiple_of(at_x * rows, rows), rows)
        there = pl.ds(pl.multiple_of((1 - at_x) * rows, rows), rows)

        @pl.when(pl.program_id(0) == 0)
        def normalise():
            for source, span in ((own_ref, here), (far_ref, there)):
                values = source[...].astype(F32)
                normed_ref[span, :] = (values * inverse_rms(values) * gains_ref[0:1, :]).astype(BF16)

        q_ref[...] = mm(normed_ref[here, :], columns_of(place_ref, weights, 0, 0)).astype(BF16)
        normed = normed_ref[...]
        k_ref[...] = mm(normed, columns_of(place_ref, weights, 1, 0)).astype(BF16)
        v_ref[...] = mm(normed, columns_of(place_ref, weights, 2, 0)).astype(BF16)

    low, high = pack[0], pack[2]
    low_spec = pl.BlockSpec(low.shape[:1] + (1,) + low.shape[2:], lambda m: (0, m, 0, 0, 0, 0))
    high_spec = pl.BlockSpec((1,) + high.shape[1:], lambda m: (m, 0, 0, 0, 0, 0))
    return kernel_call(
        body, "project_self_kernel", (2,),
        [
            smem(), whole_spec(own.shape), whole_spec(far.shape), whole_spec(gains.shape),
            low_spec, low_spec, high_spec, high_spec,
        ],
        [
            pl.BlockSpec((rows, columns), lambda m: (0, m)),
            pl.BlockSpec((2 * rows, columns), lambda m: (0, m)),
            pl.BlockSpec((2 * rows, columns), lambda m: (0, m)),
            whole_spec((2 * rows, width)),
        ],
        [
            jax.ShapeDtypeStruct((rows, width), BF16),
            jax.ShapeDtypeStruct((2 * rows, width), BF16),
            jax.ShapeDtypeStruct((2 * rows, width), BF16),
            jax.ShapeDtypeStruct((2 * rows, width), BF16),
        ],
        (place, own, far, gains, *pack),
        after=after,
    )


def specs_of(arrays):
    return [whole_spec(array.shape) for array in arrays]


def after_self(place, own, attn, gains, pack):
    rows, width = own.shape
    count = len(attn)

    def body(place_ref, own_ref, gains_ref, *refs):
        attended = join(refs[:count])
        out_weight, q_weight = refs[count : count + 4], refs[count + 4 : count + 8]
        middle_ref, normed_ref, q_ref = refs[count + 8 :]
        middle = own_ref[...].astype(F32) + mm(attended, matrix_of(place_ref, out_weight))
        middle_ref[...] = middle
        normed = (middle * inverse_rms(middle) * gains_ref[1:2, :]).astype(BF16)
        normed_ref[...] = normed
        q_ref[...] = mm(normed, matrix_of(place_ref, q_weight)).astype(BF16)

    return kernel_call(
        body, "after_self_kernel", (1,),
        [smem(), whole_spec(own.shape), whole_spec(gains.shape), *specs_of(attn)]
        + weight_specs(pack, 3) + weight_specs(pack, 0),
        [whole_spec(own.shape)] * 3,
        [
            jax.ShapeDtypeStruct((rows, width), F32),
            jax.ShapeDtypeStruct((rows, width), BF16),
            jax.ShapeDtypeStruct((rows, width), BF16),
        ],
        (place, own, gains, *attn, *pack, *pack),
    )


def three_way(step, own_ref, far_a, far_b):
    return jnp.where(step < 2, own_ref[...], jnp.where(step == 2, far_a[...], far_b[...]))


def project_memory(place, own, far, pack):
    rows, width = own.shape
    step = rows // 2

    def body(place_ref, own_ref, far_a, far_b, *refs):
        k_ref, v_ref = refs[8:]
        source = three_way(pl.program_id(0), own_ref, far_a, far_b)
        k_ref[...] = mm(source, matrix_of(place_ref, refs[:4])).astype(BF16)
        v_ref[...] = mm(source, matrix_of(place_ref, refs[4:8])).astype(BF16)

    def result(i, place_ref):
        return ((place_ref[3] ^ (i // 2)) * 2 + i % 2, 0)

    shape = jax.ShapeDtypeStruct((2 * rows, width), BF16)
    return pl.pallas_call(
        body,
        grid_spec=pltpu.PrefetchScalarGridSpec(
            num_scalar_prefetch=1,
            grid=(4,),
            in_specs=[
                pl.BlockSpec((step, width), lambda i, _: (jnp.minimum(i, 1), 0)),
                whole_spec((step, width)),
                whole_spec((step, width)),
            ]
            + weight_specs(pack, 1) + weight_specs(pack, 2),
            out_specs=[pl.BlockSpec((step, width), result)] * 2,
        ),
        out_shape=[shape, shape],
        compiler_params=pltpu.CompilerParams(vmem_limit_bytes=60 << 20),
        cost_estimate=MEDIUM,
        name="project_memory_kernel",
    )(place, own, *far, *pack, *pack)


def feed_forward(place, middle_one, attn, cotangent, gains, pack, wide, half):
    rows, width = cotangent.shape
    batch_count = wide.shape[0]
    slab = width // batch_count
    chunk = half // 2
    across = chunk // 128
    down_rows = half * 2 // batch_count
    down_across = width // 256
    down_units = down_across * down_rows

    def body(
        place_ref, middle_ref, attn_ref, cot_ref, gains_ref, co_one, co_two, co_three, co_four,
        gate_ref, up_ref, down_ref, out_ref, grad_middle_ref, grad_attn_ref, gain_ref, wide_grad,
        middle_two, normed, normed_t, grad_normed, result,
    ):
        step = pl.program_id(0)
        co_refs = (co_one, co_two, co_three, co_four)

        @pl.when(step == 0)
        def start():
            middle = middle_ref[...] + mm(attn_ref[...], matrix_of(place_ref, co_refs))
            middle_two[...] = middle
            rounded = (middle * inverse_rms(middle) * gains_ref[2:3, :]).astype(BF16)
            normed[...] = rounded
            normed_t[...] = rounded.T
            grad_normed[...] = jnp.zeros_like(grad_normed)
            result[...] = middle

        def wide_weight(ref):
            blocks = [
                ref[:, 0, index * slab : (index + 1) * slab, :].reshape(width, 128)
                for index in range(across)
            ]
            return jnp.concatenate(blocks, axis=1)

        cot = cot_ref[...]
        gate_weight, up_weight = wide_weight(gate_ref), wide_weight(up_ref)
        down_weight = jnp.concatenate(
            [
                down_ref[:, x, index * down_rows : (index + 1) * down_rows, :].reshape(chunk, 128)
                for x in range(2)
                for index in range(down_across)
            ],
            axis=1,
        )
        gate = mm(normed[...], gate_weight)
        up = mm(normed[...], up_weight)
        square = gate * gate
        bend = jnp.tanh(GELU_SCALE * (gate + GELU_CUBE * (gate * square)))
        half_one = 0.5 * (1.0 + bend)
        gelu = gate * half_one
        slope = half_one + 0.5 * gate * (1.0 - bend * bend) * (
            GELU_SCALE * (1.0 + 3.0 * GELU_CUBE * square)
        )
        act = (gelu * up).astype(BF16)
        result[...] += mm(act, down_weight)
        grad_act = mm_t(cot, down_weight)
        grad_gate = (grad_act * up * slope).astype(BF16)
        grad_up = (grad_act * gelu).astype(BF16)
        grad_normed[...] += mm_t(grad_gate, gate_weight) + mm_t(grad_up, up_weight)
        down_grad = t_mm(act, cot).astype(BF16)
        gate_rows = 2 * across * slab
        for block in range(chunk // down_rows):
            for x in range(2):
                for index in range(down_across):
                    span = slice((x * down_across + index) * 128, (x * down_across + index + 1) * 128)
                    start_row = 2 * gate_rows + index * down_rows
                    wide_grad[step * (chunk // down_rows) + block, x, start_row : start_row + down_rows, :] = (
                        down_grad[block * down_rows : (block + 1) * down_rows, span]
                    )
        for which, grad in enumerate((grad_gate, grad_up)):
            whole = mm(normed_t[...], grad).astype(BF16).reshape(batch_count, slab, chunk)
            for index in range(across):
                start_row = pl.multiple_of(
                    which * gate_rows + (step % 2) * across * slab + index * slab, slab
                )
                wide_grad[:, step // 2, pl.ds(start_row, slab), :] = whole[
                    :, :, index * 128 : (index + 1) * 128
                ]

        @pl.when(step == pl.num_programs(0) - 1)
        def finish():
            out_ref[...] = result[...].astype(BF16)
            pulled, gain_grad = norm_backward(middle_two[...], gains_ref[2:3, :], grad_normed[...])
            gain_ref[...] = gain_grad
            grad_middle = cot_ref[...].astype(F32) + pulled
            grad_middle_ref[...] = grad_middle
            branch = grad_middle.astype(BF16)
            grad_attn_ref[...] = mm_t(branch, matrix_of(place_ref, co_refs)).astype(BF16)

    row_shape = (rows, width)
    wide_spec = lambda which: pl.BlockSpec(
        (batch_count, 1, across * slab, 128), lambda i: (0, i // 2, 2 * which + i % 2, 0)
    )
    down_spec = pl.BlockSpec(
        (chunk // down_rows, 2, down_units, 128), lambda i: (i, 0, 4 * across * slab // down_units, 0)
    )
    return kernel_call(
        body, "feed_forward_kernel", (4,),
        [smem(), *[whole_spec(row_shape)] * 3, whole_spec(gains.shape)] + weight_specs(pack, 4) + [wide_spec(0), wide_spec(1), down_spec],
        [whole_spec(row_shape)] * 3 + [whole_spec((1, width)), whole_spec(wide.shape)],
        [
            jax.ShapeDtypeStruct(row_shape, BF16),
            jax.ShapeDtypeStruct(row_shape, F32),
            jax.ShapeDtypeStruct(row_shape, BF16),
            jax.ShapeDtypeStruct((1, width), F32),
            jax.ShapeDtypeStruct(wide.shape, BF16),
        ],
        (place, middle_one, attn, cotangent, gains, *pack, wide, wide, wide),
        scratch=[
            pltpu.VMEM(row_shape, F32), pltpu.VMEM(row_shape, BF16), pltpu.VMEM((width, rows), BF16),
            pltpu.VMEM(row_shape, F32), pltpu.VMEM(row_shape, F32),
        ],
    )


def after_cross(
    place, grad_query, middle_one, grad_middle_two, normed_cross, attn_self, attn_cross, gains, pack, after
):
    rows, width = middle_one.shape
    z_count = pack[0].shape[2] * 2
    slab = pack[0].shape[4]
    one, two = len(grad_query), len(attn_self)

    def body(place_ref, middle_ref, grad_ref, normed_ref, cross_ref, gains_ref, *refs):
        grad_query = join(refs[:one])
        attended = join(refs[one : one + two])
        so_refs, q_refs = refs[one + two : one + two + 4], refs[one + two + 4 : one + two + 8]
        grad_middle_ref, grad_attn_ref, gain_ref, keep_ref, send_ref = refs[one + two + 8 :]
        grads = mm_t(grad_query, matrix_of(place_ref, q_refs))
        pulled, gain_grad = norm_backward(middle_ref[...], gains_ref[1:2, :], grads)
        gain_ref[...] = gain_grad
        grad_middle = grad_ref[...] + pulled
        grad_middle_ref[...] = grad_middle
        branch = grad_middle.astype(BF16)
        grad_attn_ref[...] = mm_t(branch, matrix_of(place_ref, so_refs)).astype(BF16)
        branch_two = grad_ref[...].astype(BF16)
        for index, (left, right) in enumerate(
            ((normed_ref[...], grad_query), (attended, branch), (cross_ref[...], branch_two))
        ):
            targets = [(keep_ref, send_ref, (3 * index + part) * slab) for part in range(3)]
            store_square(place_ref, targets, t_mm(left, right), z_count)

    pieces = piece_shape(z_count, 9 * slab)
    row_shape = (rows, width)
    return kernel_call(
        body, "after_cross_kernel", (1,),
        [smem()] + [whole_spec(row_shape)] * 4 + [whole_spec(gains.shape)]
        + specs_of(grad_query) + specs_of(attn_self)
        + weight_specs(pack, 3) + weight_specs(pack, 0),
        [whole_spec(row_shape), whole_spec(row_shape), whole_spec((1, width))]
        + [whole_spec(pieces.shape)] * 2,
        [
            jax.ShapeDtypeStruct(row_shape, F32),
            jax.ShapeDtypeStruct(row_shape, BF16),
            jax.ShapeDtypeStruct((1, width), F32),
            pieces,
            pieces,
        ],
        (
            place, middle_one, grad_middle_two, normed_cross, attn_cross, gains,
            *grad_query, *attn_self, *pack, *pack,
        ),
        after=after,
    )


def memory_backward(place, grad_key, grad_value, own, far, pack):
    rows, width = own.shape
    step = rows // 2
    z_count = pack[0].shape[2] * 2
    slab = pack[0].shape[4]

    def body(
        place_ref, dk_ref, dv_ref, own_ref, far_a, far_b, *refs,
    ):
        k_refs, v_refs = refs[:4], refs[4:8]
        grad_own_ref, grad_far_a, grad_far_b, keep_ref, send_ref, key_total, value_total = refs[8:]
        i = pl.program_id(0)
        source = three_way(i ^ 2, own_ref, far_a, far_b)
        source_t = source.T

        @pl.when(i == 0)
        def clear():
            key_total[...] = jnp.zeros_like(key_total)
            value_total[...] = jnp.zeros_like(value_total)

        grad_key, grad_value = dk_ref[...], dv_ref[...]
        key_total[...] += mm(source_t, grad_key)
        value_total[...] += mm(source_t, grad_value)
        grads = mm_t(grad_key, matrix_of(place_ref, k_refs)) + mm_t(
            grad_value, matrix_of(place_ref, v_refs)
        )

        @pl.when(i == 0)
        def there_first():
            grad_far_a[...] = grads.astype(BF16)

        @pl.when(i == 1)
        def there_second():
            grad_far_b[...] = grads.astype(BF16)

        @pl.when(i >= 2)
        def here():
            grad_own_ref[...] = grads

        @pl.when(i == 3)
        def finish():
            for index, total in enumerate((key_total, value_total)):
                targets = [(keep_ref, send_ref, (3 * index + part) * slab) for part in range(3)]
                store_square(place_ref, targets, total[...], z_count)

    def block(i, place_ref):
        return ((place_ref[3] ^ (1 - i // 2)) * 2 + i % 2, 0)

    pieces = piece_shape(z_count, 6 * slab)
    return pl.pallas_call(
        body,
        grid_spec=pltpu.PrefetchScalarGridSpec(
            num_scalar_prefetch=1,
            grid=(4,),
            in_specs=[
                *[pl.BlockSpec((step, width), block)] * 2,
                pl.BlockSpec((step, width), lambda i, _: (jnp.maximum(i - 2, 0), 0)),
                whole_spec((step, width)),
                whole_spec((step, width)),
            ]
            + weight_specs(pack, 1) + weight_specs(pack, 2),
            out_specs=[
                pl.BlockSpec((step, width), lambda i, _: (jnp.maximum(i - 2, 0), 0)),
                whole_spec((step, width)),
                whole_spec((step, width)),
                whole_spec(pieces.shape),
                whole_spec(pieces.shape),
            ],
            scratch_shapes=[pltpu.VMEM((width, width), F32), pltpu.VMEM((width, width), F32)],
        ),
        out_shape=[
            jax.ShapeDtypeStruct((rows, width), F32),
            jax.ShapeDtypeStruct((step, width), BF16),
            jax.ShapeDtypeStruct((step, width), BF16),
            pieces,
            pieces,
        ],
        compiler_params=pltpu.CompilerParams(vmem_limit_bytes=60 << 20),
        cost_estimate=MEDIUM,
        name="memory_backward_kernel",
    )(place, grad_key, grad_value, own, *far, *pack, *pack)


def self_weight_grads(place, grad_query, grad_key, grad_value, normed, z_count, after):
    rows, half = grad_query[0].shape
    width = 2 * half
    slab = width // (4 * z_count)

    def body(place_ref, dq_a, dq_b, dk_a, dk_b, dv_a, dv_b, normed_ref, keep_a, send_a, keep_b, send_b):
        here = pl.ds(pl.multiple_of(place_ref[3] * rows, rows), rows)
        normed_t = normed_ref[...].T
        grads = (
            t_mm(normed_ref[here, :], join((dq_a, dq_b))),
            mm(normed_t, join((dk_a, dk_b))),
            mm(normed_t, join((dv_a, dv_b))),
        )
        for index, grad in enumerate(grads):
            targets = []
            for unit in range(3 * index, 3 * index + 3):
                first = unit < 5
                targets.append(
                    (keep_a if first else keep_b, send_a if first else send_b, (unit if first else unit - 5) * slab)
                )
            store_square(place_ref, targets, grad, z_count)

    shapes = [piece_shape(z_count, count * slab) for count in (5, 5, 4, 4)]
    return kernel_call(
        body, "self_weight_grads_kernel", (1,),
        [smem()] + [whole_spec((rows, half))] * 2 + [whole_spec((2 * rows, half))] * 4
        + [whole_spec((2 * rows, width))],
        [whole_spec(shape.shape) for shape in shapes],
        shapes,
        (place, *grad_query, *grad_key, *grad_value, normed),
        after=after,
    )


def self_row_grads(place, own, far, gains, grad_query, grad_key, grad_value, pack, after):
    rows, half = grad_query[0].shape
    width = 2 * half

    def body(place_ref, own_rows, far_rows, dq_a, dq_b, dk_a, dk_b, dv_a, dv_b, *refs):
        weights, (own_ref, far_ref, gain_ref) = refs[:4], refs[4:]
        key_weight = matrix_of(place_ref, weights, 1)
        value_weight = matrix_of(place_ref, weights, 2)
        here = pl.ds(pl.multiple_of(place_ref[3] * rows, rows), rows)
        there = pl.ds(pl.multiple_of((1 - place_ref[3]) * rows, rows), rows)
        split = lambda pair, span: jnp.concatenate([pair[0][span, :], pair[1][span, :]], axis=1)
        keys, values = (dk_a, dk_b), (dv_a, dv_b)

        def gain_of(rows_ref, grads):
            values = rows_ref[...].astype(F32)
            return jnp.sum(grads * (values * inverse_rms(values)), axis=0, keepdims=True)

        far_grads = mm_t(split(keys, there), key_weight) + mm_t(split(values, there), value_weight)
        far_ref[...] = far_grads.astype(BF16)
        own_grads = (
            mm_t(split(keys, here), key_weight)
            + mm_t(split(values, here), value_weight)
            + mm_t(join((dq_a, dq_b)), matrix_of(place_ref, weights, 0))
        )
        own_ref[...] = own_grads
        gain_ref[...] = gain_of(own_rows, own_grads) + gain_of(far_rows, far_grads)

    row_shape = (rows, width)
    return kernel_call(
        body, "self_row_grads_kernel", (1,),
        [smem()] + [whole_spec(row_shape)] * 2
        + specs_of(grad_query) + specs_of(grad_key) + specs_of(grad_value) + specs_of(pack),
        [whole_spec(row_shape)] * 2 + [whole_spec((1, width))],
        [
            jax.ShapeDtypeStruct(row_shape, F32),
            jax.ShapeDtypeStruct(row_shape, BF16),
            jax.ShapeDtypeStruct((1, width), F32),
        ],
        (place, own, far, *grad_query, *grad_key, *grad_value, *pack),
        after=after,
    )


def finish_rows(own, grads, far_grads, grad_middle, gains, after):
    def body(own_ref, grads_ref, far_ref, middle_ref, gains_ref, out_ref):
        total = grads_ref[...] + far_ref[...].astype(F32)
        pulled, _ = norm_backward(own_ref[...].astype(F32), gains_ref[0:1, :], total)
        out_ref[...] = middle_ref[...] + pulled

    shape = jax.ShapeDtypeStruct(own.shape, F32)
    return simple_call(body, "finish_rows_kernel", [shape], [own, grads, far_grads, grad_middle, gains], after)[0]


def shards_plain(
    hidden,
    memory,
    decoder_lengths,
    memory_lengths,
    distance_buckets,
    norm_gains,
    position_bias,
    self_weights,
    self_output,
    cross_weights,
    cross_output,
    expand_weights,
    contract_weight,
    cotangent,
):
    mem_count = lax.axis_size("mem")
    mem_index = lax.axis_index("mem")
    row_count, model_width = hidden.shape[1:]
    head_count = position_bias.shape[1]
    head_width = model_width // head_count
    key_count = row_count * mem_count
    first_row = mem_index * row_count
    first = jnp.reshape(first_row, (1,)).astype(jnp.int32)

    self_full = gather_plain(self_weights)
    tokens_all = all_rows(hidden[0])
    memory_all = all_rows(memory[0])
    square_full = gather_plain(
        jnp.concatenate([cross_weights, self_output[None], cross_output[None]])
    )
    cross_full, self_out_full, cross_out_full = square_full[:3], square_full[3], square_full[4]
    expand_full = gather_plain(expand_weights)
    contract_full = gather_plain(contract_weight[None])[0]

    distance_table, one_hot = bias_window(distance_buckets, position_bias, first_row, row_count)

    tokens = hidden[0].astype(F32)
    normed_self, pull_self = jax.vjp(rms_norm, tokens, norm_gains[0])
    input_self = normed_self.astype(BF16)
    input_all = rms_norm(tokens_all.astype(F32), norm_gains[0]).astype(BF16)
    query_self = mm(input_self, self_full[0]).astype(BF16)
    key_self = mm(input_all, self_full[1]).astype(BF16)
    value_self = mm(input_all, self_full[2]).astype(BF16)
    attn_self, self_totals, tiles = attention_forward(
        first, decoder_lengths, decoder_lengths, query_self, key_self, value_self,
        distance_table, head_width, key_count, (0, head_count // 2),
    )
    middle_one = tokens + mm(attn_self, self_out_full)
    normed_cross, pull_cross = jax.vjp(rms_norm, middle_one, norm_gains[1])
    input_cross = normed_cross.astype(BF16)
    query_cross = mm(input_cross, cross_full[0]).astype(BF16)
    key_memory = mm(memory_all, cross_full[1]).astype(BF16)
    value_memory = mm(memory_all, cross_full[2]).astype(BF16)
    attn_cross, cross_totals = attention_forward(
        first, decoder_lengths, memory_lengths, query_cross, key_memory, value_memory,
        None, head_width, memory_all.shape[0], (0, head_count // 2),
    )
    middle_two = middle_one + mm(attn_cross, cross_out_full)
    normed_feed, pull_feed = jax.vjp(rms_norm, middle_two, norm_gains[2])
    input_feed = normed_feed.astype(BF16)
    gate_part = mm(input_feed, expand_full[0])
    up_part = mm(input_feed, expand_full[1])
    activated, pull_activate = jax.vjp(activate, gate_part, up_part)
    hidden_act = activated.astype(BF16)
    result_rows = middle_two + mm(hidden_act, contract_full)
    grad_branch_three = cotangent[0]
    grad_out = grad_branch_three.astype(F32)
    grad_gate, grad_up = pull_activate(mm_t(grad_branch_three, contract_full))
    grad_gate, grad_up = grad_gate.astype(BF16), grad_up.astype(BF16)
    contract_grad = scatter_plain(t_mm(hidden_act, grad_branch_three).astype(BF16)[None])[0]
    expand_grad = scatter_plain(
        jnp.stack([t_mm(input_feed, grad_gate), t_mm(input_feed, grad_up)]).astype(BF16)
    )
    grad_norm_two, gain_grad_three = pull_feed(
        mm_t(grad_gate, expand_full[0]) + mm_t(grad_up, expand_full[1])
    )
    grad_middle_two = grad_out + grad_norm_two
    grad_branch_two = grad_middle_two.astype(BF16)
    grad_cross_out = t_mm(attn_cross, grad_branch_two)
    grad_attn_cross = mm_t(grad_branch_two, cross_out_full).astype(BF16)
    grad_query_cross, grad_key_memory, grad_value_memory = attention_backward(
        first, decoder_lengths, memory_lengths, query_cross, key_memory, value_memory,
        grad_attn_cross, cross_totals, None, head_width, memory_all.shape[0], (0, head_count // 2),
    )
    cross_grads = scatter_plain(
        jnp.stack(
            [
                t_mm(input_cross, grad_query_cross),
                t_mm(memory_all, grad_key_memory),
                t_mm(memory_all, grad_value_memory),
                grad_cross_out,
            ]
        ).astype(BF16)
    )
    memory_gradient = own_rows(
        mm_t(grad_key_memory, cross_full[1]) + mm_t(grad_value_memory, cross_full[2])
    )
    grad_norm_one, gain_grad_two = pull_cross(mm_t(grad_query_cross, cross_full[0]))
    grad_middle_one = grad_middle_two + grad_norm_one
    grad_branch_one = grad_middle_one.astype(BF16)
    grad_self_out = t_mm(attn_self, grad_branch_one)
    grad_attn_self = mm_t(grad_branch_one, self_out_full).astype(BF16)
    grad_query_self, grad_key_self, grad_value_self, diagonals = attention_backward(
        first, decoder_lengths, decoder_lengths, query_self, key_self, value_self,
        grad_attn_self, self_totals, tiles, head_width, key_count, (0, head_count // 2),
    )
    bias_partial = bias_gradient(diagonals, one_hot)
    self_grads = scatter_plain(
        jnp.stack(
            [
                t_mm(input_self, grad_query_self),
                t_mm(input_all, grad_key_self),
                t_mm(input_all, grad_value_self),
                grad_self_out,
            ]
        ).astype(BF16)
    )
    grad_input_self = own_rows(
        mm_t(grad_key_self, self_full[1]) + mm_t(grad_value_self, self_full[2])
    ) + mm_t(grad_query_self, self_full[0])
    grad_norm_zero, gain_grad_one = pull_self(grad_input_self)
    grad_tokens = grad_middle_one + grad_norm_zero
    gain_sums, bias_sums = lax.psum(
        (jnp.stack([gain_grad_one, gain_grad_two, gain_grad_three]), bias_partial), ("batch", "mem")
    )
    return (
        result_rows.astype(BF16)[None],
        grad_tokens[None],
        memory_gradient[None],
        gain_sums,
        bias_sums,
        self_grads[:3],
        self_grads[3],
        cross_grads[:3],
        cross_grads[3],
        expand_grad,
        contract_grad,
    )


def shards_hops(
    hidden,
    memory,
    decoder_lengths,
    memory_lengths,
    distance_buckets,
    norm_gains,
    position_bias,
    self_weights,
    self_output,
    cross_weights,
    cross_output,
    expand_weights,
    contract_weight,
    cotangent,
):
    batch_count, mem_count = lax.axis_size("batch"), lax.axis_size("mem")
    row_count, model_width = hidden.shape[1:]
    bucket_count, head_count = position_bias.shape
    head_width = model_width // head_count
    key_count = row_count * mem_count
    spot = jnp.stack(grid_place()).astype(jnp.int32)
    first = jnp.reshape(lax.axis_index("mem") * row_count, (1,)).astype(jnp.int32)
    own, own_memory = hidden[0], memory[0]

    slab, columns = self_weights.shape[1:]
    z_count = batch_count // 4

    pairs = head_count // 2
    pairs = head_count // 2
    far = send_mem(own)
    low, high = place_line(spot, line_of(self_weights))
    across = expand_weights.shape[2] // 128
    wide = jnp.concatenate(
        [
            expand_weights.reshape(2, slab, across, 128).transpose(0, 2, 1, 3).reshape(-1, 128),
            contract_weight.reshape(-1, columns // 128, 128).transpose(1, 0, 2).reshape(-1, 128),
        ]
    )
    second = jnp.concatenate([cross_weights, self_output[None], cross_output[None]])
    (second,) = hold((second,), (low, high))
    line = line_of(second)
    low, high = gather_first(spot, low, high, (far,))
    low, high = gather_second(spot, low, high)
    middle = own_memory.shape[0] // 2
    memory_a, wide = hold((own_memory[:middle], wide), (low, high))
    far_memory_a = send_mem(memory_a)
    wide = lax.all_gather(wide, ("batch", "mem"), axis=0, tiled=False)
    wide = wide.reshape(batch_count, mem_count, *wide.shape[1:])
    self_pack = gather_cores(low, high)

    distance_table, one_hot = bias_window(
        distance_buckets, position_bias, lax.axis_index("mem") * row_count, row_count
    )

    query_self, key_self, value_self, normed_self = project_self(
        spot, own, far, norm_gains, self_pack, ()
    )

    halves = ((0, pairs // 2), (pairs // 2, pairs // 2))

    def self_forward(span, after, cost):
        return attention_forward(
            first, decoder_lengths, decoder_lengths, query_self, key_self, value_self,
            distance_table, head_width, key_count, span, after, cost,
        )

    low, high = place_line(spot, line, (query_self,))
    one = self_forward(halves[0], (low, high), LONG)
    low, high = gather_first(spot, low, high, (one[0], far_memory_a))
    two = self_forward(halves[1], (low, high), LONG)
    low, high = gather_second(spot, low, high, (two[0],))
    (memory_b,) = hold((own_memory[middle:],), (low, high))
    far_memory = (far_memory_a, send_mem(memory_b))
    square_pack = gather_cores(low, high)
    attn_self, self_totals, tiles = zip(one, two)
    middle_one, normed_cross, query_cross = after_self(spot, own, attn_self, norm_gains, square_pack)
    key_memory, value_memory = project_memory(spot, own_memory, far_memory, square_pack)
    attn_cross, cross_totals = attention_forward(
        first, decoder_lengths, memory_lengths, query_cross, key_memory, value_memory,
        None, head_width, key_memory.shape[0], (0, pairs),
    )
    (
        result, grad_middle_two, grad_attn_cross, gain_three, wide_grad,
    ) = feed_forward(
        spot, middle_one, attn_cross, cotangent[0], norm_gains, square_pack, wide, expand_weights.shape[2]
    )
    wide_grad = lax.psum_scatter(
        wide_grad.reshape(batch_count * mem_count, *wide_grad.shape[2:]),
        ("batch", "mem"), scatter_dimension=0, tiled=True,
    )[0]
    grad_query_cross, grad_key_memory, grad_value_memory = attention_backward(
        first, decoder_lengths, memory_lengths, query_cross, key_memory, value_memory,
        grad_attn_cross, cross_totals, None, head_width, key_memory.shape[0], (0, pairs),
    )
    memory_own, memory_far_a, memory_far_b, kv_keep, kv_send = memory_backward(
        spot, grad_key_memory, grad_value_memory, own_memory, far_memory, square_pack
    )
    grad_middle_one, grad_attn_self, gain_two, qo_keep, qo_send = after_cross(
        spot, (grad_query_cross,), middle_one, grad_middle_two, normed_cross, attn_self, attn_cross,
        norm_gains, square_pack, (memory_far_a,),
    )

    def self_backward(half, after):
        return attention_backward(
            first, decoder_lengths, decoder_lengths, query_self, key_self, value_self,
            grad_attn_self, self_totals[half], tiles[half], head_width, key_count, halves[half], after,
        )

    one = self_backward(0, (qo_keep,))
    (kv_keep, kv_send), (qo_keep, qo_send) = scatter_step(
        ((kv_keep, send_batch(kv_send, 1)), (qo_keep, send_batch(qo_send, 1))), (one[0],), (2, 1)
    )
    (memory_far_b,) = hold((memory_far_b,), (kv_keep, qo_keep))
    memory_far = (send_mem(memory_far_a), send_mem(memory_far_b))
    two = self_backward(1, (kv_keep, one[0], memory_far[0]))
    grad_query_self, grad_key_self, grad_value_self, diagonals = zip(one, two)
    rows_own, rows_far, gain_one = self_row_grads(
        spot, own, far, norm_gains, grad_query_self, grad_key_self, grad_value_self, self_pack, ()
    )
    (kv_keep, kv_send), (qo_keep, qo_send) = scatter_step(
        ((kv_keep, send_mem(kv_send)), (qo_keep, send_batch(qo_send, 2))),
        (rows_own, memory_far[1]), (1, 1),
    )
    rows_far = send_mem(rows_far)
    bias_partial = bias_gradient(jnp.concatenate(diagonals, axis=0), one_hot)
    gains = jnp.concatenate([gain_one, gain_two, gain_three], axis=0)
    sums = jnp.concatenate([gains.reshape(-1), bias_partial.reshape(-1)]).reshape(-1, 128)
    keep_a, send_a, keep_b, send_b = self_weight_grads(
        spot, grad_query_self, grad_key_self, grad_value_self, normed_self, z_count, (kv_keep, sums)
    )
    sums = sum_small(sums, (2, 4, 6), (keep_a,))
    (keep_a, send_a), (keep_b, send_b) = scatter_step(
        ((keep_a, send_batch(send_a, 1)), (keep_b, send_batch(send_b, 1))), (sums,), (2, 1)
    )
    line = scatter_to_line(
        ((kv_keep, send_batch(kv_send, 2)), (qo_keep, send_mem(qo_send))), (keep_a,)
    )
    sums = sum_small(sums, (8, 16, 24), (line[0],))
    memory_gradient = add_rows(memory_own, memory_far, (sums,))
    (keep_a, send_a), (keep_b, send_b) = scatter_step(
        ((keep_a, send_mem(send_a)), (keep_b, send_batch(send_b, 2))), (memory_gradient,), (1, 1)
    )
    hidden_gradient = finish_rows(own, rows_own, rows_far, grad_middle_one, norm_gains, (keep_a,))
    self_line = scatter_to_line(
        ((keep_a, send_batch(send_a, 2)), (keep_b, send_mem(send_b))), (hidden_gradient,)
    )
    units = [(0, matrix, block) for matrix in range(5) for block in range(3)]
    cross_grad, self_out_grad, cross_out_grad = scatter_end(
        (send_line(line),),
        (cross_weights.shape, self_output.shape, cross_output.shape),
        square_moves(units, slab, columns, ((0, 1), (0, 2), (0, 0), (1, None), (2, None))),
        (self_line[0],),
    )
    sums = sum_small(sums, (1,), (cross_grad,)).reshape(-1)
    units = [(0, unit // 3, unit % 3) for unit in range(9)]
    (self_grad,) = scatter_end(
        (send_line(self_line),), (self_weights.shape,),
        square_moves(units, slab, columns, ((0, 0), (0, 1), (0, 2))), (sums,),
    )
    gate_rows, down_rows = across * slab, contract_weight.shape[0]
    moves = []
    for which in range(2):
        for block in range(across):
            span = (which, slice(None), slice(block * 128, block * 128 + 128))
            moves.append((0, which * gate_rows + block * slab, slab, 0, span))
    for block in range(columns // 128):
        span = (slice(None), slice(block * 128, block * 128 + 128))
        moves.append((0, 2 * gate_rows + block * down_rows, down_rows, 1, span))
    expand_grad, contract_grad = scatter_end(
        ((wide_grad,),), (expand_weights.shape, contract_weight.shape), moves, (self_line[0],)
    )
    return (
        result[None],
        hidden_gradient[None],
        memory_gradient[None],
        sums[: gains.size].reshape(gains.shape),
        sums[gains.size :].reshape(bucket_count, head_count),
        self_grad,
        self_out_grad,
        cross_grad,
        cross_out_grad,
        expand_grad,
        contract_grad,
    )


def shards(*arrays):
    row_count, slab, columns = arrays[0].shape[1], arrays[7].shape[1], arrays[7].shape[2]
    allowed = row_count == 512 and slab % 16 == 0 and columns % 128 == 0
    if lax.axis_size("mem") == 2 and lax.axis_size("batch") == 16 and allowed:
        return shards_hops(*arrays)
    return shards_plain(*arrays)


def solution(mesh):
    placed = (
        P("batch", "mem", None),
        P("batch", "mem", None),
        P("batch", None),
        P("batch", None),
        P(),
        P(),
        P(),
        P(None, "batch", "mem"),
        P("batch", "mem"),
        P(None, "batch", "mem"),
        P("batch", "mem"),
        P(None, "batch", "mem"),
        P("batch", "mem"),
        P("batch", "mem", None),
    )
    return jax.shard_map(
        shards,
        mesh=mesh,
        in_specs=placed,
        out_specs=(
            P("batch", "mem", None),
            P("batch", "mem", None),
            P("batch", "mem", None),
            P(),
            P(),
            P(None, "batch", "mem"),
            P("batch", "mem"),
            P(None, "batch", "mem"),
            P("batch", "mem"),
            P(None, "batch", "mem"),
            P("batch", "mem"),
        ),
        check_vma=False,
    )
```

```python
import functools
import math

import jax
import jax.numpy as jnp
from jax import lax
from jax.experimental import pallas as pl
from jax.experimental.pallas import tpu as pltpu
from jax.sharding import PartitionSpec as P

EPSILON = 1e-06
NEGATIVE = -1e30
F32 = jnp.float32
BF16 = jnp.bfloat16
EXACT = lax.Precision.HIGHEST
GELU_SCALE = (2 / math.pi) ** 0.5
GELU_CUBE = 0.044715
LONG = pl.CostEstimate(flops=20_000_000_000, bytes_accessed=1_000, transcendentals=0)
MEDIUM = pl.CostEstimate(flops=6_000_000_000, bytes_accessed=1_000, transcendentals=0)
BRIEF = pl.CostEstimate(flops=2_000_000_000, bytes_accessed=1_000, transcendentals=0)
SHORT = pl.CostEstimate(flops=100_000, bytes_accessed=1_000, transcendentals=0)
NT = (((1,), (1,)), ((), ()))
NN = (((1,), (0,)), ((), ()))


def rms_norm(values, gain_row):
    return (
        values * lax.rsqrt(jnp.mean(values * values, axis=-1, keepdims=True) + EPSILON) * gain_row
    )


def activate(gate_part, up_part):
    return jax.nn.gelu(gate_part, approximate=True) * up_part


def dot(left, right, dims):
    return lax.dot_general(left, right, dims, preferred_element_type=F32)


def bounds_of(sizes_ref):
    edges = [jnp.int32(0)]
    for slot in range(sizes_ref.shape[1]):
        edges.append(edges[-1] + sizes_ref[0, slot])
    return edges


def pick(place, edges, values):
    chosen = jnp.zeros_like(place) + values[0]
    for slot in range(1, len(edges) - 1):
        chosen = jnp.where(place >= edges[slot], values[slot], chosen)
    return chosen


def stack_heads(block, width):
    lane = lax.broadcasted_iota(jnp.int32, block.shape, 1)
    zero = jnp.zeros_like(block)
    return jnp.concatenate(
        [jnp.where(lane < width, block, zero), jnp.where(lane < width, zero, block)], axis=0
    )


def transposed_blocks(source_ref, scratch, step):
    for index in range(scratch.shape[0]):
        scratch[index] = source_ref[index * step : (index + 1) * step, :].T


def limits(first, rows, q_edges, k_edges, causal):
    place = lax.broadcasted_iota(jnp.int32, (1, rows), 1) + first
    begin = pick(place, q_edges, k_edges[:-1])
    end = pick(place, q_edges, k_edges[1:])
    if causal:
        end = jnp.minimum(end, place + 1)
    return begin, end


def fold(block, combine):
    parts = [block[start : start + 8] for start in range(0, block.shape[0], 8)]
    while len(parts) > 1:
        joined = [combine(parts[i], parts[i + 1]) for i in range(0, len(parts) - 1, 2)]
        parts = joined + parts[2 * len(joined) :]
    return parts[0]


def fill_mask(mask, first, q_edges, k_edges, causal):
    blocks, key_count, rows = mask.shape
    for block in range(blocks):
        begin, end = limits(first + block * rows, rows, q_edges, k_edges, causal)
        place = lax.broadcasted_iota(jnp.int32, (key_count, rows), 0)
        mask[block] = jnp.where((place >= begin) & (place < end), 0.0, NEGATIVE)


def fill_tiles(table_ref, tiles):
    count, tile = tiles.shape[:2]
    for head in range(2):
        wide = jnp.broadcast_to(table_ref[0, head : head + 1, :], (8, (count + 1) * tile))
        wide = pltpu.roll(wide, 0, 1, stride=1, stride_axis=0)
        for start in range(0, tile, 8):
            moved = pltpu.roll(wide, start, 1) if start else wide
            for index in range(count):
                tiles[index, start : start + 8, head * tile : (head + 1) * tile] = moved[
                    :, (index + 1) * tile : (index + 2) * tile
                ]


def sum_diagonals(tiles, out_ref):
    count, tile = tiles.shape[:2]
    for head in range(2):
        parts = jnp.zeros((8, (count + 1) * tile), F32)
        for start in range(0, tile, 8):
            line = [jnp.zeros((8, tile), F32)]
            for index in range(count):
                line.append(tiles[index, start : start + 8, head * tile : (head + 1) * tile])
            line = jnp.concatenate(line, axis=1)
            parts = parts + (pltpu.roll(line, line.shape[1] - start, 1) if start else line)
        line = parts[0:1]
        for row in range(1, 8):
            line = line + pltpu.roll(parts[row : row + 1], parts.shape[1] - row, 1)
        out_ref[0, head : head + 1, :] = line


def tile_of(u, t, key_tiles, row_tiles):
    return key_tiles - row_tiles + t - u


def bias_of(tiles, key_tiles, row_tiles):
    tile = tiles.shape[1]
    lines = []
    for u in range(key_tiles):
        line = [
            tiles[max(tile_of(u, t, key_tiles, row_tiles), 0), :, head * tile : (head + 1) * tile]
            for head in range(2)
            for t in range(row_tiles)
        ]
        lines.append(jnp.concatenate(line, axis=1))
    return jnp.concatenate(lines, axis=0)


def score_block(k_ref, queries, mask, tiles, block, index, step):
    here = pl.ds(pl.multiple_of(index * step, step), step)
    scores = dot(k_ref[here, :], queries, NT)
    if tiles is not None:
        tile = tiles.shape[1]
        scores = scores + bias_of(tiles, step // tile, queries.shape[0] // 2 // tile)
    hidden = mask[block, here, :]
    return scores + jnp.concatenate([hidden, hidden], axis=1)


def key_range(first, rows, q_edges, k_edges, step):
    high = pick(first + rows - 1, q_edges, k_edges[1:])
    return pick(first, q_edges, k_edges[:-1]) // step, (high + step - 1) // step


def forward_kernel(causal, step, width, first_ref, q_sizes, k_sizes, q_ref, k_ref, v_ref, *rest):
    if causal:
        table_ref, out_ref, total_ref, tiles_ref, value_t, scores, mask = rest
        tiles = tiles_ref.at[0]
    else:
        out_ref, total_ref, value_t, scores, mask = rest
        tiles = None
    blocks, rows = total_ref.shape[1], total_ref.shape[3] // 2
    q_edges = bounds_of(q_sizes)
    k_edges = bounds_of(k_sizes)

    @pl.when(pl.program_id(0) == 0)
    def once():
        fill_mask(mask, first_ref[0], q_edges, k_edges, causal)

    transposed_blocks(v_ref, value_t, step)
    if causal:
        fill_tiles(table_ref, tiles)
    for block in range(blocks):
        first = first_ref[0] + block * rows
        low, high = (0, 1) if causal else key_range(first, rows, q_edges, k_edges, step)
        queries = stack_heads(q_ref[block * rows : (block + 1) * rows, :], width)

        def measure(index, top):
            block_scores = score_block(k_ref, queries, mask, tiles, block, index, step)
            scores[index] = block_scores
            return jnp.maximum(top, fold(block_scores, jnp.maximum))

        top = lax.fori_loop(low, high, measure, jnp.full((8, 2 * rows), NEGATIVE, F32))
        top = jnp.max(top, axis=0, keepdims=True)

        def gather(index, carry):
            total, out_a, out_b = carry
            weights = jnp.exp(scores[index] - top)
            total = total + fold(weights, jnp.add)
            rounded = weights.astype(BF16)
            out_a = out_a + dot(value_t[index], rounded[:, :rows], NN)
            out_b = out_b + dot(value_t[index], rounded[:, rows:], NN)
            return total, out_a, out_b

        zero = jnp.zeros((2 * width, rows), F32)
        total, out_a, out_b = lax.fori_loop(
            low, high, gather, (jnp.zeros((8, 2 * rows), F32), zero, zero)
        )
        total = jnp.sum(total, axis=0, keepdims=True)
        joined = jnp.concatenate(
            [out_a[:width] / total[:, :rows], out_b[width:] / total[:, rows:]], axis=0
        )
        out_ref[block * rows : (block + 1) * rows, :] = joined.T.astype(BF16)
        total_ref[0, block] = top + jnp.log(total)


def backward_kernel(
    causal, step, width, first_ref, q_sizes, k_sizes, q_ref, k_ref, v_ref, g_ref, total_ref, *rest
):
    if causal:
        tiles_ref, dq_ref, dk_ref, dv_ref, diag_ref, key_t, probs, grads, dk, dv, mask, sums = rest
        tiles = tiles_ref.at[0]
    else:
        dq_ref, dk_ref, dv_ref, key_t, probs, grads, dk, dv, mask = rest
        tiles = None
    blocks, rows = total_ref.shape[1], total_ref.shape[3] // 2
    q_edges = bounds_of(q_sizes)
    k_edges = bounds_of(k_sizes)

    @pl.when(pl.program_id(0) == 0)
    def once():
        fill_mask(mask, first_ref[0], q_edges, k_edges, causal)

    transposed_blocks(k_ref, key_t, step)
    dk[...] = jnp.zeros_like(dk)
    dv[...] = jnp.zeros_like(dv)
    for block in range(blocks):
        first = first_ref[0] + block * rows
        low, high = (0, 1) if causal else key_range(first, rows, q_edges, k_edges, step)
        queries = stack_heads(q_ref[block * rows : (block + 1) * rows, :], width)
        targets = stack_heads(g_ref[block * rows : (block + 1) * rows, :], width)
        total = total_ref[0, block]

        def measure(index, inner):
            here = pl.ds(pl.multiple_of(index * step, step), step)
            block_scores = score_block(k_ref, queries, mask, tiles, block, index, step)
            weights = jnp.exp(block_scores - total)
            pulled = dot(v_ref[here, :], targets, NT)
            probs[index] = weights
            grads[index] = pulled
            dv[here, :] += dot(weights.astype(BF16), targets, NN)
            return inner + fold(weights * pulled, jnp.add)

        inner = lax.fori_loop(low, high, measure, jnp.zeros((8, 2 * rows), F32))
        inner = jnp.sum(inner, axis=0, keepdims=True)

        def gather(index, carry):
            out_a, out_b = carry
            here = pl.ds(pl.multiple_of(index * step, step), step)
            rounded = (probs[index] * (grads[index] - inner)).astype(BF16)
            dk[here, :] += dot(rounded, queries, NN)
            if causal:
                tile = tiles.shape[1]
                spots = [(u, t) for u in range(step // tile) for t in range(rows // tile)]
                for which in range(sums.shape[0]):
                    parts = [
                        jnp.concatenate(
                            [
                                rounded[u * tile : (u + 1) * tile, start + t * tile : start + (t + 1) * tile]
                                for start in (0, rows)
                            ],
                            axis=1,
                        ).astype(F32)
                        for u, t in spots
                        if tile_of(u, t, step // tile, rows // tile) == which
                    ]
                    sums[which] = functools.reduce(jnp.add, parts)
            out_a = out_a + dot(key_t[index], rounded[:, :rows], NN)
            out_b = out_b + dot(key_t[index], rounded[:, rows:], NN)
            return out_a, out_b

        zero = jnp.zeros((2 * width, rows), F32)
        out_a, out_b = lax.fori_loop(low, high, gather, (zero, zero))
        joined = jnp.concatenate([out_a[:width], out_b[width:]], axis=0)
        dq_ref[block * rows : (block + 1) * rows, :] = joined.T.astype(BF16)
    dk_ref[...] = dk[...].astype(BF16)
    dv_ref[...] = dv[...].astype(BF16)
    if causal:
        sum_diagonals(sums, diag_ref)


def unread():
    return pl.BlockSpec(memory_space=pl.ANY)


def ignoring(body, first, count):
    return lambda *refs: body(*refs[:first], *refs[first + count :])


def hold(values, after):
    count = len(values)
    return pl.pallas_call(
        lambda *refs: None,
        in_specs=[unread()] * (count + len(after)),
        out_specs=[unread()] * count,
        out_shape=[jax.ShapeDtypeStruct(value.shape, value.dtype) for value in values],
        input_output_aliases={index: index for index in range(count)},
        cost_estimate=SHORT,
        name="hold",
    )(*values, *after)


def smem():
    return pl.BlockSpec(memory_space=pltpu.SMEM)


def attention_forward(
    first, q_sizes, k_sizes, queries, keys, values, table, width, step, span, after=(), cost=LONG
):
    causal = table is not None
    count, model = queries.shape
    key_count = keys.shape[0]
    rows, tile = min(512, count), min(256, count)
    step = key_count if causal else min(step, key_count)
    pair_first, pairs = span
    blocks = count // rows
    column = lambda size: pl.BlockSpec((size, 2 * width), lambda pair: (0, pair + pair_first))
    result = lambda size: pl.BlockSpec((size, 2 * width), lambda pair: (0, pair))
    scratch = [
        pltpu.VMEM((key_count // step, 2 * width, step), BF16),
        pltpu.VMEM((key_count // step, step, 2 * rows), F32),
        pltpu.VMEM((count // rows, key_count, rows), F32),
    ]
    in_specs = [smem(), smem(), smem(), column(count), column(key_count), column(key_count)]
    args = [first, q_sizes, k_sizes, queries, keys, values]
    out_specs = [
        result(count),
        pl.BlockSpec((1, blocks, 1, 2 * rows), lambda pair: (pair, 0, 0, 0)),
    ]
    out_shape = [
        jax.ShapeDtypeStruct((count, pairs * 2 * width), BF16),
        jax.ShapeDtypeStruct((pairs, blocks, 1, 2 * rows), F32),
    ]
    if causal:
        in_specs.append(pl.BlockSpec((1, 2, table.shape[2]), lambda pair: (pair + pair_first, 0, 0)))
        args.append(table)
        tiles = (1, key_count // tile, tile, 2 * tile)
        out_specs.append(pl.BlockSpec(tiles, lambda pair: (pair, 0, 0, 0)))
        out_shape.append(jax.ShapeDtypeStruct((pairs, *tiles[1:]), F32))
    return pl.pallas_call(
        ignoring(functools.partial(forward_kernel, causal, step, width), len(args), len(after)),
        grid=(pairs,),
        in_specs=in_specs + [unread()] * len(after),
        out_specs=out_specs,
        out_shape=out_shape,
        scratch_shapes=scratch,
        compiler_params=pltpu.CompilerParams(vmem_limit_bytes=60 << 20),
        cost_estimate=cost,
        name="self_forward" if causal else "cross_forward",
    )(*args, *after)


def attention_backward(
    first, q_sizes, k_sizes, queries, keys, values, grads, totals, table, width, step, span, after=()
):
    causal = table is not None
    count, model = queries.shape
    key_count = keys.shape[0]
    rows, tile = min(512, count), min(256, count)
    step = key_count if causal else min(step, key_count)
    pair_first, pairs = span
    blocks = count // rows
    column = lambda size: pl.BlockSpec((size, 2 * width), lambda pair: (0, pair + pair_first))
    result = lambda size: pl.BlockSpec((size, 2 * width), lambda pair: (0, pair))
    n_step = key_count // step
    scratch = [
        pltpu.VMEM((n_step, 2 * width, step), BF16),
        pltpu.VMEM((n_step, step, 2 * rows), F32),
        pltpu.VMEM((n_step, step, 2 * rows), F32),
        pltpu.VMEM((key_count, 2 * width), F32),
        pltpu.VMEM((key_count, 2 * width), F32),
        pltpu.VMEM((count // rows, key_count, rows), F32),
    ]
    in_specs = [
        smem(), smem(), smem(), column(count), column(key_count), column(key_count), column(count),
        pl.BlockSpec((1, blocks, 1, 2 * rows), lambda pair: (pair, 0, 0, 0)),
    ]
    args = [first, q_sizes, k_sizes, queries, keys, values, grads, totals]
    out_specs = [result(count), result(key_count), result(key_count)]
    out_shape = [
        jax.ShapeDtypeStruct((count, pairs * 2 * width), BF16),
        jax.ShapeDtypeStruct((key_count, pairs * 2 * width), BF16),
        jax.ShapeDtypeStruct((key_count, pairs * 2 * width), BF16),
    ]
    if causal:
        in_specs.append(pl.BlockSpec((1, *table.shape[1:]), lambda pair: (pair, 0, 0, 0)))
        args.append(table)
        deltas = key_count // tile
        scratch.append(pltpu.VMEM((deltas, tile, 2 * tile), F32))
        out_specs.append(pl.BlockSpec((1, 2, (deltas + 1) * tile), lambda pair: (pair, 0, 0)))
        out_shape.append(jax.ShapeDtypeStruct((pairs, 2, (deltas + 1) * tile), F32))
    return pl.pallas_call(
        ignoring(functools.partial(backward_kernel, causal, step, width), len(args), len(after)),
        grid=(pairs,),
        in_specs=in_specs + [unread()] * len(after),
        out_specs=out_specs,
        out_shape=out_shape,
        scratch_shapes=scratch,
        compiler_params=pltpu.CompilerParams(vmem_limit_bytes=60 << 20),
        cost_estimate=LONG,
        name="self_backward" if causal else "cross_backward",
    )(*args, *after)


def bias_window(distance_buckets, position_bias, first, rows):
    key_count = distance_buckets.shape[0]
    tile = min(256, rows)
    margin = key_count - rows + tile
    buckets = jnp.arange(position_bias.shape[0], dtype=jnp.int32)
    one_hot = (distance_buckets[:, None] == buckets[None, :]).astype(F32)
    one_hot = jnp.pad(one_hot, ((margin, 0), (0, 0)))
    one_hot = lax.dynamic_slice_in_dim(one_hot, first, key_count + tile, 0)
    table = jnp.einsum("db,bh->hd", one_hot, position_bias, precision=EXACT)
    return table.reshape(position_bias.shape[1] // 2, 2, key_count + tile), one_hot


def bias_gradient(diagonals, one_hot):
    diagonals = diagonals.reshape(-1, one_hot.shape[0])
    return jnp.einsum("db,hd->bh", one_hot, diagonals, precision=EXACT)


def send_batch(block, distance):
    count = lax.axis_size("batch")
    return lax.ppermute(block, "batch", [(i, i ^ distance) for i in range(count)])


def send_mem(block):
    return lax.ppermute(block, "mem", [(0, 1), (1, 0)])


def place(pieces, mine):
    ordered = []
    for index in range(len(pieces)):
        chosen = pieces[0]
        for distance in range(1, len(pieces)):
            chosen = jnp.where(mine == (index ^ distance), pieces[distance], chosen)
        ordered.append(chosen)
    return jnp.stack(ordered)


def grid_place():
    batch_index = lax.axis_index("batch")
    return batch_index >> 2, (batch_index >> 1) & 1, batch_index & 1, lax.axis_index("mem")


def gather_plain(shard):
    within = lax.all_gather(shard, "mem", axis=2, tiled=True)
    return lax.all_gather(within, "batch", axis=1, tiled=True)


def scatter_plain(whole):
    part = lax.psum_scatter(whole, "batch", scatter_dimension=1, tiled=True)
    return lax.psum_scatter(part, "mem", scatter_dimension=2, tiled=True).astype(F32)


def whole_spec(shape):
    return pl.BlockSpec(tuple(shape), lambda *_: (0,) * len(shape))


def kernel_call(
    body, name, grid, in_specs, out_specs, out_shape, args, scratch=(), after=()
):
    return pl.pallas_call(
        ignoring(body, len(args), len(after)),
        grid=grid,
        in_specs=in_specs + [unread()] * len(after),
        out_specs=out_specs,
        out_shape=out_shape,
        scratch_shapes=list(scratch),
        compiler_params=pltpu.CompilerParams(vmem_limit_bytes=60 << 20),
        cost_estimate=MEDIUM if name.endswith("kernel") else SHORT,
        name=name,
    )(*args, *after)


def simple_call(body, name, out_shape, args, after=(), spot=None):
    lead = [] if spot is None else [spot]
    return kernel_call(
        body, name, (1,), [smem()] * len(lead) + [whole_spec(arg.shape) for arg in args],
        [whole_spec(shape.shape) for shape in out_shape], out_shape, (*lead, *args), after=after,
    )


def place_line(spot, pieces, after=()):
    count = len(pieces)
    half = count // 2
    shape = jax.ShapeDtypeStruct((half, *pieces[0].shape), BF16)

    def body(spot_ref, *refs):
        low_ref, high_ref = refs[count:]
        for distance in range(count):
            z = spot_ref[0] ^ distance

            @pl.when(z < half)
            def lower():
                low_ref[z] = refs[distance][...]

            @pl.when(z >= half)
            def upper():
                high_ref[z - half] = refs[distance][...]

    return simple_call(body, "place_line", [shape, shape], pieces, after, spot)


def place_pairs(spot, axes, pairs, after=()):
    shapes = [jax.ShapeDtypeStruct((2, *own.shape), BF16) for own, _ in pairs]

    def body(spot_ref, *refs):
        for index, axis in enumerate(axes):
            own_ref, far_ref, out_ref = refs[2 * index], refs[2 * index + 1], refs[2 * len(axes) + index]
            mine = spot_ref[axis]
            out_ref[mine] = own_ref[...]
            out_ref[1 - mine] = far_ref[...]

    return simple_call(body, "place_pairs", shapes, [part for pair in pairs for part in pair], after, spot)


def line_of(shard):
    return [shard] + [send_batch(shard, 4 * d) for d in range(1, lax.axis_size("batch") // 4)]


def gather_first(spot, low, high, after=()):
    return place_pairs(spot, (3, 1), ((low, send_mem(low)), (high, send_batch(high, 2))), after)


def gather_second(spot, low, high, after=()):
    return place_pairs(spot, (1, 3), ((low, send_batch(low, 2)), (high, send_mem(high))), after)


def gather_cores(low, high):
    return low, send_batch(low, 1), high, send_batch(high, 1)


def add_refs(refs):
    total = refs[0][...].astype(F32)
    for ref in refs[1:]:
        total = total + ref[...].astype(F32)
    return total


def scatter_step(groups, after, axes):
    def body(*refs):
        outs = refs[2 * len(groups) :]
        for index, axis in enumerate(axes):
            total = add_refs(refs[2 * index : 2 * index + 2]).astype(BF16)
            cut = (slice(None),) * axis
            outs[2 * index][...] = total[(*cut, 0)]
            outs[2 * index + 1][...] = total[(*cut, 1)]

    in_specs, out_specs, shapes, args = [], [], [], []
    for (kept, received), axis in zip(groups, axes):
        args += [kept, received]
        block = (1, *kept.shape[1:])
        zeros = (0,) * (len(block) - 1)
        in_specs += [pl.BlockSpec(block, lambda z, zeros=zeros: (z, *zeros))] * 2
        rest = kept.shape[:axis] + kept.shape[axis + 1 :]
        out_specs += [pl.BlockSpec((1, *rest[1:]), lambda z, zeros=zeros: (z, *zeros[1:]))] * 2
        shapes += [jax.ShapeDtypeStruct(rest, BF16)] * 2
    outs = kernel_call(
        body, "scatter_step", (args[0].shape[0],), in_specs, out_specs, shapes, args, after=after
    )
    return [tuple(outs[2 * index : 2 * index + 2]) for index in range(len(groups))]


def scatter_to_line(groups, after):
    count = groups[0][0].shape[0]
    ends = [0]
    for kept, _ in groups:
        ends.append(ends[-1] + kept.shape[1])

    def body(*refs):
        outs = refs[2 * len(groups) :]
        for index in range(len(groups)):
            total = add_refs(refs[2 * index : 2 * index + 2]).astype(BF16)
            for distance in range(count):
                outs[distance][ends[index] : ends[index + 1], :] = total[distance]

    shapes = [jax.ShapeDtypeStruct((ends[-1], 128), BF16)] * count
    return simple_call(body, "scatter_to_line", shapes, [part for group in groups for part in group], after)


def send_line(pieces):
    return [pieces[0]] + [send_batch(pieces[d], 4 * d) for d in range(1, len(pieces))]


def scatter_end(groups, out_shapes, moves, after):
    def body(*refs):
        outs = refs[sum(len(group) for group in groups) :]
        totals, start = [], 0
        for group in groups:
            totals.append(add_refs(refs[start : start + len(group)]))
            start += len(group)
        for group, first, rows, out, index in moves:
            outs[out][index] = totals[group][first : first + rows]

    shapes = [jax.ShapeDtypeStruct(shape, F32) for shape in out_shapes]
    return simple_call(body, "scatter_end", shapes, [part for group in groups for part in group], after)


def square_moves(units, slab, columns, outputs):
    moves, used = [], {}
    for group, matrix, block in units:
        first = used.get(group, 0)
        used[group] = first + slab
        out, index = outputs[matrix]
        span = slice(block * 128, (block + 1) * 128)
        moves.append((group, first, slab, out, (slice(None), span) if index is None else (index, slice(None), span)))
    return moves


def sum_small(block, distances, after):
    count = lax.axis_size("batch") * 2
    parts = [block]
    for distance in distances:
        pairs = [(i, i ^ distance) for i in range(count)]
        parts.append(lax.ppermute(block, ("batch", "mem"), pairs))

    def body(*refs):
        values = [ref[...] for ref in refs[:-1]]
        while len(values) > 1:
            values = [values[i] + values[i + 1] for i in range(0, len(values), 2)]
        refs[-1][...] = values[0]

    return simple_call(body, "sum_small", [jax.ShapeDtypeStruct(block.shape, F32)], parts, after)[0]


def add_rows(block, far, after):
    rows, width = block.shape

    def body(one_ref, two_ref, out_ref):
        out_ref[...] = one_ref[...] + two_ref[...].astype(F32)

    spec = pl.BlockSpec((rows // 4, width), lambda i: (i, 0))
    shape = jax.ShapeDtypeStruct(block.shape, F32)
    return kernel_call(body, "add_rows", (4,), [spec, spec], spec, shape, (block, far), after=after)


def chosen(block, axis, index):
    return lax.dynamic_index_in_dim(block, index, axis, keepdims=False)


def all_rows(block):
    if lax.axis_size("mem") == 2:
        return place([block, send_mem(block)], lax.axis_index("mem")).reshape(-1, block.shape[1])
    return lax.all_gather(block, "mem", axis=0, tiled=True)


def own_rows(partial_rows):
    mem_count = lax.axis_size("mem")
    if mem_count == 2:
        halves = partial_rows.reshape(2, -1, partial_rows.shape[1])
        index = lax.axis_index("mem")
        far = send_mem(chosen(halves, 0, 1 - index).astype(BF16))
        return chosen(halves, 0, index) + far.astype(F32)
    return lax.psum_scatter(
        partial_rows.astype(BF16), "mem", scatter_dimension=0, tiled=True
    ).astype(F32)


def mm(left, right):
    return dot(left, right, NN)


def mm_t(left, right):
    return dot(left, right, NT)


def t_mm(left, right):
    return dot(left, right, (((0,), (0,)), ((), ())))


def weight_specs(pack, index):
    return [
        pl.BlockSpec(
            part.shape[:3] + (1,) + part.shape[4:], lambda *_: (0, 0, 0, index, 0, 0)
        )
        for part in pack
    ]


def columns_of(spot_ref, refs, index, column):
    low_own, low_far, high_own, high_far = refs
    half = low_own.shape[2]
    pieces = []
    for z in range(2 * half):
        for y in range(2):
            for core in range(2):
                if z < half:
                    spot = (y, column, z, index)
                    own, far = low_own[spot], low_far[spot]
                else:
                    spot = (column, y, z - half, index)
                    own, far = high_own[spot], high_far[spot]
                pieces.append(jnp.where(spot_ref[2] == core, own, far))
    return jnp.concatenate(pieces, axis=0)


def matrix_of(spot_ref, refs, index=0):
    return jnp.concatenate(
        [columns_of(spot_ref, refs, index, 0), columns_of(spot_ref, refs, index, 1)], axis=1
    )


def join(parts):
    return jnp.concatenate([part[...] for part in parts], axis=1)


def store_shard(place_ref, keep_ref, send_ref, z, y, x, unit, even, odd):
    at_z, at_y, at_core, at_x = (place_ref[axis] for axis in range(4))
    rows = even.shape[0]
    span = slice(unit, unit + rows)
    keep_ref[z ^ at_z, y ^ at_y, x ^ at_x, span, :] = jnp.where(at_core == 0, even, odd)
    send_ref[z ^ at_z, y ^ at_y, x ^ at_x, span, :] = jnp.where(at_core == 0, odd, even)


def store_square(place_ref, targets, matrix, z_count):
    rounded = matrix.astype(BF16)
    rows, columns = rounded.shape[0] // (4 * z_count), rounded.shape[1] // 2
    for z in range(z_count):
        for y in range(2):
            start = (z * 2 + y) * 2 * rows
            for x in range(2):
                for index, (keep_ref, send_ref, unit) in enumerate(targets):
                    span = slice(x * columns + index * 128, x * columns + (index + 1) * 128)
                    store_shard(
                        place_ref, keep_ref, send_ref, z, y, x, unit,
                        rounded[start : start + rows, span],
                        rounded[start + rows : start + 2 * rows, span],
                    )


def piece_shape(z_count, rows):
    return jax.ShapeDtypeStruct((z_count, 2, 2, rows, 128), BF16)


def inverse_rms(values):
    return lax.rsqrt(jnp.mean(values * values, axis=1, keepdims=True) + EPSILON)


def norm_backward(values, gain_row, grads):
    scale = inverse_rms(values)
    normed = values * scale
    gain_grad = jnp.sum(grads * normed, axis=0, keepdims=True)
    pulled = grads * gain_row
    inner = jnp.mean(pulled * normed, axis=1, keepdims=True)
    return scale * (pulled - normed * inner), gain_grad


def project_self(place, own, far, gains, pack, after):
    rows, width = own.shape
    columns = width // 2

    def body(place_ref, own_ref, far_ref, gains_ref, *refs):
        weights, (q_ref, k_ref, v_ref, normed_ref) = refs[:4], refs[4:]
        at_x = place_ref[3]
        here = pl.ds(pl.multiple_of(at_x * rows, rows), rows)
        there = pl.ds(pl.multiple_of((1 - at_x) * rows, rows), rows)

        @pl.when(pl.program_id(0) == 0)
        def normalise():
            for source, span in ((own_ref, here), (far_ref, there)):
                values = source[...].astype(F32)
                normed_ref[span, :] = (values * inverse_rms(values) * gains_ref[0:1, :]).astype(BF16)

        q_ref[...] = mm(normed_ref[here, :], columns_of(place_ref, weights, 0, 0)).astype(BF16)
        normed = normed_ref[...]
        k_ref[...] = mm(normed, columns_of(place_ref, weights, 1, 0)).astype(BF16)
        v_ref[...] = mm(normed, columns_of(place_ref, weights, 2, 0)).astype(BF16)

    low, high = pack[0], pack[2]
    low_spec = pl.BlockSpec(low.shape[:1] + (1,) + low.shape[2:], lambda m: (0, m, 0, 0, 0, 0))
    high_spec = pl.BlockSpec((1,) + high.shape[1:], lambda m: (m, 0, 0, 0, 0, 0))
    return kernel_call(
        body, "project_self_kernel", (2,),
        [
            smem(), whole_spec(own.shape), whole_spec(far.shape), whole_spec(gains.shape),
            low_spec, low_spec, high_spec, high_spec,
        ],
        [
            pl.BlockSpec((rows, columns), lambda m: (0, m)),
            pl.BlockSpec((2 * rows, columns), lambda m: (0, m)),
            pl.BlockSpec((2 * rows, columns), lambda m: (0, m)),
            whole_spec((2 * rows, width)),
        ],
        [
            jax.ShapeDtypeStruct((rows, width), BF16),
            jax.ShapeDtypeStruct((2 * rows, width), BF16),
            jax.ShapeDtypeStruct((2 * rows, width), BF16),
            jax.ShapeDtypeStruct((2 * rows, width), BF16),
        ],
        (place, own, far, gains, *pack),
        after=after,
    )


def specs_of(arrays):
    return [whole_spec(array.shape) for array in arrays]


def after_self(place, own, attn, gains, pack):
    rows, width = own.shape
    count = len(attn)

    def body(place_ref, own_ref, gains_ref, *refs):
        attended = join(refs[:count])
        out_weight, q_weight = refs[count : count + 4], refs[count + 4 : count + 8]
        middle_ref, normed_ref, q_ref = refs[count + 8 :]
        middle = own_ref[...].astype(F32) + mm(attended, matrix_of(place_ref, out_weight))
        middle_ref[...] = middle
        normed = (middle * inverse_rms(middle) * gains_ref[1:2, :]).astype(BF16)
        normed_ref[...] = normed
        q_ref[...] = mm(normed, matrix_of(place_ref, q_weight)).astype(BF16)

    return kernel_call(
        body, "after_self", (1,),
        [smem(), whole_spec(own.shape), whole_spec(gains.shape), *specs_of(attn)]
        + weight_specs(pack, 3) + weight_specs(pack, 0),
        [whole_spec(own.shape)] * 3,
        [
            jax.ShapeDtypeStruct((rows, width), F32),
            jax.ShapeDtypeStruct((rows, width), BF16),
            jax.ShapeDtypeStruct((rows, width), BF16),
        ],
        (place, own, gains, *attn, *pack, *pack),
    )


def halves_of(block):
    return [pl.BlockSpec(block, lambda *_: (0, 0)), pl.BlockSpec(block, lambda *_: (1, 0))]


def three_way(step, own_ref, far_a, far_b):
    return jnp.where(step < 2, own_ref[...], jnp.where(step == 2, far_a[...], far_b[...]))


def project_memory(place, own, far, pack):
    rows, width = own.shape
    step = rows // 2

    def body(place_ref, own_ref, far_a, far_b, *refs):
        k_ref, v_ref, key_weight, value_weight = refs[8:]

        @pl.when(pl.program_id(0) == 0)
        def once():
            key_weight[...] = matrix_of(place_ref, refs[:4])
            value_weight[...] = matrix_of(place_ref, refs[4:8])

        source = three_way(pl.program_id(0), own_ref, far_a, far_b)
        k_ref[...] = mm(source, key_weight[...]).astype(BF16)
        v_ref[...] = mm(source, value_weight[...]).astype(BF16)

    def result(i, place_ref):
        return ((place_ref[3] ^ (i // 2)) * 2 + i % 2, 0)

    shape = jax.ShapeDtypeStruct((2 * rows, width), BF16)
    return pl.pallas_call(
        body,
        grid_spec=pltpu.PrefetchScalarGridSpec(
            num_scalar_prefetch=1,
            grid=(4,),
            in_specs=[
                pl.BlockSpec((step, width), lambda i, _: (jnp.minimum(i, 1), 0)),
                *halves_of((step, width)),
            ]
            + weight_specs(pack, 1) + weight_specs(pack, 2),
            out_specs=[pl.BlockSpec((step, width), result)] * 2,
            scratch_shapes=[pltpu.VMEM((width, width), BF16)] * 2,
        ),
        out_shape=[shape, shape],
        compiler_params=pltpu.CompilerParams(vmem_limit_bytes=60 << 20),
        cost_estimate=MEDIUM,
        name="project_memory_kernel",
    )(place, own, far, far, *pack, *pack)


def feed_forward(place, middle_one, attn, cotangent, gains, pack, wide, half):
    rows, width = cotangent.shape
    batch_count = wide.shape[0]
    slab = width // batch_count
    chunk = half // 2
    across = chunk // 128
    down_rows = half * 2 // batch_count
    down_across = width // 256
    down_units = down_across * down_rows

    def body(
        place_ref, middle_ref, attn_ref, cot_ref, gains_ref, co_one, co_two, co_three, co_four,
        gate_ref, up_ref, down_ref, out_ref, grad_middle_ref, grad_attn_ref, gain_ref, wide_grad,
        middle_two, normed, normed_t, grad_normed, result,
    ):
        step = pl.program_id(0)
        co_refs = (co_one, co_two, co_three, co_four)

        @pl.when(step == 0)
        def start():
            middle = middle_ref[...] + mm(attn_ref[...], matrix_of(place_ref, co_refs))
            middle_two[...] = middle
            rounded = (middle * inverse_rms(middle) * gains_ref[2:3, :]).astype(BF16)
            normed[...] = rounded
            normed_t[...] = rounded.T
            grad_normed[...] = jnp.zeros_like(grad_normed)
            result[...] = middle

        def wide_weight(ref):
            blocks = [
                ref[:, 0, index * slab : (index + 1) * slab, :].reshape(width, 128)
                for index in range(across)
            ]
            return jnp.concatenate(blocks, axis=1)

        cot = cot_ref[...]
        gate_weight, up_weight = wide_weight(gate_ref), wide_weight(up_ref)
        down_weight = jnp.concatenate(
            [
                down_ref[:, x, index * down_rows : (index + 1) * down_rows, :].reshape(chunk, 128)
                for x in range(2)
                for index in range(down_across)
            ],
            axis=1,
        )
        gate = mm(normed[...], gate_weight)
        up = mm(normed[...], up_weight)
        square = gate * gate
        bend = jnp.tanh(GELU_SCALE * (gate + GELU_CUBE * (gate * square)))
        half_one = 0.5 * (1.0 + bend)
        gelu = gate * half_one
        slope = half_one + 0.5 * gate * (1.0 - bend * bend) * (
            GELU_SCALE * (1.0 + 3.0 * GELU_CUBE * square)
        )
        act = (gelu * up).astype(BF16)
        result[...] += mm(act, down_weight)
        grad_act = mm_t(cot, down_weight)
        grad_gate = (grad_act * up * slope).astype(BF16)
        grad_up = (grad_act * gelu).astype(BF16)
        grad_normed[...] += mm_t(grad_gate, gate_weight) + mm_t(grad_up, up_weight)
        down_grad = t_mm(act, cot).astype(BF16)
        gate_rows = 2 * across * slab
        for block in range(chunk // down_rows):
            for x in range(2):
                for index in range(down_across):
                    span = slice((x * down_across + index) * 128, (x * down_across + index + 1) * 128)
                    start_row = 2 * gate_rows + index * down_rows
                    wide_grad[step * (chunk // down_rows) + block, x, start_row : start_row + down_rows, :] = (
                        down_grad[block * down_rows : (block + 1) * down_rows, span]
                    )
        for which, grad in enumerate((grad_gate, grad_up)):
            whole = mm(normed_t[...], grad).astype(BF16).reshape(batch_count, slab, chunk)
            for index in range(across):
                start_row = pl.multiple_of(
                    which * gate_rows + (step % 2) * across * slab + index * slab, slab
                )
                wide_grad[:, step // 2, pl.ds(start_row, slab), :] = whole[
                    :, :, index * 128 : (index + 1) * 128
                ]

        @pl.when(step == pl.num_programs(0) - 1)
        def finish():
            out_ref[...] = result[...].astype(BF16)
            pulled, gain_grad = norm_backward(middle_two[...], gains_ref[2:3, :], grad_normed[...])
            gain_ref[...] = gain_grad
            grad_middle = cot_ref[...].astype(F32) + pulled
            grad_middle_ref[...] = grad_middle
            branch = grad_middle.astype(BF16)
            grad_attn_ref[...] = mm_t(branch, matrix_of(place_ref, co_refs)).astype(BF16)

    row_shape = (rows, width)
    wide_spec = lambda which: pl.BlockSpec(
        (batch_count, 1, across * slab, 128), lambda i: (0, i // 2, 2 * which + i % 2, 0)
    )
    down_spec = pl.BlockSpec(
        (chunk // down_rows, 2, down_units, 128), lambda i: (i, 0, 4 * across * slab // down_units, 0)
    )
    return kernel_call(
        body, "feed_forward_kernel", (4,),
        [smem(), *[whole_spec(row_shape)] * 3, whole_spec(gains.shape)] + weight_specs(pack, 4) + [wide_spec(0), wide_spec(1), down_spec],
        [whole_spec(row_shape)] * 3 + [whole_spec((1, width)), whole_spec(wide.shape)],
        [
            jax.ShapeDtypeStruct(row_shape, BF16),
            jax.ShapeDtypeStruct(row_shape, F32),
            jax.ShapeDtypeStruct(row_shape, BF16),
            jax.ShapeDtypeStruct((1, width), F32),
            jax.ShapeDtypeStruct(wide.shape, BF16),
        ],
        (place, middle_one, attn, cotangent, gains, *pack, wide, wide, wide),
        scratch=[
            pltpu.VMEM(row_shape, F32), pltpu.VMEM(row_shape, BF16), pltpu.VMEM((width, rows), BF16),
            pltpu.VMEM(row_shape, F32), pltpu.VMEM(row_shape, F32),
        ],
    )


def after_cross(
    place, grad_query, middle_one, grad_middle_two, normed_cross, attn_self, attn_cross, gains, pack, after
):
    rows, width = middle_one.shape
    z_count = pack[0].shape[2] * 2
    slab = pack[0].shape[4]
    one, two = len(grad_query), len(attn_self)

    def body(place_ref, middle_ref, grad_ref, normed_ref, cross_ref, gains_ref, *refs):
        grad_query = join(refs[:one])
        attended = join(refs[one : one + two])
        so_refs, q_refs = refs[one + two : one + two + 4], refs[one + two + 4 : one + two + 8]
        grad_middle_ref, grad_attn_ref, gain_ref, keep_ref, send_ref = refs[one + two + 8 :]
        grads = mm_t(grad_query, matrix_of(place_ref, q_refs))
        pulled, gain_grad = norm_backward(middle_ref[...], gains_ref[1:2, :], grads)
        gain_ref[...] = gain_grad
        grad_middle = grad_ref[...] + pulled
        grad_middle_ref[...] = grad_middle
        branch = grad_middle.astype(BF16)
        grad_attn_ref[...] = mm_t(branch, matrix_of(place_ref, so_refs)).astype(BF16)
        branch_two = grad_ref[...].astype(BF16)
        for index, (left, right) in enumerate(
            ((normed_ref[...], grad_query), (attended, branch), (cross_ref[...], branch_two))
        ):
            targets = [(keep_ref, send_ref, (3 * index + part) * slab) for part in range(3)]
            store_square(place_ref, targets, t_mm(left, right), z_count)

    pieces = piece_shape(z_count, 9 * slab)
    row_shape = (rows, width)
    return kernel_call(
        body, "after_cross_kernel", (1,),
        [smem()] + [whole_spec(row_shape)] * 4 + [whole_spec(gains.shape)]
        + specs_of(grad_query) + specs_of(attn_self)
        + weight_specs(pack, 3) + weight_specs(pack, 0),
        [whole_spec(row_shape), whole_spec(row_shape), whole_spec((1, width))]
        + [whole_spec(pieces.shape)] * 2,
        [
            jax.ShapeDtypeStruct(row_shape, F32),
            jax.ShapeDtypeStruct(row_shape, BF16),
            jax.ShapeDtypeStruct((1, width), F32),
            pieces,
            pieces,
        ],
        (
            place, middle_one, grad_middle_two, normed_cross, attn_cross, gains,
            *grad_query, *attn_self, *pack, *pack,
        ),
        after=after,
    )


def memory_backward(place, grad_key, grad_value, own, far, pack):
    rows, width = own.shape
    step = rows // 2
    z_count = pack[0].shape[2] * 2
    slab = pack[0].shape[4]

    def body(
        place_ref, dk_ref, dv_ref, own_ref, far_a, far_b, *refs,
    ):
        k_refs, v_refs = refs[:4], refs[4:8]
        grad_own_ref, grad_far_ref, keep_ref, send_ref = refs[8:12]
        key_total, value_total, key_weight, value_weight = refs[12:]
        i = pl.program_id(0)
        source = three_way(i ^ 2, own_ref, far_a, far_b)
        source_t = source.T

        @pl.when(i == 0)
        def clear():
            key_total[...] = jnp.zeros_like(key_total)
            value_total[...] = jnp.zeros_like(value_total)
            key_weight[...] = matrix_of(place_ref, k_refs)
            value_weight[...] = matrix_of(place_ref, v_refs)

        grad_key, grad_value = dk_ref[...], dv_ref[...]
        key_total[...] += mm(source_t, grad_key)
        value_total[...] += mm(source_t, grad_value)
        grads = mm_t(grad_key, key_weight[...]) + mm_t(grad_value, value_weight[...])

        @pl.when(i < 2)
        def there():
            grad_far_ref[...] = grads.astype(BF16)

        @pl.when(i >= 2)
        def here():
            grad_own_ref[...] = grads

        @pl.when(i == 3)
        def finish():
            for index, total in enumerate((key_total, value_total)):
                targets = [(keep_ref, send_ref, (3 * index + part) * slab) for part in range(3)]
                store_square(place_ref, targets, total[...], z_count)

    def block(i, place_ref):
        return ((place_ref[3] ^ (1 - i // 2)) * 2 + i % 2, 0)

    pieces = piece_shape(z_count, 6 * slab)
    return pl.pallas_call(
        body,
        grid_spec=pltpu.PrefetchScalarGridSpec(
            num_scalar_prefetch=1,
            grid=(4,),
            in_specs=[
                *[pl.BlockSpec((step, width), block)] * 2,
                pl.BlockSpec((step, width), lambda i, _: (jnp.maximum(i - 2, 0), 0)),
                *halves_of((step, width)),
            ]
            + weight_specs(pack, 1) + weight_specs(pack, 2),
            out_specs=[
                pl.BlockSpec((step, width), lambda i, _: (jnp.maximum(i - 2, 0), 0)),
                pl.BlockSpec((step, width), lambda i, _: (jnp.minimum(i, 1), 0)),
                whole_spec(pieces.shape),
                whole_spec(pieces.shape),
            ],
            scratch_shapes=[pltpu.VMEM((width, width), F32)] * 2
            + [pltpu.VMEM((width, width), BF16)] * 2,
        ),
        out_shape=[
            jax.ShapeDtypeStruct((rows, width), F32),
            jax.ShapeDtypeStruct((rows, width), BF16),
            pieces,
            pieces,
        ],
        compiler_params=pltpu.CompilerParams(vmem_limit_bytes=60 << 20),
        cost_estimate=MEDIUM,
        name="memory_backward_kernel",
    )(place, grad_key, grad_value, own, far, far, *pack, *pack)


def self_weight_grads(place, grad_query, grad_key, grad_value, normed, z_count, after):
    rows, half = grad_query[0].shape
    width = 2 * half
    slab = width // (4 * z_count)

    def body(place_ref, dq_a, dq_b, dk_a, dk_b, dv_a, dv_b, normed_ref, keep_a, send_a, keep_b, send_b):
        here = pl.ds(pl.multiple_of(place_ref[3] * rows, rows), rows)
        normed_t = normed_ref[...].T
        grads = (
            t_mm(normed_ref[here, :], join((dq_a, dq_b))),
            mm(normed_t, join((dk_a, dk_b))),
            mm(normed_t, join((dv_a, dv_b))),
        )
        for index, grad in enumerate(grads):
            targets = []
            for unit in range(3 * index, 3 * index + 3):
                first = unit < 5
                targets.append(
                    (keep_a if first else keep_b, send_a if first else send_b, (unit if first else unit - 5) * slab)
                )
            store_square(place_ref, targets, grad, z_count)

    shapes = [piece_shape(z_count, count * slab) for count in (5, 5, 4, 4)]
    return kernel_call(
        body, "self_weight_grads_kernel", (1,),
        [smem()] + [whole_spec((rows, half))] * 2 + [whole_spec((2 * rows, half))] * 4
        + [whole_spec((2 * rows, width))],
        [whole_spec(shape.shape) for shape in shapes],
        shapes,
        (place, *grad_query, *grad_key, *grad_value, normed),
        after=after,
    )


def self_row_grads(place, own, far, gains, grad_query, grad_key, grad_value, pack, after):
    rows, half = grad_query[0].shape
    width = 2 * half

    def body(place_ref, own_rows, far_rows, dq_a, dq_b, dk_a, dk_b, dv_a, dv_b, *refs):
        weights, (own_ref, far_ref, gain_ref) = refs[:4], refs[4:]
        key_weight = matrix_of(place_ref, weights, 1)
        value_weight = matrix_of(place_ref, weights, 2)
        here = pl.ds(pl.multiple_of(place_ref[3] * rows, rows), rows)
        there = pl.ds(pl.multiple_of((1 - place_ref[3]) * rows, rows), rows)
        split = lambda pair, span: jnp.concatenate([pair[0][span, :], pair[1][span, :]], axis=1)
        keys, values = (dk_a, dk_b), (dv_a, dv_b)

        def gain_of(rows_ref, grads):
            values = rows_ref[...].astype(F32)
            return jnp.sum(grads * (values * inverse_rms(values)), axis=0, keepdims=True)

        far_grads = mm_t(split(keys, there), key_weight) + mm_t(split(values, there), value_weight)
        far_ref[...] = far_grads.astype(BF16)
        own_grads = (
            mm_t(split(keys, here), key_weight)
            + mm_t(split(values, here), value_weight)
            + mm_t(join((dq_a, dq_b)), matrix_of(place_ref, weights, 0))
        )
        own_ref[...] = own_grads
        gain_ref[...] = gain_of(own_rows, own_grads) + gain_of(far_rows, far_grads)

    row_shape = (rows, width)
    return kernel_call(
        body, "self_row_grads_kernel", (1,),
        [smem()] + [whole_spec(row_shape)] * 2
        + specs_of(grad_query) + specs_of(grad_key) + specs_of(grad_value) + specs_of(pack),
        [whole_spec(row_shape)] * 2 + [whole_spec((1, width))],
        [
            jax.ShapeDtypeStruct(row_shape, F32),
            jax.ShapeDtypeStruct(row_shape, BF16),
            jax.ShapeDtypeStruct((1, width), F32),
        ],
        (place, own, far, *grad_query, *grad_key, *grad_value, *pack),
        after=after,
    )


def finish_rows(own, grads, far_grads, grad_middle, gains, after):
    def body(own_ref, grads_ref, far_ref, middle_ref, gains_ref, out_ref):
        total = grads_ref[...] + far_ref[...].astype(F32)
        pulled, _ = norm_backward(own_ref[...].astype(F32), gains_ref[0:1, :], total)
        out_ref[...] = middle_ref[...] + pulled

    shape = jax.ShapeDtypeStruct(own.shape, F32)
    return simple_call(body, "finish_rows_kernel", [shape], [own, grads, far_grads, grad_middle, gains], after)[0]


def shards_plain(
    hidden,
    memory,
    decoder_lengths,
    memory_lengths,
    distance_buckets,
    norm_gains,
    position_bias,
    self_weights,
    self_output,
    cross_weights,
    cross_output,
    expand_weights,
    contract_weight,
    cotangent,
):
    mem_count = lax.axis_size("mem")
    mem_index = lax.axis_index("mem")
    row_count, model_width = hidden.shape[1:]
    head_count = position_bias.shape[1]
    head_width = model_width // head_count
    key_count = row_count * mem_count
    first_row = mem_index * row_count
    first = jnp.reshape(first_row, (1,)).astype(jnp.int32)

    self_full = gather_plain(self_weights)
    tokens_all = all_rows(hidden[0])
    memory_all = all_rows(memory[0])
    square_full = gather_plain(
        jnp.concatenate([cross_weights, self_output[None], cross_output[None]])
    )
    cross_full, self_out_full, cross_out_full = square_full[:3], square_full[3], square_full[4]
    expand_full = gather_plain(expand_weights)
    contract_full = gather_plain(contract_weight[None])[0]

    distance_table, one_hot = bias_window(distance_buckets, position_bias, first_row, row_count)

    tokens = hidden[0].astype(F32)
    normed_self, pull_self = jax.vjp(rms_norm, tokens, norm_gains[0])
    input_self = normed_self.astype(BF16)
    input_all = rms_norm(tokens_all.astype(F32), norm_gains[0]).astype(BF16)
    query_self = mm(input_self, self_full[0]).astype(BF16)
    key_self = mm(input_all, self_full[1]).astype(BF16)
    value_self = mm(input_all, self_full[2]).astype(BF16)
    attn_self, self_totals, tiles = attention_forward(
        first, decoder_lengths, decoder_lengths, query_self, key_self, value_self,
        distance_table, head_width, key_count, (0, head_count // 2),
    )
    middle_one = tokens + mm(attn_self, self_out_full)
    normed_cross, pull_cross = jax.vjp(rms_norm, middle_one, norm_gains[1])
    input_cross = normed_cross.astype(BF16)
    query_cross = mm(input_cross, cross_full[0]).astype(BF16)
    key_memory = mm(memory_all, cross_full[1]).astype(BF16)
    value_memory = mm(memory_all, cross_full[2]).astype(BF16)
    attn_cross, cross_totals = attention_forward(
        first, decoder_lengths, memory_lengths, query_cross, key_memory, value_memory,
        None, head_width, memory_all.shape[0], (0, head_count // 2),
    )
    middle_two = middle_one + mm(attn_cross, cross_out_full)
    normed_feed, pull_feed = jax.vjp(rms_norm, middle_two, norm_gains[2])
    input_feed = normed_feed.astype(BF16)
    gate_part = mm(input_feed, expand_full[0])
    up_part = mm(input_feed, expand_full[1])
    activated, pull_activate = jax.vjp(activate, gate_part, up_part)
    hidden_act = activated.astype(BF16)
    result_rows = middle_two + mm(hidden_act, contract_full)
    grad_branch_three = cotangent[0]
    grad_out = grad_branch_three.astype(F32)
    grad_gate, grad_up = pull_activate(mm_t(grad_branch_three, contract_full))
    grad_gate, grad_up = grad_gate.astype(BF16), grad_up.astype(BF16)
    contract_grad = scatter_plain(t_mm(hidden_act, grad_branch_three).astype(BF16)[None])[0]
    expand_grad = scatter_plain(
        jnp.stack([t_mm(input_feed, grad_gate), t_mm(input_feed, grad_up)]).astype(BF16)
    )
    grad_norm_two, gain_grad_three = pull_feed(
        mm_t(grad_gate, expand_full[0]) + mm_t(grad_up, expand_full[1])
    )
    grad_middle_two = grad_out + grad_norm_two
    grad_branch_two = grad_middle_two.astype(BF16)
    grad_cross_out = t_mm(attn_cross, grad_branch_two)
    grad_attn_cross = mm_t(grad_branch_two, cross_out_full).astype(BF16)
    grad_query_cross, grad_key_memory, grad_value_memory = attention_backward(
        first, decoder_lengths, memory_lengths, query_cross, key_memory, value_memory,
        grad_attn_cross, cross_totals, None, head_width, memory_all.shape[0], (0, head_count // 2),
    )
    cross_grads = scatter_plain(
        jnp.stack(
            [
                t_mm(input_cross, grad_query_cross),
                t_mm(memory_all, grad_key_memory),
                t_mm(memory_all, grad_value_memory),
                grad_cross_out,
            ]
        ).astype(BF16)
    )
    memory_gradient = own_rows(
        mm_t(grad_key_memory, cross_full[1]) + mm_t(grad_value_memory, cross_full[2])
    )
    grad_norm_one, gain_grad_two = pull_cross(mm_t(grad_query_cross, cross_full[0]))
    grad_middle_one = grad_middle_two + grad_norm_one
    grad_branch_one = grad_middle_one.astype(BF16)
    grad_self_out = t_mm(attn_self, grad_branch_one)
    grad_attn_self = mm_t(grad_branch_one, self_out_full).astype(BF16)
    grad_query_self, grad_key_self, grad_value_self, diagonals = attention_backward(
        first, decoder_lengths, decoder_lengths, query_self, key_self, value_self,
        grad_attn_self, self_totals, tiles, head_width, key_count, (0, head_count // 2),
    )
    bias_partial = bias_gradient(diagonals, one_hot)
    self_grads = scatter_plain(
        jnp.stack(
            [
                t_mm(input_self, grad_query_self),
                t_mm(input_all, grad_key_self),
                t_mm(input_all, grad_value_self),
                grad_self_out,
            ]
        ).astype(BF16)
    )
    grad_input_self = own_rows(
        mm_t(grad_key_self, self_full[1]) + mm_t(grad_value_self, self_full[2])
    ) + mm_t(grad_query_self, self_full[0])
    grad_norm_zero, gain_grad_one = pull_self(grad_input_self)
    grad_tokens = grad_middle_one + grad_norm_zero
    gain_sums, bias_sums = lax.psum(
        (jnp.stack([gain_grad_one, gain_grad_two, gain_grad_three]), bias_partial), ("batch", "mem")
    )
    return (
        result_rows.astype(BF16)[None],
        grad_tokens[None],
        memory_gradient[None],
        gain_sums,
        bias_sums,
        self_grads[:3],
        self_grads[3],
        cross_grads[:3],
        cross_grads[3],
        expand_grad,
        contract_grad,
    )


def shards_hops(
    hidden,
    memory,
    decoder_lengths,
    memory_lengths,
    distance_buckets,
    norm_gains,
    position_bias,
    self_weights,
    self_output,
    cross_weights,
    cross_output,
    expand_weights,
    contract_weight,
    cotangent,
):
    batch_count, mem_count = lax.axis_size("batch"), lax.axis_size("mem")
    row_count, model_width = hidden.shape[1:]
    bucket_count, head_count = position_bias.shape
    head_width = model_width // head_count
    key_count = row_count * mem_count
    spot = jnp.stack(grid_place()).astype(jnp.int32)
    first = jnp.reshape(lax.axis_index("mem") * row_count, (1,)).astype(jnp.int32)
    own, own_memory = hidden[0], memory[0]

    slab, columns = self_weights.shape[1:]
    z_count = batch_count // 4

    pairs = head_count // 2
    pairs = head_count // 2
    far = send_mem(own)
    low, high = place_line(spot, line_of(self_weights))
    across = expand_weights.shape[2] // 128
    wide = jnp.concatenate(
        [
            expand_weights.reshape(2, slab, across, 128).transpose(0, 2, 1, 3).reshape(-1, 128),
            contract_weight.reshape(-1, columns // 128, 128).transpose(1, 0, 2).reshape(-1, 128),
        ]
    )
    second = jnp.concatenate([cross_weights, self_output[None], cross_output[None]])
    (second,) = hold((second,), (low, high))
    line = line_of(second)
    low, high = gather_first(spot, low, high, (far,))
    next_low, next_high = place_line(spot, line, (low, high))
    low, high = gather_second(spot, low, high, (next_low, next_high))
    self_pack = gather_cores(low, high)

    distance_table, one_hot = bias_window(
        distance_buckets, position_bias, lax.axis_index("mem") * row_count, row_count
    )

    query_self, key_self, value_self, normed_self = project_self(
        spot, own, far, norm_gains, self_pack, ()
    )

    halves = ((0, pairs // 2), (pairs // 2, pairs // 2))

    def self_forward(span, after, cost):
        return attention_forward(
            first, decoder_lengths, decoder_lengths, query_self, key_self, value_self,
            distance_table, head_width, key_count, span, after, cost,
        )

    low, high = gather_first(spot, next_low, next_high, (query_self,))
    memory_start, wide = hold((own_memory, wide), (low, high))
    wide = lax.all_gather(wide, ("batch", "mem"), axis=0, tiled=False)
    wide = wide.reshape(batch_count, mem_count, *wide.shape[1:])
    far_memory = send_mem(memory_start)
    one = self_forward(halves[0], (low, high), LONG)
    two = self_forward(halves[1], (one[0], memory_start), LONG)
    low, high = gather_second(spot, low, high, (two[0],))
    square_pack = gather_cores(low, high)
    attn_self, self_totals, tiles = zip(one, two)
    middle_one, normed_cross, query_cross = after_self(spot, own, attn_self, norm_gains, square_pack)
    key_memory, value_memory = project_memory(spot, own_memory, far_memory, square_pack)
    attn_cross, cross_totals = attention_forward(
        first, decoder_lengths, memory_lengths, query_cross, key_memory, value_memory,
        None, head_width, key_memory.shape[0], (0, pairs),
    )
    (
        result, grad_middle_two, grad_attn_cross, gain_three, wide_grad,
    ) = feed_forward(
        spot, middle_one, attn_cross, cotangent[0], norm_gains, square_pack, wide, expand_weights.shape[2]
    )
    wide_grad = lax.psum_scatter(
        wide_grad.reshape(batch_count * mem_count, *wide_grad.shape[2:]),
        ("batch", "mem"), scatter_dimension=0, tiled=True,
    )[0]
    grad_query_cross, grad_key_memory, grad_value_memory = attention_backward(
        first, decoder_lengths, memory_lengths, query_cross, key_memory, value_memory,
        grad_attn_cross, cross_totals, None, head_width, key_memory.shape[0], (0, pairs),
    )
    memory_own, memory_far, kv_keep, kv_send = memory_backward(
        spot, grad_key_memory, grad_value_memory, own_memory, far_memory, square_pack
    )
    grad_middle_one, grad_attn_self, gain_two, qo_keep, qo_send = after_cross(
        spot, (grad_query_cross,), middle_one, grad_middle_two, normed_cross, attn_self, attn_cross,
        norm_gains, square_pack, (memory_far,),
    )

    def self_backward(half, after):
        return attention_backward(
            first, decoder_lengths, decoder_lengths, query_self, key_self, value_self,
            grad_attn_self, self_totals[half], tiles[half], head_width, key_count, halves[half], after,
        )

    one = self_backward(0, (qo_keep,))
    (kv_keep, kv_send), (qo_keep, qo_send) = scatter_step(
        ((kv_keep, send_batch(kv_send, 1)), (qo_keep, send_batch(qo_send, 1))), (one[0],), (2, 1)
    )
    memory_far = send_mem(memory_far)
    two = self_backward(1, (kv_keep, one[0]))
    grad_query_self, grad_key_self, grad_value_self, diagonals = zip(one, two)
    rows_own, rows_far, gain_one = self_row_grads(
        spot, own, far, norm_gains, grad_query_self, grad_key_self, grad_value_self, self_pack, ()
    )
    (kv_keep, kv_send), (qo_keep, qo_send) = scatter_step(
        ((kv_keep, send_mem(kv_send)), (qo_keep, send_batch(qo_send, 2))),
        (rows_own, memory_far), (1, 1),
    )
    rows_far = send_mem(rows_far)
    bias_partial = bias_gradient(jnp.concatenate(diagonals, axis=0), one_hot)
    gains = jnp.concatenate([gain_one, gain_two, gain_three], axis=0)
    sums = jnp.concatenate([gains.reshape(-1), bias_partial.reshape(-1)]).reshape(-1, 128)
    keep_a, send_a, keep_b, send_b = self_weight_grads(
        spot, grad_query_self, grad_key_self, grad_value_self, normed_self, z_count, (kv_keep, sums)
    )
    line = scatter_to_line(
        ((kv_keep, send_batch(kv_send, 2)), (qo_keep, send_mem(qo_send))), (keep_a,)
    )
    sums = sum_small(sums, (2, 4, 6), (line[0],))
    (keep_a, send_a), (keep_b, send_b) = scatter_step(
        ((keep_a, send_batch(send_a, 1)), (keep_b, send_batch(send_b, 1))), (sums,), (2, 1)
    )
    sums = sum_small(sums, (8, 16, 24), (keep_a,))
    memory_gradient = add_rows(memory_own, memory_far, (sums,))
    (keep_a, send_a), (keep_b, send_b) = scatter_step(
        ((keep_a, send_mem(send_a)), (keep_b, send_batch(send_b, 2))), (memory_gradient,), (1, 1)
    )
    hidden_gradient = finish_rows(own, rows_own, rows_far, grad_middle_one, norm_gains, (keep_a,))
    self_line = scatter_to_line(
        ((keep_a, send_batch(send_a, 2)), (keep_b, send_mem(send_b))), (hidden_gradient,)
    )
    units = [(0, matrix, block) for matrix in range(5) for block in range(3)]
    cross_grad, self_out_grad, cross_out_grad = scatter_end(
        (send_line(line),),
        (cross_weights.shape, self_output.shape, cross_output.shape),
        square_moves(units, slab, columns, ((0, 1), (0, 2), (0, 0), (1, None), (2, None))),
        (self_line[0],),
    )
    sums = sum_small(sums, (1,), (cross_grad,)).reshape(-1)
    units = [(0, unit // 3, unit % 3) for unit in range(9)]
    (self_grad,) = scatter_end(
        (send_line(self_line),), (self_weights.shape,),
        square_moves(units, slab, columns, ((0, 0), (0, 1), (0, 2))), (sums,),
    )
    gate_rows, down_rows = across * slab, contract_weight.shape[0]
    moves = []
    for which in range(2):
        for block in range(across):
            span = (which, slice(None), slice(block * 128, block * 128 + 128))
            moves.append((0, which * gate_rows + block * slab, slab, 0, span))
    for block in range(columns // 128):
        span = (slice(None), slice(block * 128, block * 128 + 128))
        moves.append((0, 2 * gate_rows + block * down_rows, down_rows, 1, span))
    expand_grad, contract_grad = scatter_end(
        ((wide_grad,),), (expand_weights.shape, contract_weight.shape), moves, (self_line[0],)
    )
    return (
        result[None],
        hidden_gradient[None],
        memory_gradient[None],
        sums[: gains.size].reshape(gains.shape),
        sums[gains.size :].reshape(bucket_count, head_count),
        self_grad,
        self_out_grad,
        cross_grad,
        cross_out_grad,
        expand_grad,
        contract_grad,
    )


def shards(*arrays):
    row_count, slab, columns = arrays[0].shape[1], arrays[7].shape[1], arrays[7].shape[2]
    allowed = row_count == 512 and slab % 16 == 0 and columns % 128 == 0
    if lax.axis_size("mem") == 2 and lax.axis_size("batch") == 16 and allowed:
        return shards_hops(*arrays)
    return shards_plain(*arrays)


def solution(mesh):
    placed = (
        P("batch", "mem", None),
        P("batch", "mem", None),
        P("batch", None),
        P("batch", None),
        P(),
        P(),
        P(),
        P(None, "batch", "mem"),
        P("batch", "mem"),
        P(None, "batch", "mem"),
        P("batch", "mem"),
        P(None, "batch", "mem"),
        P("batch", "mem"),
        P("batch", "mem", None),
    )
    return jax.shard_map(
        shards,
        mesh=mesh,
        in_specs=placed,
        out_specs=(
            P("batch", "mem", None),
            P("batch", "mem", None),
            P("batch", "mem", None),
            P(),
            P(),
            P(None, "batch", "mem"),
            P("batch", "mem"),
            P(None, "batch", "mem"),
            P("batch", "mem"),
            P(None, "batch", "mem"),
            P("batch", "mem"),
        ),
        check_vma=False,
    )
```

```python
import functools
import math

import jax
import jax.numpy as jnp
from jax import lax
from jax.experimental import pallas as pl
from jax.experimental.pallas import tpu as pltpu
from jax.sharding import PartitionSpec as P

EPSILON = 1e-06
NEGATIVE = -1e30
F32 = jnp.float32
BF16 = jnp.bfloat16
EXACT = lax.Precision.HIGHEST
GELU_SCALE = (2 / math.pi) ** 0.5
GELU_CUBE = 0.044715
LONG = pl.CostEstimate(flops=20_000_000_000, bytes_accessed=1_000, transcendentals=0)
MEDIUM = pl.CostEstimate(flops=6_000_000_000, bytes_accessed=1_000, transcendentals=0)
BRIEF = pl.CostEstimate(flops=2_000_000_000, bytes_accessed=1_000, transcendentals=0)
SHORT = pl.CostEstimate(flops=100_000, bytes_accessed=1_000, transcendentals=0)
NT = (((1,), (1,)), ((), ()))
NN = (((1,), (0,)), ((), ()))


def rms_norm(values, gain_row):
    return (
        values * lax.rsqrt(jnp.mean(values * values, axis=-1, keepdims=True) + EPSILON) * gain_row
    )


def activate(gate_part, up_part):
    return jax.nn.gelu(gate_part, approximate=True) * up_part


def dot(left, right, dims):
    return lax.dot_general(left, right, dims, preferred_element_type=F32)


def bounds_of(sizes_ref):
    edges = [jnp.int32(0)]
    for slot in range(sizes_ref.shape[1]):
        edges.append(edges[-1] + sizes_ref[0, slot])
    return edges


def pick(place, edges, values):
    chosen = jnp.zeros_like(place) + values[0]
    for slot in range(1, len(edges) - 1):
        chosen = jnp.where(place >= edges[slot], values[slot], chosen)
    return chosen


def stack_heads(block, width):
    lane = lax.broadcasted_iota(jnp.int32, block.shape, 1)
    zero = jnp.zeros_like(block)
    return jnp.concatenate(
        [jnp.where(lane < width, block, zero), jnp.where(lane < width, zero, block)], axis=0
    )


def transposed_blocks(source_ref, scratch, step):
    for index in range(scratch.shape[0]):
        scratch[index] = source_ref[index * step : (index + 1) * step, :].T


def limits(first, rows, q_edges, k_edges, causal):
    place = lax.broadcasted_iota(jnp.int32, (1, rows), 1) + first
    begin = pick(place, q_edges, k_edges[:-1])
    end = pick(place, q_edges, k_edges[1:])
    if causal:
        end = jnp.minimum(end, place + 1)
    return begin, end


def fold(block, combine):
    parts = [block[start : start + 8] for start in range(0, block.shape[0], 8)]
    while len(parts) > 1:
        joined = [combine(parts[i], parts[i + 1]) for i in range(0, len(parts) - 1, 2)]
        parts = joined + parts[2 * len(joined) :]
    return parts[0]


def fill_mask(mask, first, q_edges, k_edges, causal):
    blocks, key_count, rows = mask.shape
    for block in range(blocks):
        begin, end = limits(first + block * rows, rows, q_edges, k_edges, causal)
        place = lax.broadcasted_iota(jnp.int32, (key_count, rows), 0)
        mask[block] = jnp.where((place >= begin) & (place < end), 0.0, NEGATIVE)


def fill_tiles(table_ref, tiles):
    count, tile = tiles.shape[:2]
    for head in range(2):
        wide = jnp.broadcast_to(table_ref[0, head : head + 1, :], (8, (count + 1) * tile))
        wide = pltpu.roll(wide, 0, 1, stride=1, stride_axis=0)
        for start in range(0, tile, 8):
            moved = pltpu.roll(wide, start, 1) if start else wide
            for index in range(count):
                tiles[index, start : start + 8, head * tile : (head + 1) * tile] = moved[
                    :, (index + 1) * tile : (index + 2) * tile
                ]


def sum_diagonals(tiles, out_ref):
    count, tile = tiles.shape[:2]
    for head in range(2):
        parts = jnp.zeros((8, (count + 1) * tile), F32)
        for start in range(0, tile, 8):
            line = [jnp.zeros((8, tile), F32)]
            for index in range(count):
                line.append(tiles[index, start : start + 8, head * tile : (head + 1) * tile])
            line = jnp.concatenate(line, axis=1)
            parts = parts + (pltpu.roll(line, line.shape[1] - start, 1) if start else line)
        line = parts[0:1]
        for row in range(1, 8):
            line = line + pltpu.roll(parts[row : row + 1], parts.shape[1] - row, 1)
        out_ref[0, head : head + 1, :] = line


def tile_of(u, t, key_tiles, row_tiles):
    return key_tiles - row_tiles + t - u


def bias_of(tiles, key_tiles, row_tiles):
    tile = tiles.shape[1]
    lines = []
    for u in range(key_tiles):
        line = [
            tiles[max(tile_of(u, t, key_tiles, row_tiles), 0), :, head * tile : (head + 1) * tile]
            for head in range(2)
            for t in range(row_tiles)
        ]
        lines.append(jnp.concatenate(line, axis=1))
    return jnp.concatenate(lines, axis=0)


def score_block(k_ref, queries, mask, tiles, block, index, step):
    here = pl.ds(pl.multiple_of(index * step, step), step)
    scores = dot(k_ref[here, :], queries, NT)
    if tiles is not None:
        tile = tiles.shape[1]
        scores = scores + bias_of(tiles, step // tile, queries.shape[0] // 2 // tile)
    hidden = mask[block, here, :]
    return scores + jnp.concatenate([hidden, hidden], axis=1)


def key_range(first, rows, q_edges, k_edges, step):
    high = pick(first + rows - 1, q_edges, k_edges[1:])
    return pick(first, q_edges, k_edges[:-1]) // step, (high + step - 1) // step


def forward_kernel(causal, step, width, first_ref, q_sizes, k_sizes, q_ref, k_ref, v_ref, *rest):
    if causal:
        table_ref, out_ref, total_ref, tiles_ref, value_t, scores, mask = rest
        tiles = tiles_ref.at[0]
    else:
        out_ref, total_ref, value_t, scores, mask = rest
        tiles = None
    blocks, rows = total_ref.shape[1], total_ref.shape[3] // 2
    q_edges = bounds_of(q_sizes)
    k_edges = bounds_of(k_sizes)

    @pl.when(pl.program_id(0) == 0)
    def once():
        fill_mask(mask, first_ref[0], q_edges, k_edges, causal)

    transposed_blocks(v_ref, value_t, step)
    if causal:
        fill_tiles(table_ref, tiles)
    for block in range(blocks):
        first = first_ref[0] + block * rows
        low, high = (0, 1) if causal else key_range(first, rows, q_edges, k_edges, step)
        queries = stack_heads(q_ref[block * rows : (block + 1) * rows, :], width)

        def measure(index, top):
            block_scores = score_block(k_ref, queries, mask, tiles, block, index, step)
            scores[index] = block_scores
            return jnp.maximum(top, fold(block_scores, jnp.maximum))

        top = lax.fori_loop(low, high, measure, jnp.full((8, 2 * rows), NEGATIVE, F32))
        top = jnp.max(top, axis=0, keepdims=True)

        def gather(index, carry):
            total, out_a, out_b = carry
            weights = jnp.exp(scores[index] - top)
            total = total + fold(weights, jnp.add)
            rounded = weights.astype(BF16)
            out_a = out_a + dot(value_t[index], rounded[:, :rows], NN)
            out_b = out_b + dot(value_t[index], rounded[:, rows:], NN)
            return total, out_a, out_b

        zero = jnp.zeros((2 * width, rows), F32)
        total, out_a, out_b = lax.fori_loop(
            low, high, gather, (jnp.zeros((8, 2 * rows), F32), zero, zero)
        )
        total = jnp.sum(total, axis=0, keepdims=True)
        joined = jnp.concatenate(
            [out_a[:width] / total[:, :rows], out_b[width:] / total[:, rows:]], axis=0
        )
        out_ref[block * rows : (block + 1) * rows, :] = joined.T.astype(BF16)
        total_ref[0, block] = top + jnp.log(total)


def backward_kernel(
    causal, step, width, first_ref, q_sizes, k_sizes, q_ref, k_ref, v_ref, g_ref, total_ref, *rest
):
    if causal:
        tiles_ref, dq_ref, dk_ref, dv_ref, diag_ref, key_t, probs, grads, dk, dv, mask, sums = rest
        tiles = tiles_ref.at[0]
    else:
        dq_ref, dk_ref, dv_ref, key_t, probs, grads, dk, dv, mask = rest
        tiles = None
    blocks, rows = total_ref.shape[1], total_ref.shape[3] // 2
    q_edges = bounds_of(q_sizes)
    k_edges = bounds_of(k_sizes)

    @pl.when(pl.program_id(0) == 0)
    def once():
        fill_mask(mask, first_ref[0], q_edges, k_edges, causal)

    transposed_blocks(k_ref, key_t, step)
    dk[...] = jnp.zeros_like(dk)
    dv[...] = jnp.zeros_like(dv)
    for block in range(blocks):
        first = first_ref[0] + block * rows
        low, high = (0, 1) if causal else key_range(first, rows, q_edges, k_edges, step)
        queries = stack_heads(q_ref[block * rows : (block + 1) * rows, :], width)
        targets = stack_heads(g_ref[block * rows : (block + 1) * rows, :], width)
        total = total_ref[0, block]

        def measure(index, inner):
            here = pl.ds(pl.multiple_of(index * step, step), step)
            block_scores = score_block(k_ref, queries, mask, tiles, block, index, step)
            weights = jnp.exp(block_scores - total)
            pulled = dot(v_ref[here, :], targets, NT)
            probs[index] = weights
            grads[index] = pulled
            dv[here, :] += dot(weights.astype(BF16), targets, NN)
            return inner + fold(weights * pulled, jnp.add)

        inner = lax.fori_loop(low, high, measure, jnp.zeros((8, 2 * rows), F32))
        inner = jnp.sum(inner, axis=0, keepdims=True)

        def gather(index, carry):
            out_a, out_b = carry
            here = pl.ds(pl.multiple_of(index * step, step), step)
            rounded = (probs[index] * (grads[index] - inner)).astype(BF16)
            dk[here, :] += dot(rounded, queries, NN)
            if causal:
                tile = tiles.shape[1]
                spots = [(u, t) for u in range(step // tile) for t in range(rows // tile)]
                for which in range(sums.shape[0]):
                    parts = [
                        jnp.concatenate(
                            [
                                rounded[u * tile : (u + 1) * tile, start + t * tile : start + (t + 1) * tile]
                                for start in (0, rows)
                            ],
                            axis=1,
                        ).astype(F32)
                        for u, t in spots
                        if tile_of(u, t, step // tile, rows // tile) == which
                    ]
                    sums[which] = functools.reduce(jnp.add, parts)
            out_a = out_a + dot(key_t[index], rounded[:, :rows], NN)
            out_b = out_b + dot(key_t[index], rounded[:, rows:], NN)
            return out_a, out_b

        zero = jnp.zeros((2 * width, rows), F32)
        out_a, out_b = lax.fori_loop(low, high, gather, (zero, zero))
        joined = jnp.concatenate([out_a[:width], out_b[width:]], axis=0)
        dq_ref[block * rows : (block + 1) * rows, :] = joined.T.astype(BF16)
    dk_ref[...] = dk[...].astype(BF16)
    dv_ref[...] = dv[...].astype(BF16)
    if causal:
        sum_diagonals(sums, diag_ref)


def unread():
    return pl.BlockSpec(memory_space=pl.ANY)


def ignoring(body, first, count):
    return lambda *refs: body(*refs[:first], *refs[first + count :])


def hold(values, after):
    count = len(values)
    return pl.pallas_call(
        lambda *refs: None,
        in_specs=[unread()] * (count + len(after)),
        out_specs=[unread()] * count,
        out_shape=[jax.ShapeDtypeStruct(value.shape, value.dtype) for value in values],
        input_output_aliases={index: index for index in range(count)},
        cost_estimate=SHORT,
        name="hold",
    )(*values, *after)


def smem():
    return pl.BlockSpec(memory_space=pltpu.SMEM)


def attention_forward(
    first, q_sizes, k_sizes, queries, keys, values, table, width, step, span, after=(), cost=LONG
):
    causal = table is not None
    count, model = queries.shape
    key_count = keys.shape[0]
    rows, tile = min(512, count), min(256, count)
    step = key_count if causal else min(step, key_count)
    pair_first, pairs = span
    blocks = count // rows
    column = lambda size: pl.BlockSpec((size, 2 * width), lambda pair: (0, pair + pair_first))
    result = lambda size: pl.BlockSpec((size, 2 * width), lambda pair: (0, pair))
    scratch = [
        pltpu.VMEM((key_count // step, 2 * width, step), BF16),
        pltpu.VMEM((key_count // step, step, 2 * rows), F32),
        pltpu.VMEM((count // rows, key_count, rows), F32),
    ]
    in_specs = [smem(), smem(), smem(), column(count), column(key_count), column(key_count)]
    args = [first, q_sizes, k_sizes, queries, keys, values]
    out_specs = [
        result(count),
        pl.BlockSpec((1, blocks, 1, 2 * rows), lambda pair: (pair, 0, 0, 0)),
    ]
    out_shape = [
        jax.ShapeDtypeStruct((count, pairs * 2 * width), BF16),
        jax.ShapeDtypeStruct((pairs, blocks, 1, 2 * rows), F32),
    ]
    if causal:
        in_specs.append(pl.BlockSpec((1, 2, table.shape[2]), lambda pair: (pair + pair_first, 0, 0)))
        args.append(table)
        tiles = (1, key_count // tile, tile, 2 * tile)
        out_specs.append(pl.BlockSpec(tiles, lambda pair: (pair, 0, 0, 0)))
        out_shape.append(jax.ShapeDtypeStruct((pairs, *tiles[1:]), F32))
    return pl.pallas_call(
        ignoring(functools.partial(forward_kernel, causal, step, width), len(args), len(after)),
        grid=(pairs,),
        in_specs=in_specs + [unread()] * len(after),
        out_specs=out_specs,
        out_shape=out_shape,
        scratch_shapes=scratch,
        compiler_params=pltpu.CompilerParams(vmem_limit_bytes=60 << 20),
        cost_estimate=cost,
        name="self_forward" if causal else "cross_forward",
    )(*args, *after)


def attention_backward(
    first, q_sizes, k_sizes, queries, keys, values, grads, totals, table, width, step, span, after=()
):
    causal = table is not None
    count, model = queries.shape
    key_count = keys.shape[0]
    rows, tile = min(512, count), min(256, count)
    step = key_count if causal else min(step, key_count)
    pair_first, pairs = span
    blocks = count // rows
    column = lambda size: pl.BlockSpec((size, 2 * width), lambda pair: (0, pair + pair_first))
    result = lambda size: pl.BlockSpec((size, 2 * width), lambda pair: (0, pair))
    n_step = key_count // step
    scratch = [
        pltpu.VMEM((n_step, 2 * width, step), BF16),
        pltpu.VMEM((n_step, step, 2 * rows), F32),
        pltpu.VMEM((n_step, step, 2 * rows), F32),
        pltpu.VMEM((key_count, 2 * width), F32),
        pltpu.VMEM((key_count, 2 * width), F32),
        pltpu.VMEM((count // rows, key_count, rows), F32),
    ]
    in_specs = [
        smem(), smem(), smem(), column(count), column(key_count), column(key_count), column(count),
        pl.BlockSpec((1, blocks, 1, 2 * rows), lambda pair: (pair, 0, 0, 0)),
    ]
    args = [first, q_sizes, k_sizes, queries, keys, values, grads, totals]
    out_specs = [result(count), result(key_count), result(key_count)]
    out_shape = [
        jax.ShapeDtypeStruct((count, pairs * 2 * width), BF16),
        jax.ShapeDtypeStruct((key_count, pairs * 2 * width), BF16),
        jax.ShapeDtypeStruct((key_count, pairs * 2 * width), BF16),
    ]
    if causal:
        in_specs.append(pl.BlockSpec((1, *table.shape[1:]), lambda pair: (pair, 0, 0, 0)))
        args.append(table)
        deltas = key_count // tile
        scratch.append(pltpu.VMEM((deltas, tile, 2 * tile), F32))
        out_specs.append(pl.BlockSpec((1, 2, (deltas + 1) * tile), lambda pair: (pair, 0, 0)))
        out_shape.append(jax.ShapeDtypeStruct((pairs, 2, (deltas + 1) * tile), F32))
    return pl.pallas_call(
        ignoring(functools.partial(backward_kernel, causal, step, width), len(args), len(after)),
        grid=(pairs,),
        in_specs=in_specs + [unread()] * len(after),
        out_specs=out_specs,
        out_shape=out_shape,
        scratch_shapes=scratch,
        compiler_params=pltpu.CompilerParams(vmem_limit_bytes=60 << 20),
        cost_estimate=LONG,
        name="self_backward" if causal else "cross_backward",
    )(*args, *after)


def bias_window(distance_buckets, position_bias, first, rows):
    key_count = distance_buckets.shape[0]
    tile = min(256, rows)
    margin = key_count - rows + tile
    buckets = jnp.arange(position_bias.shape[0], dtype=jnp.int32)
    one_hot = (distance_buckets[:, None] == buckets[None, :]).astype(F32)
    one_hot = jnp.pad(one_hot, ((margin, 0), (0, 0)))
    one_hot = lax.dynamic_slice_in_dim(one_hot, first, key_count + tile, 0)
    table = jnp.einsum("db,bh->hd", one_hot, position_bias, precision=EXACT)
    return table.reshape(position_bias.shape[1] // 2, 2, key_count + tile), one_hot


def bias_gradient(diagonals, one_hot):
    diagonals = diagonals.reshape(-1, one_hot.shape[0])
    return jnp.einsum("db,hd->bh", one_hot, diagonals, precision=EXACT)


def send_batch(block, distance):
    count = lax.axis_size("batch")
    return lax.ppermute(block, "batch", [(i, i ^ distance) for i in range(count)])


def send_mem(block):
    return lax.ppermute(block, "mem", [(0, 1), (1, 0)])


def place(pieces, mine):
    ordered = []
    for index in range(len(pieces)):
        chosen = pieces[0]
        for distance in range(1, len(pieces)):
            chosen = jnp.where(mine == (index ^ distance), pieces[distance], chosen)
        ordered.append(chosen)
    return jnp.stack(ordered)


def grid_place():
    batch_index = lax.axis_index("batch")
    return batch_index >> 2, (batch_index >> 1) & 1, batch_index & 1, lax.axis_index("mem")


def gather_plain(shard):
    within = lax.all_gather(shard, "mem", axis=2, tiled=True)
    return lax.all_gather(within, "batch", axis=1, tiled=True)


def scatter_plain(whole):
    part = lax.psum_scatter(whole, "batch", scatter_dimension=1, tiled=True)
    return lax.psum_scatter(part, "mem", scatter_dimension=2, tiled=True).astype(F32)


def whole_spec(shape):
    return pl.BlockSpec(tuple(shape), lambda *_: (0,) * len(shape))


def kernel_call(
    body, name, grid, in_specs, out_specs, out_shape, args, scratch=(), after=()
):
    return pl.pallas_call(
        ignoring(body, len(args), len(after)),
        grid=grid,
        in_specs=in_specs + [unread()] * len(after),
        out_specs=out_specs,
        out_shape=out_shape,
        scratch_shapes=list(scratch),
        compiler_params=pltpu.CompilerParams(vmem_limit_bytes=60 << 20),
        cost_estimate=MEDIUM if name.endswith("kernel") else SHORT,
        name=name,
    )(*args, *after)


def simple_call(body, name, out_shape, args, after=(), spot=None):
    lead = [] if spot is None else [spot]
    return kernel_call(
        body, name, (1,), [smem()] * len(lead) + [whole_spec(arg.shape) for arg in args],
        [whole_spec(shape.shape) for shape in out_shape], out_shape, (*lead, *args), after=after,
    )


def place_line(spot, pieces, after=()):
    count = len(pieces)
    half = count // 2
    shape = jax.ShapeDtypeStruct((half, *pieces[0].shape), BF16)

    def body(spot_ref, *refs):
        low_ref, high_ref = refs[count:]
        for distance in range(count):
            z = spot_ref[0] ^ distance

            @pl.when(z < half)
            def lower():
                low_ref[z] = refs[distance][...]

            @pl.when(z >= half)
            def upper():
                high_ref[z - half] = refs[distance][...]

    return simple_call(body, "place_line", [shape, shape], pieces, after, spot)


def place_pairs(spot, axes, pairs, after=()):
    shapes = [jax.ShapeDtypeStruct((2, *own.shape), BF16) for own, _ in pairs]

    def body(spot_ref, *refs):
        for index, axis in enumerate(axes):
            own_ref, far_ref, out_ref = refs[2 * index], refs[2 * index + 1], refs[2 * len(axes) + index]
            mine = spot_ref[axis]
            out_ref[mine] = own_ref[...]
            out_ref[1 - mine] = far_ref[...]

    return simple_call(body, "place_pairs", shapes, [part for pair in pairs for part in pair], after, spot)


def line_of(shard):
    return [shard] + [send_batch(shard, 4 * d) for d in range(1, lax.axis_size("batch") // 4)]


def gather_first(spot, low, high, after=()):
    return place_pairs(spot, (3, 1), ((low, send_mem(low)), (high, send_batch(high, 2))), after)


def gather_second(spot, low, high, after=()):
    return place_pairs(spot, (1, 3), ((low, send_batch(low, 2)), (high, send_mem(high))), after)


def gather_cores(low, high):
    return low, send_batch(low, 1), high, send_batch(high, 1)


def add_refs(refs):
    total = refs[0][...].astype(F32)
    for ref in refs[1:]:
        total = total + ref[...].astype(F32)
    return total


def scatter_step(groups, after, axes):
    def body(*refs):
        outs = refs[2 * len(groups) :]
        for index, axis in enumerate(axes):
            total = add_refs(refs[2 * index : 2 * index + 2]).astype(BF16)
            cut = (slice(None),) * axis
            outs[2 * index][...] = total[(*cut, 0)]
            outs[2 * index + 1][...] = total[(*cut, 1)]

    in_specs, out_specs, shapes, args = [], [], [], []
    for (kept, received), axis in zip(groups, axes):
        args += [kept, received]
        block = (1, *kept.shape[1:])
        zeros = (0,) * (len(block) - 1)
        in_specs += [pl.BlockSpec(block, lambda z, zeros=zeros: (z, *zeros))] * 2
        rest = kept.shape[:axis] + kept.shape[axis + 1 :]
        out_specs += [pl.BlockSpec((1, *rest[1:]), lambda z, zeros=zeros: (z, *zeros[1:]))] * 2
        shapes += [jax.ShapeDtypeStruct(rest, BF16)] * 2
    outs = kernel_call(
        body, "scatter_step", (args[0].shape[0],), in_specs, out_specs, shapes, args, after=after
    )
    return [tuple(outs[2 * index : 2 * index + 2]) for index in range(len(groups))]


def scatter_to_line(groups, after):
    count = groups[0][0].shape[0]
    ends = [0]
    for kept, _ in groups:
        ends.append(ends[-1] + kept.shape[1])

    def body(*refs):
        outs = refs[2 * len(groups) :]
        for index in range(len(groups)):
            total = add_refs(refs[2 * index : 2 * index + 2]).astype(BF16)
            for distance in range(count):
                outs[distance][ends[index] : ends[index + 1], :] = total[distance]

    shapes = [jax.ShapeDtypeStruct((ends[-1], 128), BF16)] * count
    return simple_call(body, "scatter_to_line", shapes, [part for group in groups for part in group], after)


def send_line(pieces):
    return [pieces[0]] + [send_batch(pieces[d], 4 * d) for d in range(1, len(pieces))]


def scatter_end(groups, out_shapes, moves, after):
    def body(*refs):
        outs = refs[sum(len(group) for group in groups) :]
        totals, start = [], 0
        for group in groups:
            totals.append(add_refs(refs[start : start + len(group)]))
            start += len(group)
        for group, first, rows, out, index in moves:
            outs[out][index] = totals[group][first : first + rows]

    shapes = [jax.ShapeDtypeStruct(shape, F32) for shape in out_shapes]
    return simple_call(body, "scatter_end", shapes, [part for group in groups for part in group], after)


def square_moves(units, slab, columns, outputs):
    moves, used = [], {}
    for group, matrix, block in units:
        first = used.get(group, 0)
        used[group] = first + slab
        out, index = outputs[matrix]
        span = slice(block * 128, (block + 1) * 128)
        moves.append((group, first, slab, out, (slice(None), span) if index is None else (index, slice(None), span)))
    return moves


def sum_small(block, distances, after):
    count = lax.axis_size("batch") * 2
    parts = [block]
    for distance in distances:
        pairs = [(i, i ^ distance) for i in range(count)]
        parts.append(lax.ppermute(block, ("batch", "mem"), pairs))

    def body(*refs):
        values = [ref[...] for ref in refs[:-1]]
        while len(values) > 1:
            values = [values[i] + values[i + 1] for i in range(0, len(values), 2)]
        refs[-1][...] = values[0]

    return simple_call(body, "sum_small", [jax.ShapeDtypeStruct(block.shape, F32)], parts, after)[0]


def add_rows(block, far, after):
    rows, width = block.shape

    def body(one_ref, two_ref, out_ref):
        out_ref[...] = one_ref[...] + two_ref[...].astype(F32)

    spec = pl.BlockSpec((rows // 4, width), lambda i: (i, 0))
    shape = jax.ShapeDtypeStruct(block.shape, F32)
    return kernel_call(body, "add_rows", (4,), [spec, spec], spec, shape, (block, far), after=after)


def chosen(block, axis, index):
    return lax.dynamic_index_in_dim(block, index, axis, keepdims=False)


def all_rows(block):
    if lax.axis_size("mem") == 2:
        return place([block, send_mem(block)], lax.axis_index("mem")).reshape(-1, block.shape[1])
    return lax.all_gather(block, "mem", axis=0, tiled=True)


def own_rows(partial_rows):
    mem_count = lax.axis_size("mem")
    if mem_count == 2:
        halves = partial_rows.reshape(2, -1, partial_rows.shape[1])
        index = lax.axis_index("mem")
        far = send_mem(chosen(halves, 0, 1 - index).astype(BF16))
        return chosen(halves, 0, index) + far.astype(F32)
    return lax.psum_scatter(
        partial_rows.astype(BF16), "mem", scatter_dimension=0, tiled=True
    ).astype(F32)


def mm(left, right):
    return dot(left, right, NN)


def mm_t(left, right):
    return dot(left, right, NT)


def t_mm(left, right):
    return dot(left, right, (((0,), (0,)), ((), ())))


def weight_specs(pack, index):
    return [
        pl.BlockSpec(
            part.shape[:3] + (1,) + part.shape[4:], lambda *_: (0, 0, 0, index, 0, 0)
        )
        for part in pack
    ]


def columns_of(spot_ref, refs, index, column):
    low_own, low_far, high_own, high_far = refs
    half = low_own.shape[2]
    pieces = []
    for z in range(2 * half):
        for y in range(2):
            for core in range(2):
                if z < half:
                    spot = (y, column, z, index)
                    own, far = low_own[spot], low_far[spot]
                else:
                    spot = (column, y, z - half, index)
                    own, far = high_own[spot], high_far[spot]
                pieces.append(jnp.where(spot_ref[2] == core, own, far))
    return jnp.concatenate(pieces, axis=0)


def matrix_of(spot_ref, refs, index=0):
    return jnp.concatenate(
        [columns_of(spot_ref, refs, index, 0), columns_of(spot_ref, refs, index, 1)], axis=1
    )


def join(parts):
    return jnp.concatenate([part[...] for part in parts], axis=1)


def store_shard(place_ref, keep_ref, send_ref, z, y, x, unit, even, odd):
    at_z, at_y, at_core, at_x = (place_ref[axis] for axis in range(4))
    rows = even.shape[0]
    span = slice(unit, unit + rows)
    keep_ref[z ^ at_z, y ^ at_y, x ^ at_x, span, :] = jnp.where(at_core == 0, even, odd)
    send_ref[z ^ at_z, y ^ at_y, x ^ at_x, span, :] = jnp.where(at_core == 0, odd, even)


def store_square(place_ref, targets, matrix, z_count):
    rounded = matrix.astype(BF16)
    rows, columns = rounded.shape[0] // (4 * z_count), rounded.shape[1] // 2
    for z in range(z_count):
        for y in range(2):
            start = (z * 2 + y) * 2 * rows
            for x in range(2):
                for index, (keep_ref, send_ref, unit) in enumerate(targets):
                    span = slice(x * columns + index * 128, x * columns + (index + 1) * 128)
                    store_shard(
                        place_ref, keep_ref, send_ref, z, y, x, unit,
                        rounded[start : start + rows, span],
                        rounded[start + rows : start + 2 * rows, span],
                    )


def piece_shape(z_count, rows):
    return jax.ShapeDtypeStruct((z_count, 2, 2, rows, 128), BF16)


def inverse_rms(values):
    return lax.rsqrt(jnp.mean(values * values, axis=1, keepdims=True) + EPSILON)


def norm_backward(values, gain_row, grads):
    scale = inverse_rms(values)
    normed = values * scale
    gain_grad = jnp.sum(grads * normed, axis=0, keepdims=True)
    pulled = grads * gain_row
    inner = jnp.mean(pulled * normed, axis=1, keepdims=True)
    return scale * (pulled - normed * inner), gain_grad


def project_self(place, own, far, gains, pack, after):
    rows, width = own.shape
    columns = width // 2

    def body(place_ref, own_ref, far_ref, gains_ref, *refs):
        weights, (q_ref, k_ref, v_ref, normed_ref) = refs[:4], refs[4:]
        at_x = place_ref[3]
        here = pl.ds(pl.multiple_of(at_x * rows, rows), rows)
        there = pl.ds(pl.multiple_of((1 - at_x) * rows, rows), rows)

        @pl.when(pl.program_id(0) == 0)
        def normalise():
            for source, span in ((own_ref, here), (far_ref, there)):
                values = source[...].astype(F32)
                normed_ref[span, :] = (values * inverse_rms(values) * gains_ref[0:1, :]).astype(BF16)

        q_ref[...] = mm(normed_ref[here, :], columns_of(place_ref, weights, 0, 0)).astype(BF16)
        normed = normed_ref[...]
        k_ref[...] = mm(normed, columns_of(place_ref, weights, 1, 0)).astype(BF16)
        v_ref[...] = mm(normed, columns_of(place_ref, weights, 2, 0)).astype(BF16)

    low, high = pack[0], pack[2]
    low_spec = pl.BlockSpec(low.shape[:1] + (1,) + low.shape[2:], lambda m: (0, m, 0, 0, 0, 0))
    high_spec = pl.BlockSpec((1,) + high.shape[1:], lambda m: (m, 0, 0, 0, 0, 0))
    return kernel_call(
        body, "project_self_kernel", (2,),
        [
            smem(), whole_spec(own.shape), whole_spec(far.shape), whole_spec(gains.shape),
            low_spec, low_spec, high_spec, high_spec,
        ],
        [
            pl.BlockSpec((rows, columns), lambda m: (0, m)),
            pl.BlockSpec((2 * rows, columns), lambda m: (0, m)),
            pl.BlockSpec((2 * rows, columns), lambda m: (0, m)),
            whole_spec((2 * rows, width)),
        ],
        [
            jax.ShapeDtypeStruct((rows, width), BF16),
            jax.ShapeDtypeStruct((2 * rows, width), BF16),
            jax.ShapeDtypeStruct((2 * rows, width), BF16),
            jax.ShapeDtypeStruct((2 * rows, width), BF16),
        ],
        (place, own, far, gains, *pack),
        after=after,
    )


def specs_of(arrays):
    return [whole_spec(array.shape) for array in arrays]


def after_self(place, own, attn, gains, pack):
    rows, width = own.shape
    count = len(attn)

    def body(place_ref, own_ref, gains_ref, *refs):
        attended = join(refs[:count])
        out_weight, q_weight = refs[count : count + 4], refs[count + 4 : count + 8]
        middle_ref, normed_ref, q_ref = refs[count + 8 :]
        middle = own_ref[...].astype(F32) + mm(attended, matrix_of(place_ref, out_weight))
        middle_ref[...] = middle
        normed = (middle * inverse_rms(middle) * gains_ref[1:2, :]).astype(BF16)
        normed_ref[...] = normed
        q_ref[...] = mm(normed, matrix_of(place_ref, q_weight)).astype(BF16)

    return kernel_call(
        body, "after_self", (1,),
        [smem(), whole_spec(own.shape), whole_spec(gains.shape), *specs_of(attn)]
        + weight_specs(pack, 3) + weight_specs(pack, 0),
        [whole_spec(own.shape)] * 3,
        [
            jax.ShapeDtypeStruct((rows, width), F32),
            jax.ShapeDtypeStruct((rows, width), BF16),
            jax.ShapeDtypeStruct((rows, width), BF16),
        ],
        (place, own, gains, *attn, *pack, *pack),
    )


def project_memory(place, own, far, pack):
    rows, width = own.shape

    def body(place_ref, own_ref, far_ref, *refs):
        k_ref, v_ref, key_weight, value_weight = refs[8:]

        @pl.when(pl.program_id(0) == 0)
        def once():
            key_weight[...] = matrix_of(place_ref, refs[:4])
            value_weight[...] = matrix_of(place_ref, refs[4:8])

        source = jnp.where(pl.program_id(0) == 0, own_ref[...], far_ref[...])
        k_ref[...] = mm(source, key_weight[...]).astype(BF16)
        v_ref[...] = mm(source, value_weight[...]).astype(BF16)

    def result(i, place_ref):
        return (place_ref[3] ^ i, 0)

    shape = jax.ShapeDtypeStruct((2 * rows, width), BF16)
    return pl.pallas_call(
        body,
        grid_spec=pltpu.PrefetchScalarGridSpec(
            num_scalar_prefetch=1,
            grid=(2,),
            in_specs=[
                whole_spec((rows, width)),
                whole_spec((rows, width)),
            ]
            + weight_specs(pack, 1) + weight_specs(pack, 2),
            out_specs=[pl.BlockSpec((rows, width), result)] * 2,
            scratch_shapes=[pltpu.VMEM((width, width), BF16)] * 2,
        ),
        out_shape=[shape, shape],
        compiler_params=pltpu.CompilerParams(vmem_limit_bytes=60 << 20),
        cost_estimate=MEDIUM,
        name="project_memory_kernel",
    )(place, own, far, *pack, *pack)


def feed_forward(place, middle_one, attn, cotangent, gains, pack, wide, half):
    rows, width = cotangent.shape
    batch_count = wide.shape[0]
    slab = width // batch_count
    chunk = half
    across = chunk // 128
    down_rows = half * 2 // batch_count
    down_across = width // 256
    down_units = down_across * down_rows

    def body(
        place_ref, middle_ref, attn_ref, cot_ref, gains_ref, co_one, co_two, co_three, co_four,
        gate_ref, up_ref, down_ref, out_ref, grad_middle_ref, grad_attn_ref, gain_ref, wide_grad,
        middle_two, normed, normed_t, grad_normed, result,
    ):
        step = pl.program_id(0)
        co_refs = (co_one, co_two, co_three, co_four)

        @pl.when(step == 0)
        def start():
            middle = middle_ref[...] + mm(attn_ref[...], matrix_of(place_ref, co_refs))
            middle_two[...] = middle
            rounded = (middle * inverse_rms(middle) * gains_ref[2:3, :]).astype(BF16)
            normed[...] = rounded
            normed_t[...] = rounded.T
            grad_normed[...] = jnp.zeros_like(grad_normed)
            result[...] = middle

        def wide_weight(ref):
            blocks = [
                ref[:, 0, index * slab : (index + 1) * slab, :].reshape(width, 128)
                for index in range(across)
            ]
            return jnp.concatenate(blocks, axis=1)

        cot = cot_ref[...]
        gate_weight, up_weight = wide_weight(gate_ref), wide_weight(up_ref)
        down_weight = jnp.concatenate(
            [
                down_ref[:, x, index * down_rows : (index + 1) * down_rows, :].reshape(chunk, 128)
                for x in range(2)
                for index in range(down_across)
            ],
            axis=1,
        )
        gate = mm(normed[...], gate_weight)
        up = mm(normed[...], up_weight)
        square = gate * gate
        bend = jnp.tanh(GELU_SCALE * (gate + GELU_CUBE * (gate * square)))
        half_one = 0.5 * (1.0 + bend)
        gelu = gate * half_one
        slope = half_one + 0.5 * gate * (1.0 - bend * bend) * (
            GELU_SCALE * (1.0 + 3.0 * GELU_CUBE * square)
        )
        act = (gelu * up).astype(BF16)
        result[...] += mm(act, down_weight)
        grad_act = mm_t(cot, down_weight)
        grad_gate = (grad_act * up * slope).astype(BF16)
        grad_up = (grad_act * gelu).astype(BF16)
        grad_normed[...] += mm_t(grad_gate, gate_weight) + mm_t(grad_up, up_weight)
        down_grad = t_mm(act, cot).astype(BF16)
        gate_rows = across * slab
        for block in range(chunk // down_rows):
            for x in range(2):
                for index in range(down_across):
                    span = slice((x * down_across + index) * 128, (x * down_across + index + 1) * 128)
                    start_row = 2 * gate_rows + index * down_rows
                    wide_grad[step * (chunk // down_rows) + block, x, start_row : start_row + down_rows, :] = (
                        down_grad[block * down_rows : (block + 1) * down_rows, span]
                    )
        for which, grad in enumerate((grad_gate, grad_up)):
            whole = mm(normed_t[...], grad).astype(BF16).reshape(batch_count, slab, chunk)
            for index in range(across):
                start_row = which * gate_rows + index * slab
                wide_grad[:, step, pl.ds(start_row, slab), :] = whole[
                    :, :, index * 128 : (index + 1) * 128
                ]

        @pl.when(step == pl.num_programs(0) - 1)
        def finish():
            out_ref[...] = result[...].astype(BF16)
            pulled, gain_grad = norm_backward(middle_two[...], gains_ref[2:3, :], grad_normed[...])
            gain_ref[...] = gain_grad
            grad_middle = cot_ref[...].astype(F32) + pulled
            grad_middle_ref[...] = grad_middle
            branch = grad_middle.astype(BF16)
            grad_attn_ref[...] = mm_t(branch, matrix_of(place_ref, co_refs)).astype(BF16)

    row_shape = (rows, width)
    wide_spec = lambda which: pl.BlockSpec(
        (batch_count, 1, across * slab, 128), lambda i: (0, i, which, 0)
    )
    down_spec = pl.BlockSpec(
        (chunk // down_rows, 2, down_units, 128), lambda i: (i, 0, 2 * across * slab // down_units, 0)
    )
    return kernel_call(
        body, "feed_forward_kernel", (2,),
        [smem(), *[whole_spec(row_shape)] * 3, whole_spec(gains.shape)] + weight_specs(pack, 4) + [wide_spec(0), wide_spec(1), down_spec],
        [whole_spec(row_shape)] * 3 + [whole_spec((1, width)), whole_spec(wide.shape)],
        [
            jax.ShapeDtypeStruct(row_shape, BF16),
            jax.ShapeDtypeStruct(row_shape, F32),
            jax.ShapeDtypeStruct(row_shape, BF16),
            jax.ShapeDtypeStruct((1, width), F32),
            jax.ShapeDtypeStruct(wide.shape, BF16),
        ],
        (place, middle_one, attn, cotangent, gains, *pack, wide, wide, wide),
        scratch=[
            pltpu.VMEM(row_shape, F32), pltpu.VMEM(row_shape, BF16), pltpu.VMEM((width, rows), BF16),
            pltpu.VMEM(row_shape, F32), pltpu.VMEM(row_shape, F32),
        ],
    )


def after_cross(
    place, grad_query, middle_one, grad_middle_two, normed_cross, attn_self, attn_cross, gains, pack, after
):
    rows, width = middle_one.shape
    z_count = pack[0].shape[2] * 2
    slab = pack[0].shape[4]
    one, two = len(grad_query), len(attn_self)

    def body(place_ref, middle_ref, grad_ref, normed_ref, cross_ref, gains_ref, *refs):
        grad_query = join(refs[:one])
        attended = join(refs[one : one + two])
        so_refs, q_refs = refs[one + two : one + two + 4], refs[one + two + 4 : one + two + 8]
        grad_middle_ref, grad_attn_ref, gain_ref, keep_ref, send_ref = refs[one + two + 8 :]
        grads = mm_t(grad_query, matrix_of(place_ref, q_refs))
        pulled, gain_grad = norm_backward(middle_ref[...], gains_ref[1:2, :], grads)
        gain_ref[...] = gain_grad
        grad_middle = grad_ref[...] + pulled
        grad_middle_ref[...] = grad_middle
        branch = grad_middle.astype(BF16)
        grad_attn_ref[...] = mm_t(branch, matrix_of(place_ref, so_refs)).astype(BF16)
        branch_two = grad_ref[...].astype(BF16)
        for index, (left, right) in enumerate(
            ((normed_ref[...], grad_query), (attended, branch), (cross_ref[...], branch_two))
        ):
            targets = [(keep_ref, send_ref, (3 * index + part) * slab) for part in range(3)]
            store_square(place_ref, targets, t_mm(left, right), z_count)

    pieces = piece_shape(z_count, 9 * slab)
    row_shape = (rows, width)
    return kernel_call(
        body, "after_cross_kernel", (1,),
        [smem()] + [whole_spec(row_shape)] * 4 + [whole_spec(gains.shape)]
        + specs_of(grad_query) + specs_of(attn_self)
        + weight_specs(pack, 3) + weight_specs(pack, 0),
        [whole_spec(row_shape), whole_spec(row_shape), whole_spec((1, width))]
        + [whole_spec(pieces.shape)] * 2,
        [
            jax.ShapeDtypeStruct(row_shape, F32),
            jax.ShapeDtypeStruct(row_shape, BF16),
            jax.ShapeDtypeStruct((1, width), F32),
            pieces,
            pieces,
        ],
        (
            place, middle_one, grad_middle_two, normed_cross, attn_cross, gains,
            *grad_query, *attn_self, *pack, *pack,
        ),
        after=after,
    )


def memory_backward(place, grad_key, grad_value, own, far, pack):
    rows, width = own.shape
    z_count = pack[0].shape[2] * 2
    slab = pack[0].shape[4]

    def body(
        place_ref, dk_ref, dv_ref, own_ref, far_ref, *refs,
    ):
        k_refs, v_refs = refs[:4], refs[4:8]
        grad_own_ref, grad_far_ref, keep_ref, send_ref = refs[8:12]
        key_total, value_total, key_weight, value_weight = refs[12:]
        i = pl.program_id(0)
        source = jnp.where(i == 0, far_ref[...], own_ref[...])
        source_t = source.T

        @pl.when(i == 0)
        def clear():
            key_total[...] = jnp.zeros_like(key_total)
            value_total[...] = jnp.zeros_like(value_total)
            key_weight[...] = matrix_of(place_ref, k_refs)
            value_weight[...] = matrix_of(place_ref, v_refs)

        grad_key, grad_value = dk_ref[...], dv_ref[...]
        key_total[...] += mm(source_t, grad_key)
        value_total[...] += mm(source_t, grad_value)
        grads = mm_t(grad_key, key_weight[...]) + mm_t(grad_value, value_weight[...])

        @pl.when(i == 0)
        def there():
            grad_far_ref[...] = grads.astype(BF16)

        @pl.when(i == 1)
        def here():
            grad_own_ref[...] = grads

        @pl.when(i == 1)
        def finish():
            for index, total in enumerate((key_total, value_total)):
                targets = [(keep_ref, send_ref, (3 * index + part) * slab) for part in range(3)]
                store_square(place_ref, targets, total[...], z_count)

    def block(i, place_ref):
        return (place_ref[3] ^ (1 - i), 0)

    pieces = piece_shape(z_count, 6 * slab)
    return pl.pallas_call(
        body,
        grid_spec=pltpu.PrefetchScalarGridSpec(
            num_scalar_prefetch=1,
            grid=(2,),
            in_specs=[
                *[pl.BlockSpec((rows, width), block)] * 2,
                whole_spec((rows, width)),
                whole_spec((rows, width)),
            ]
            + weight_specs(pack, 1) + weight_specs(pack, 2),
            out_specs=[
                whole_spec((rows, width)),
                whole_spec((rows, width)),
                whole_spec(pieces.shape),
                whole_spec(pieces.shape),
            ],
            scratch_shapes=[pltpu.VMEM((width, width), F32)] * 2
            + [pltpu.VMEM((width, width), BF16)] * 2,
        ),
        out_shape=[
            jax.ShapeDtypeStruct((rows, width), F32),
            jax.ShapeDtypeStruct((rows, width), BF16),
            pieces,
            pieces,
        ],
        compiler_params=pltpu.CompilerParams(vmem_limit_bytes=60 << 20),
        cost_estimate=MEDIUM,
        name="memory_backward_kernel",
    )(place, grad_key, grad_value, own, far, *pack, *pack)


def self_weight_grads(place, grad_query, grad_key, grad_value, normed, z_count, after):
    rows, half = grad_query[0].shape
    width = 2 * half
    slab = width // (4 * z_count)

    def body(place_ref, dq_a, dq_b, dk_a, dk_b, dv_a, dv_b, normed_ref, keep_a, send_a, keep_b, send_b):
        here = pl.ds(pl.multiple_of(place_ref[3] * rows, rows), rows)
        normed_t = normed_ref[...].T
        grads = (
            t_mm(normed_ref[here, :], join((dq_a, dq_b))),
            mm(normed_t, join((dk_a, dk_b))),
            mm(normed_t, join((dv_a, dv_b))),
        )
        for index, grad in enumerate(grads):
            targets = []
            for unit in range(3 * index, 3 * index + 3):
                first = unit < 5
                targets.append(
                    (keep_a if first else keep_b, send_a if first else send_b, (unit if first else unit - 5) * slab)
                )
            store_square(place_ref, targets, grad, z_count)

    shapes = [piece_shape(z_count, count * slab) for count in (5, 5, 4, 4)]
    return kernel_call(
        body, "self_weight_grads_kernel", (1,),
        [smem()] + [whole_spec((rows, half))] * 2 + [whole_spec((2 * rows, half))] * 4
        + [whole_spec((2 * rows, width))],
        [whole_spec(shape.shape) for shape in shapes],
        shapes,
        (place, *grad_query, *grad_key, *grad_value, normed),
        after=after,
    )


def self_row_grads(place, own, far, gains, grad_query, grad_key, grad_value, pack, after):
    rows, half = grad_query[0].shape
    width = 2 * half

    def body(place_ref, own_rows, far_rows, dq_a, dq_b, dk_a, dk_b, dv_a, dv_b, *refs):
        weights, (own_ref, far_ref, gain_ref) = refs[:4], refs[4:]
        key_weight = matrix_of(place_ref, weights, 1)
        value_weight = matrix_of(place_ref, weights, 2)
        here = pl.ds(pl.multiple_of(place_ref[3] * rows, rows), rows)
        there = pl.ds(pl.multiple_of((1 - place_ref[3]) * rows, rows), rows)
        split = lambda pair, span: jnp.concatenate([pair[0][span, :], pair[1][span, :]], axis=1)
        keys, values = (dk_a, dk_b), (dv_a, dv_b)

        def gain_of(rows_ref, grads):
            values = rows_ref[...].astype(F32)
            return jnp.sum(grads * (values * inverse_rms(values)), axis=0, keepdims=True)

        far_grads = mm_t(split(keys, there), key_weight) + mm_t(split(values, there), value_weight)
        far_ref[...] = far_grads.astype(BF16)
        own_grads = (
            mm_t(split(keys, here), key_weight)
            + mm_t(split(values, here), value_weight)
            + mm_t(join((dq_a, dq_b)), matrix_of(place_ref, weights, 0))
        )
        own_ref[...] = own_grads
        gain_ref[...] = gain_of(own_rows, own_grads) + gain_of(far_rows, far_grads)

    row_shape = (rows, width)
    return kernel_call(
        body, "self_row_grads_kernel", (1,),
        [smem()] + [whole_spec(row_shape)] * 2
        + specs_of(grad_query) + specs_of(grad_key) + specs_of(grad_value) + specs_of(pack),
        [whole_spec(row_shape)] * 2 + [whole_spec((1, width))],
        [
            jax.ShapeDtypeStruct(row_shape, F32),
            jax.ShapeDtypeStruct(row_shape, BF16),
            jax.ShapeDtypeStruct((1, width), F32),
        ],
        (place, own, far, *grad_query, *grad_key, *grad_value, *pack),
        after=after,
    )


def finish_rows(own, grads, far_grads, grad_middle, gains, after):
    def body(own_ref, grads_ref, far_ref, middle_ref, gains_ref, out_ref):
        total = grads_ref[...] + far_ref[...].astype(F32)
        pulled, _ = norm_backward(own_ref[...].astype(F32), gains_ref[0:1, :], total)
        out_ref[...] = middle_ref[...] + pulled

    shape = jax.ShapeDtypeStruct(own.shape, F32)
    return simple_call(body, "finish_rows_kernel", [shape], [own, grads, far_grads, grad_middle, gains], after)[0]


def shards_plain(
    hidden,
    memory,
    decoder_lengths,
    memory_lengths,
    distance_buckets,
    norm_gains,
    position_bias,
    self_weights,
    self_output,
    cross_weights,
    cross_output,
    expand_weights,
    contract_weight,
    cotangent,
):
    mem_count = lax.axis_size("mem")
    mem_index = lax.axis_index("mem")
    row_count, model_width = hidden.shape[1:]
    head_count = position_bias.shape[1]
    head_width = model_width // head_count
    key_count = row_count * mem_count
    first_row = mem_index * row_count
    first = jnp.reshape(first_row, (1,)).astype(jnp.int32)

    self_full = gather_plain(self_weights)
    tokens_all = all_rows(hidden[0])
    memory_all = all_rows(memory[0])
    square_full = gather_plain(
        jnp.concatenate([cross_weights, self_output[None], cross_output[None]])
    )
    cross_full, self_out_full, cross_out_full = square_full[:3], square_full[3], square_full[4]
    expand_full = gather_plain(expand_weights)
    contract_full = gather_plain(contract_weight[None])[0]

    distance_table, one_hot = bias_window(distance_buckets, position_bias, first_row, row_count)

    tokens = hidden[0].astype(F32)
    normed_self, pull_self = jax.vjp(rms_norm, tokens, norm_gains[0])
    input_self = normed_self.astype(BF16)
    input_all = rms_norm(tokens_all.astype(F32), norm_gains[0]).astype(BF16)
    query_self = mm(input_self, self_full[0]).astype(BF16)
    key_self = mm(input_all, self_full[1]).astype(BF16)
    value_self = mm(input_all, self_full[2]).astype(BF16)
    attn_self, self_totals, tiles = attention_forward(
        first, decoder_lengths, decoder_lengths, query_self, key_self, value_self,
        distance_table, head_width, key_count, (0, head_count // 2),
    )
    middle_one = tokens + mm(attn_self, self_out_full)
    normed_cross, pull_cross = jax.vjp(rms_norm, middle_one, norm_gains[1])
    input_cross = normed_cross.astype(BF16)
    query_cross = mm(input_cross, cross_full[0]).astype(BF16)
    key_memory = mm(memory_all, cross_full[1]).astype(BF16)
    value_memory = mm(memory_all, cross_full[2]).astype(BF16)
    attn_cross, cross_totals = attention_forward(
        first, decoder_lengths, memory_lengths, query_cross, key_memory, value_memory,
        None, head_width, memory_all.shape[0], (0, head_count // 2),
    )
    middle_two = middle_one + mm(attn_cross, cross_out_full)
    normed_feed, pull_feed = jax.vjp(rms_norm, middle_two, norm_gains[2])
    input_feed = normed_feed.astype(BF16)
    gate_part = mm(input_feed, expand_full[0])
    up_part = mm(input_feed, expand_full[1])
    activated, pull_activate = jax.vjp(activate, gate_part, up_part)
    hidden_act = activated.astype(BF16)
    result_rows = middle_two + mm(hidden_act, contract_full)
    grad_branch_three = cotangent[0]
    grad_out = grad_branch_three.astype(F32)
    grad_gate, grad_up = pull_activate(mm_t(grad_branch_three, contract_full))
    grad_gate, grad_up = grad_gate.astype(BF16), grad_up.astype(BF16)
    contract_grad = scatter_plain(t_mm(hidden_act, grad_branch_three).astype(BF16)[None])[0]
    expand_grad = scatter_plain(
        jnp.stack([t_mm(input_feed, grad_gate), t_mm(input_feed, grad_up)]).astype(BF16)
    )
    grad_norm_two, gain_grad_three = pull_feed(
        mm_t(grad_gate, expand_full[0]) + mm_t(grad_up, expand_full[1])
    )
    grad_middle_two = grad_out + grad_norm_two
    grad_branch_two = grad_middle_two.astype(BF16)
    grad_cross_out = t_mm(attn_cross, grad_branch_two)
    grad_attn_cross = mm_t(grad_branch_two, cross_out_full).astype(BF16)
    grad_query_cross, grad_key_memory, grad_value_memory = attention_backward(
        first, decoder_lengths, memory_lengths, query_cross, key_memory, value_memory,
        grad_attn_cross, cross_totals, None, head_width, memory_all.shape[0], (0, head_count // 2),
    )
    cross_grads = scatter_plain(
        jnp.stack(
            [
                t_mm(input_cross, grad_query_cross),
                t_mm(memory_all, grad_key_memory),
                t_mm(memory_all, grad_value_memory),
                grad_cross_out,
            ]
        ).astype(BF16)
    )
    memory_gradient = own_rows(
        mm_t(grad_key_memory, cross_full[1]) + mm_t(grad_value_memory, cross_full[2])
    )
    grad_norm_one, gain_grad_two = pull_cross(mm_t(grad_query_cross, cross_full[0]))
    grad_middle_one = grad_middle_two + grad_norm_one
    grad_branch_one = grad_middle_one.astype(BF16)
    grad_self_out = t_mm(attn_self, grad_branch_one)
    grad_attn_self = mm_t(grad_branch_one, self_out_full).astype(BF16)
    grad_query_self, grad_key_self, grad_value_self, diagonals = attention_backward(
        first, decoder_lengths, decoder_lengths, query_self, key_self, value_self,
        grad_attn_self, self_totals, tiles, head_width, key_count, (0, head_count // 2),
    )
    bias_partial = bias_gradient(diagonals, one_hot)
    self_grads = scatter_plain(
        jnp.stack(
            [
                t_mm(input_self, grad_query_self),
                t_mm(input_all, grad_key_self),
                t_mm(input_all, grad_value_self),
                grad_self_out,
            ]
        ).astype(BF16)
    )
    grad_input_self = own_rows(
        mm_t(grad_key_self, self_full[1]) + mm_t(grad_value_self, self_full[2])
    ) + mm_t(grad_query_self, self_full[0])
    grad_norm_zero, gain_grad_one = pull_self(grad_input_self)
    grad_tokens = grad_middle_one + grad_norm_zero
    gain_sums, bias_sums = lax.psum(
        (jnp.stack([gain_grad_one, gain_grad_two, gain_grad_three]), bias_partial), ("batch", "mem")
    )
    return (
        result_rows.astype(BF16)[None],
        grad_tokens[None],
        memory_gradient[None],
        gain_sums,
        bias_sums,
        self_grads[:3],
        self_grads[3],
        cross_grads[:3],
        cross_grads[3],
        expand_grad,
        contract_grad,
    )


def shards_hops(
    hidden,
    memory,
    decoder_lengths,
    memory_lengths,
    distance_buckets,
    norm_gains,
    position_bias,
    self_weights,
    self_output,
    cross_weights,
    cross_output,
    expand_weights,
    contract_weight,
    cotangent,
):
    batch_count, mem_count = lax.axis_size("batch"), lax.axis_size("mem")
    row_count, model_width = hidden.shape[1:]
    bucket_count, head_count = position_bias.shape
    head_width = model_width // head_count
    key_count = row_count * mem_count
    spot = jnp.stack(grid_place()).astype(jnp.int32)
    first = jnp.reshape(lax.axis_index("mem") * row_count, (1,)).astype(jnp.int32)
    own, own_memory = hidden[0], memory[0]

    slab, columns = self_weights.shape[1:]
    z_count = batch_count // 4

    pairs = head_count // 2
    pairs = head_count // 2
    far = send_mem(own)
    low, high = place_line(spot, line_of(self_weights))
    across = expand_weights.shape[2] // 128
    wide = jnp.concatenate(
        [
            expand_weights.reshape(2, slab, across, 128).transpose(0, 2, 1, 3).reshape(-1, 128),
            contract_weight.reshape(-1, columns // 128, 128).transpose(1, 0, 2).reshape(-1, 128),
        ]
    )
    second = jnp.concatenate([cross_weights, self_output[None], cross_output[None]])
    (second,) = hold((second,), (low, high))
    line = line_of(second)
    low, high = gather_first(spot, low, high, (far,))
    next_low, next_high = place_line(spot, line, (low, high))
    low, high = gather_second(spot, low, high, (next_low, next_high))
    self_pack = gather_cores(low, high)

    distance_table, one_hot = bias_window(
        distance_buckets, position_bias, lax.axis_index("mem") * row_count, row_count
    )

    query_self, key_self, value_self, normed_self = project_self(
        spot, own, far, norm_gains, self_pack, ()
    )

    halves = ((0, pairs // 2), (pairs // 2, pairs // 2))

    def self_forward(span, after, cost):
        return attention_forward(
            first, decoder_lengths, decoder_lengths, query_self, key_self, value_self,
            distance_table, head_width, key_count, span, after, cost,
        )

    low, high = gather_first(spot, next_low, next_high, (query_self,))
    memory_start, wide = hold((own_memory, wide), (low, high))
    wide = lax.all_gather(wide, ("batch", "mem"), axis=0, tiled=False)
    wide = wide.reshape(batch_count, mem_count, *wide.shape[1:])
    far_memory = send_mem(memory_start)
    one = self_forward(halves[0], (low, high), LONG)
    two = self_forward(halves[1], (one[0], memory_start), LONG)
    low, high = gather_second(spot, low, high, (two[0],))
    square_pack = gather_cores(low, high)
    attn_self, self_totals, tiles = zip(one, two)
    middle_one, normed_cross, query_cross = after_self(spot, own, attn_self, norm_gains, square_pack)
    key_memory, value_memory = project_memory(spot, own_memory, far_memory, square_pack)
    attn_cross, cross_totals = attention_forward(
        first, decoder_lengths, memory_lengths, query_cross, key_memory, value_memory,
        None, head_width, key_memory.shape[0], (0, pairs),
    )
    (
        result, grad_middle_two, grad_attn_cross, gain_three, wide_grad,
    ) = feed_forward(
        spot, middle_one, attn_cross, cotangent[0], norm_gains, square_pack, wide, expand_weights.shape[2]
    )
    wide_grad = lax.psum_scatter(
        wide_grad.reshape(batch_count * mem_count, *wide_grad.shape[2:]),
        ("batch", "mem"), scatter_dimension=0, tiled=True,
    )[0]
    grad_query_cross, grad_key_memory, grad_value_memory = attention_backward(
        first, decoder_lengths, memory_lengths, query_cross, key_memory, value_memory,
        grad_attn_cross, cross_totals, None, head_width, key_memory.shape[0], (0, pairs),
    )
    memory_own, memory_far, kv_keep, kv_send = memory_backward(
        spot, grad_key_memory, grad_value_memory, own_memory, far_memory, square_pack
    )
    grad_middle_one, grad_attn_self, gain_two, qo_keep, qo_send = after_cross(
        spot, (grad_query_cross,), middle_one, grad_middle_two, normed_cross, attn_self, attn_cross,
        norm_gains, square_pack, (memory_far,),
    )

    def self_backward(half, after):
        return attention_backward(
            first, decoder_lengths, decoder_lengths, query_self, key_self, value_self,
            grad_attn_self, self_totals[half], tiles[half], head_width, key_count, halves[half], after,
        )

    one = self_backward(0, (qo_keep,))
    (kv_keep, kv_send), (qo_keep, qo_send) = scatter_step(
        ((kv_keep, send_batch(kv_send, 1)), (qo_keep, send_batch(qo_send, 1))), (one[0],), (2, 1)
    )
    memory_far = send_mem(memory_far)
    two = self_backward(1, (kv_keep, one[0]))
    grad_query_self, grad_key_self, grad_value_self, diagonals = zip(one, two)
    rows_own, rows_far, gain_one = self_row_grads(
        spot, own, far, norm_gains, grad_query_self, grad_key_self, grad_value_self, self_pack, ()
    )
    (kv_keep, kv_send), (qo_keep, qo_send) = scatter_step(
        ((kv_keep, send_mem(kv_send)), (qo_keep, send_batch(qo_send, 2))),
        (rows_own, memory_far), (1, 1),
    )
    rows_far = send_mem(rows_far)
    bias_partial = bias_gradient(jnp.concatenate(diagonals, axis=0), one_hot)
    gains = jnp.concatenate([gain_one, gain_two, gain_three], axis=0)
    sums = jnp.concatenate([gains.reshape(-1), bias_partial.reshape(-1)]).reshape(-1, 128)
    keep_a, send_a, keep_b, send_b = self_weight_grads(
        spot, grad_query_self, grad_key_self, grad_value_self, normed_self, z_count, (kv_keep, sums)
    )
    line = scatter_to_line(
        ((kv_keep, send_batch(kv_send, 2)), (qo_keep, send_mem(qo_send))), (keep_a,)
    )
    sums = sum_small(sums, (2,), (line[0],))
    (keep_a, send_a), (keep_b, send_b) = scatter_step(
        ((keep_a, send_batch(send_a, 1)), (keep_b, send_batch(send_b, 1))), (sums,), (2, 1)
    )
    sums = sum_small(sums, (8, 16, 24), (keep_a,))
    memory_gradient = add_rows(memory_own, memory_far, (sums,))
    (keep_a, send_a), (keep_b, send_b) = scatter_step(
        ((keep_a, send_mem(send_a)), (keep_b, send_batch(send_b, 2))), (memory_gradient,), (1, 1)
    )
    hidden_gradient = finish_rows(own, rows_own, rows_far, grad_middle_one, norm_gains, (keep_a,))
    self_line = scatter_to_line(
        ((keep_a, send_batch(send_a, 2)), (keep_b, send_mem(send_b))), (hidden_gradient,)
    )
    units = [(0, matrix, block) for matrix in range(5) for block in range(3)]
    cross_grad, self_out_grad, cross_out_grad = scatter_end(
        (send_line(line),),
        (cross_weights.shape, self_output.shape, cross_output.shape),
        square_moves(units, slab, columns, ((0, 1), (0, 2), (0, 0), (1, None), (2, None))),
        (self_line[0],),
    )
    sums = sum_small(sums, (1, 4, 5), (cross_grad,)).reshape(-1)
    units = [(0, unit // 3, unit % 3) for unit in range(9)]
    (self_grad,) = scatter_end(
        (send_line(self_line),), (self_weights.shape,),
        square_moves(units, slab, columns, ((0, 0), (0, 1), (0, 2))), (sums,),
    )
    gate_rows, down_rows = across * slab, contract_weight.shape[0]
    moves = []
    for which in range(2):
        for block in range(across):
            span = (which, slice(None), slice(block * 128, block * 128 + 128))
            moves.append((0, which * gate_rows + block * slab, slab, 0, span))
    for block in range(columns // 128):
        span = (slice(None), slice(block * 128, block * 128 + 128))
        moves.append((0, 2 * gate_rows + block * down_rows, down_rows, 1, span))
    expand_grad, contract_grad = scatter_end(
        ((wide_grad,),), (expand_weights.shape, contract_weight.shape), moves, (self_line[0],)
    )
    return (
        result[None],
        hidden_gradient[None],
        memory_gradient[None],
        sums[: gains.size].reshape(gains.shape),
        sums[gains.size :].reshape(bucket_count, head_count),
        self_grad,
        self_out_grad,
        cross_grad,
        cross_out_grad,
        expand_grad,
        contract_grad,
    )


def shards(*arrays):
    row_count, slab, columns = arrays[0].shape[1], arrays[7].shape[1], arrays[7].shape[2]
    allowed = row_count == 512 and slab % 16 == 0 and columns % 128 == 0
    if lax.axis_size("mem") == 2 and lax.axis_size("batch") == 16 and allowed:
        return shards_hops(*arrays)
    return shards_plain(*arrays)


def solution(mesh):
    placed = (
        P("batch", "mem", None),
        P("batch", "mem", None),
        P("batch", None),
        P("batch", None),
        P(),
        P(),
        P(),
        P(None, "batch", "mem"),
        P("batch", "mem"),
        P(None, "batch", "mem"),
        P("batch", "mem"),
        P(None, "batch", "mem"),
        P("batch", "mem"),
        P("batch", "mem", None),
    )
    return jax.shard_map(
        shards,
        mesh=mesh,
        in_specs=placed,
        out_specs=(
            P("batch", "mem", None),
            P("batch", "mem", None),
            P("batch", "mem", None),
            P(),
            P(),
            P(None, "batch", "mem"),
            P("batch", "mem"),
            P(None, "batch", "mem"),
            P("batch", "mem"),
            P(None, "batch", "mem"),
            P("batch", "mem"),
        ),
        check_vma=False,
    )
```
